32 devices in a mesh: band: 2 (over x), tile: 8 (over z, y), lvl: 2 (over core).
Axes of the slice: x: 2, y: 2, z: 4, core: 2. Of those that a mesh axis runs over, the one named last changes fastest.
Arguments:
- image: float32 [512, 4096], P('band', 'tile'), parts along dimension 0, may hold values from 0 to 1
- curves: float32 [16, 17], P('lvl'), may hold values from -1 to 1
Outputs:
- toned: float32 [512, 4096], P('band', 'tile'), parts along dimension 0
The draws below stay inside these ranges and needn't reach their ends.
There are 2 independent parts, one for each index of `band`. The reference program is written for one: setup_inputs(seed, part) draws one part's arguments, and reference() takes and returns one part's arrays. A program takes and returns all parts, laid end to end along the dimension named above; an argument that names none is the same for every part. Nothing has to cross between parts.
All inputs are finite; a program needn't handle non-finite values.
Results may differ from the reference program's by a relative error of at most 0.0003.
Values sent between devices are 32-bit elements; how exact they have to be, the bound alone decides.
No kernel may reach another device: no remote copies, remote signals or barrier semaphores. Data moves between devices by JAX's collectives and lax.ppermute only.
A program may use at most 64 MiB of HBM per device.

```python
import jax
import jax.numpy as jnp
from jax import lax

ROWS = 256
LEVELS = 16
KNOTS = 17
PYR = 6
COLS = 4096


def block_levels(own_key, dims, split, least, high):
    def one(axis_at, blocks):
        draws = jax.random.uniform(jax.random.fold_in(jax.random.fold_in(own_key, 6), axis_at), (blocks,), jnp.float32, least / len(split), high / len(split))
        return jnp.repeat(jnp.exp(draws), dims[axis_at] // blocks).reshape((-1,) + (1,) * (len(dims) - axis_at - 1))

    level = one(*split[0])
    for cut in split[1:]:
        level = level * one(*cut)
    return level


def normal_values(rng, dims, spread, bound, pieces=(), kind=jnp.bfloat16):
    drawn = jax.random.normal(rng, dims, jnp.float32) * spread
    if len(pieces) > 0:
        drawn = block_levels(rng, dims, pieces, -0.22, 0.18) * drawn
    return jnp.clip(drawn, min=-bound, max=bound).astype(kind)


def setup_inputs(seed: int = 0, part: int = 0) -> dict:
    key_of = jax.random.split(jax.random.key(seed), 3)
    part_splits = jax.random.split(jax.random.fold_in(key_of[2], part), 3)
    return {
        "image": jnp.clip(1.0 * jax.random.uniform(part_splits[0], (ROWS, COLS), jnp.float32) ** block_levels(part_splits[0], (ROWS, COLS), ((1, 8),), -0.2, 0.2), 0.0, 1.0),
        "curves": normal_values(key_of[1], (LEVELS, KNOTS), 0.25, 1.0, ((0, 2),), jnp.float32),
    }


kernel = (0.0625, 0.25, 0.375, 0.25, 0.0625)


def wrap_pad(x, width):
    return jnp.concatenate([x[..., -width:], x, x[..., :width]], axis=-1)


def rows_down(x):
    count = x.shape[-2]
    padded = jnp.pad(x, [(0, 0)] * (x.ndim - 2) + [(2, 2), (0, 0)], mode="edge")
    total = kernel[0] * padded[..., 0:count:2, :]
    for tap in range(1, 5):
        total = total + kernel[tap] * padded[..., tap:tap + count:2, :]
    return total


def cols_down(padded):
    count = padded.shape[-1] - 4
    total = kernel[0] * padded[..., 0:count:2]
    for tap in range(1, 5):
        total = total + kernel[tap] * padded[..., tap:tap + count:2]
    return total


def shrink(x, padder):
    return cols_down(padder(rows_down(x)))


def rows_up(y):
    count = y.shape[-2]
    padded = jnp.pad(y, [(0, 0)] * (y.ndim - 2) + [(1, 1), (0, 0)], mode="edge")
    even = 0.125 * padded[..., 0:count, :] + 0.75 * padded[..., 1:count + 1, :] + 0.125 * padded[..., 2:count + 2, :]
    odd = 0.5 * (padded[..., 1:count + 1, :] + padded[..., 2:count + 2, :])
    stacked = jnp.stack([even, odd], axis=-2)
    return stacked.reshape(y.shape[:-2] + (2 * count, y.shape[-1]))


def cols_up(padded):
    count = padded.shape[-1] - 2
    even = 0.125 * padded[..., 0:count] + 0.75 * padded[..., 1:count + 1] + 0.125 * padded[..., 2:count + 2]
    odd = 0.5 * (padded[..., 1:count + 1] + padded[..., 2:count + 2])
    stacked = jnp.stack([even, odd], axis=-1)
    return stacked.reshape(padded.shape[:-1] + (2 * count,))


def expand(y, padder):
    return cols_up(padder(rows_up(y)))


def wide_two(x):
    return wrap_pad(x, 2)


def wide_one(x):
    return wrap_pad(x, 1)


def remap(image, curve_row, level):
    diff = image - level
    total = level + curve_row[0] * jnp.maximum(0.0, 1.0 - jnp.abs(diff - (-1.0)) * ((KNOTS - 1) / 2))
    for knot in range(1, KNOTS):
        node = -1.0 + 2.0 * knot / (KNOTS - 1)
        total = total + curve_row[knot] * jnp.maximum(0.0, 1.0 - jnp.abs(diff - node) * ((KNOTS - 1) / 2))
    return total


def reference(image, curves):
    guide = [image]
    for step in range(PYR - 1):
        guide.append(shrink(guide[-1], wide_two))

    def accumulate(index, coeffs):
        level = index.astype(jnp.float32) / (LEVELS - 1)
        curve_row = lax.dynamic_index_in_dim(curves, index, 0, keepdims=False)
        gauss = [remap(image, curve_row, level)]
        for step in range(PYR - 1):
            gauss.append(shrink(gauss[-1], wide_two))
        result = []
        for step in range(PYR - 1):
            detail = gauss[step] - expand(gauss[step + 1], wide_one)
            weight = jnp.maximum(0.0, 1.0 - (LEVELS - 1) * jnp.abs(guide[step] - level))
            result.append(coeffs[step] + weight * detail)
        return tuple(result)

    start = tuple(jnp.zeros_like(guide[step]) for step in range(PYR - 1))
    coeffs = lax.fori_loop(0, LEVELS, accumulate, start)
    out = guide[-1]
    for step in range(PYR - 2, -1, -1):
        out = coeffs[step] + expand(out, wide_one)
    return out
```

```python
import functools

import jax
import jax.numpy as jnp
from jax import lax
from jax.experimental import pallas as pl
from jax.experimental.pallas import tpu as pltpu
from jax.sharding import PartitionSpec as P

LEVELS = 16
KNOTS = 17
PYR = 6

SUB = 8
LANES = 128
RIM = 128
COPIES = LEVELS + 1

VMEM = pl.BlockSpec(memory_space=pltpu.VMEM)
HBM = pl.BlockSpec(memory_space=pltpu.HBM)
PARAMS = pltpu.CompilerParams(vmem_limit_bytes=20 * 1024 * 1024)


def iota(shape, dim):
    return lax.broadcasted_iota(jnp.int32, shape, dim)


def down_taps(distance):
    size = jnp.abs(distance)
    value = jnp.where(size == 0, 6.0, jnp.where(size == 1, 4.0, jnp.where(size == 2, 1.0, 0.0)))
    return (value / 256.0).astype(jnp.bfloat16)


def up_taps(distance):
    size = jnp.abs(distance)
    value = jnp.where(size == 0, 0.75, jnp.where(size == 1, 0.5, jnp.where(size == 2, 0.125, 0.0)))
    return (value / 8.0).astype(jnp.bfloat16)


def twice(table):
    return jnp.concatenate([table, table], axis=0)


def halves(x):
    high = x.astype(jnp.bfloat16)
    low = (x - high.astype(jnp.float32)).astype(jnp.bfloat16)
    return jnp.concatenate([high, low], axis=-1)


def dot(x, table):
    return jnp.dot(x, table, preferred_element_type=jnp.float32)


def shift_down(x):
    return pltpu.roll(x, 1, axis=x.ndim - 2)


def shift_up(x):
    return pltpu.roll(x, SUB - 1, axis=x.ndim - 2)


def sublane(x):
    return iota(x.shape, x.ndim - 2)


def rows_down(planes):
    first, last = planes[0], planes[-1]
    top = sublane(first) == 0
    minus2 = jnp.where(top, first, shift_down(planes[-2]))
    minus1 = jnp.where(top, first, shift_down(last))
    plus = jnp.where(sublane(first) == SUB - 1, last, shift_up(first))
    padded = [minus2, minus1] + list(planes) + [plus]
    out = []
    for at in range(0, len(planes), 2):
        a, b, c, d, e = padded[at:at + 5]
        out.append((a + e) + 4.0 * (b + d) + 6.0 * c)
    return out


def padded_for_up(planes):
    first, last = planes[0], planes[-1]
    below = jnp.where(sublane(first) == 0, first, shift_down(last))
    above = jnp.where(sublane(first) == SUB - 1, last, shift_up(first))
    return [below] + list(planes) + [above]


def rows_up(planes):
    padded = padded_for_up(planes)
    out = []
    for at in range(len(planes)):
        a, b, c = padded[at:at + 3]
        out.append((a + c) + 6.0 * b)
        out.append(4.0 * (b + c))
    return out


def look_up(table, index):
    return jnp.take_along_axis(table, index, axis=0, mode="promise_in_bounds")


def cell(x, cells):
    scaled = x * float(cells)
    index = jnp.clip(scaled.astype(jnp.int32), 0, cells - 1)
    return index, scaled - index.astype(jnp.float32)


def curve_tables(curve_row, k):
    steps = (KNOTS - 1) // 2
    turn = steps * k // (LEVELS - 1)
    phase = (steps * k % (LEVELS - 1)) / (LEVELS - 1)
    width = curve_row.shape[-1]
    row = jnp.broadcast_to(curve_row, (SUB, width))
    offset = iota((SUB, width), 1) - iota((SUB, width), 0)

    def node(shift):
        at = jnp.where(offset == steps - turn + shift, row, 0.0)
        return jnp.sum(at, axis=1, keepdims=True)

    left, middle, right = node(-1), node(0), node(1)
    slope = middle - left
    bend = (right - middle) - slope
    start = (k / (LEVELS - 1) + middle) - phase * slope - phase * bend
    spread = lambda v: jnp.broadcast_to(v, (SUB, LANES))
    return spread(start), spread(slope), spread(bend), jnp.full((SUB, LANES), phase, jnp.float32)


def remap(tables, index, rest):
    start, slope, bend, phase = tables
    bent = jnp.maximum(rest, phase)
    return look_up(start, index) + look_up(slope, index) * rest + look_up(bend, index) * bent


def stage_kernel(image_ref, whole_ref, edge_ref, sems):
    lvl = lax.axis_index("lvl")
    tiles = whole_ref.shape[0]
    start = pl.multiple_of(lvl * (tiles - 1) * LANES, LANES)
    copies = [pltpu.make_async_copy(image_ref.at[:, pl.ds(start, RIM)], edge_ref, sems.at[tiles])]
    for tile in range(tiles):
        source = image_ref.at[:, tile * LANES:(tile + 1) * LANES]
        copies.append(pltpu.make_async_copy(source, whole_ref.at[tile], sems.at[tile]))
    for copy in copies:
        copy.start()
    for copy in copies:
        copy.wait()


def put_kernel(half_ref, out_ref, sems, lvl):
    tiles = half_ref.shape[0]
    copies = []
    for tile in range(tiles):
        start = pl.multiple_of((lvl * tiles + tile) * LANES, LANES)
        target = out_ref.at[:, pl.ds(start, LANES)]
        copies.append(pltpu.make_async_copy(half_ref.at[tile], target, sems.at[tile]))
    for copy in copies:
        copy.start()
    for copy in copies:
        copy.wait()


def put_mine_kernel(mine_ref, out_ref, sems):
    put_kernel(mine_ref, out_ref, sems, lax.axis_index("lvl"))


def put_theirs_kernel(theirs_ref, begun_ref, out_ref, sems):
    put_kernel(theirs_ref, out_ref, sems, 1 - lax.axis_index("lvl"))


def pick(index, values):
    low = high = None
    before = None
    for k in range(LEVELS):
        value = values(k)
        mask = index == k if k < LEVELS - 1 else None
        if k == 0:
            low = value
        elif k < LEVELS - 1:
            low = jnp.where(mask, value, low)
        if k == 1:
            high = value
        elif k > 1:
            high = jnp.where(before, value, high)
        before = mask
    return low, high


def own_kernel(image_ref, mine_ref, other_ref, gauss_ref, tone_ref, index_ref, rest_ref, table_ref,
               x_scr, cell_scr, rest_scr, low_scr, high_scr, part_scr, down_scr):
    lvl = lax.axis_index("lvl")
    tiles, rows, _ = image_ref.shape
    planes = rows // SUB
    half = tiles * LANES // 2
    own = half + RIM

    at = iota((own, half), 0)
    place = jnp.where((at >= half) & (lvl == 1), at - own, at)
    down = down_taps(place - 2 * (iota((own, half), 1) - RIM // 2))
    down_scr[0:own, :] = down
    down_scr[own:2 * own, :] = down

    first = jnp.where(lvl == 0, mine_ref[...], other_ref[...])
    second = jnp.where(lvl == 0, other_ref[...], mine_ref[...])
    for k in range(LEVELS):
        source = first if k < LEVELS // 2 else second
        row = k % (LEVELS // 2)
        for kind, table in enumerate(curve_tables(source[row:row + 1, :], k)):
            table_ref[k, kind] = table

    sources = [lvl * (tiles // 2) + tile for tile in range(tiles // 2)] + [tiles // 2 - lvl]
    for p in range(planes):
        for tile, source in enumerate(sources):
            span = slice(tile * LANES, (tile + 1) * LANES)
            x_scr[p, :, span] = image_ref[source, pl.ds(p, SUB, stride=planes), :]
    for p in range(planes):
        x = x_scr[p]
        index, rest = cell(x, (KNOTS - 1) // 2)
        cell_scr[p] = index
        rest_scr[p] = rest
        index, rest = cell(x[:, 0:half], LEVELS - 1)
        index_ref[p] = index
        rest_ref[p] = rest

    def store(k, column, reduced):
        for pair in range(planes // 4):
            both = jnp.concatenate(reduced[2 * pair:2 * pair + 2], axis=0)
            high = both.astype(jnp.bfloat16)
            low = (both - high.astype(jnp.float32)).astype(jnp.bfloat16)
            part_scr[pair, k, :, column:column + LANES] = high
            part_scr[pair, k, :, own + column:own + column + LANES] = low

    def one_copy(k, carry):
        tables = tuple(table_ref[k, kind] for kind in range(4))
        for column in range(0, own, LANES):
            span = slice(column, column + LANES)
            mapped = [remap(tables, cell_scr[p, :, span], rest_scr[p, :, span]) for p in range(planes)]
            if column < half:
                for p in range(planes):
                    index = index_ref[p, :, span]
                    low_scr[p, :, span] = jnp.where(index == k, mapped[p], low_scr[p, :, span])
                    high_scr[p, :, span] = jnp.where(index == k - 1, mapped[p], high_scr[p, :, span])
            store(k, column, rows_down(mapped))
        return carry

    lax.fori_loop(0, LEVELS, one_copy, 0)
    for column in range(0, own, LANES):
        store(LEVELS, column, rows_down([x_scr[p, :, column:column + LANES] for p in range(planes)]))
    for p in range(planes):
        tone_ref[p] = low_scr[p] + rest_ref[p] * (high_scr[p] - low_scr[p])

    part = part_scr[...].reshape(-1, 2 * own)
    gauss_ref[...] = dot(part, down_scr[...]).reshape(gauss_ref.shape)


def rest_kernel(halo_ref, gauss_in_ref, tone_ref, index_ref, rest_ref, table_ref, out_ref,
                x_scr, cell_scr, frac_scr, part_scr, gauss_scr, up_scr):
    lvl = lax.axis_index("lvl")
    rows = halo_ref.shape[0]
    planes = rows // SUB
    half = out_ref.shape[0] * LANES

    for p in range(planes):
        x = halo_ref[pl.ds(p, SUB, stride=planes), :]
        x_scr[p] = x
        index, rest = cell(x, (KNOTS - 1) // 2)
        cell_scr[p] = index
        frac_scr[p] = rest

    def store(k, reduced):
        for pair in range(planes // 4):
            both = jnp.concatenate(reduced[2 * pair:2 * pair + 2], axis=0)
            part_scr[pair, k] = halves(both)

    def one_copy(k, carry):
        tables = tuple(table_ref[k, kind] for kind in range(4))
        store(k, rows_down([remap(tables, cell_scr[p], frac_scr[p]) for p in range(planes)]))
        return carry

    lax.fori_loop(0, LEVELS, one_copy, 0)
    store(LEVELS, rows_down([x_scr[p] for p in range(planes)]))
    at = iota((RIM, LANES), 0)
    place = jnp.where(lvl == 0, at - RIM, at + half)
    target = iota((RIM, LANES), 1) + lvl * LANES - RIM // 2
    share = dot(part_scr[...].reshape(-1, 2 * RIM), twice(down_taps(place - 2 * target)))
    share = share.reshape(planes // 4, COPIES, 2, SUB, LANES)
    near = pl.multiple_of(lvl * LANES, LANES)
    away = pl.multiple_of((1 - lvl) * LANES, LANES)
    gauss_scr[:, :, :, :, pl.ds(near, LANES)] = gauss_in_ref[:, :, :, :, pl.ds(near, LANES)] + share
    gauss_scr[:, :, :, :, pl.ds(away, LANES)] = gauss_in_ref[:, :, :, :, pl.ds(away, LANES)]

    gauss = [None, [gauss_scr[p // 2, :, p % 2] for p in range(planes // 2)]]
    small = down_taps(iota((LANES, LANES), 0) - 2 * iota((LANES, LANES), 1))
    wide = down_taps(iota((half, LANES), 0) - 2 * iota((half, LANES), 1))
    for level in range(1, PYR - 1):
        reduced = rows_down(gauss[level])
        count = len(reduced)
        stacked = jnp.concatenate(reduced, axis=0)
        stacked = stacked.reshape(-1, stacked.shape[-1])
        result = dot(halves(stacked), twice(wide if level == 1 else small))
        result = result.reshape(count, COPIES, SUB, LANES)
        gauss.append([result[p] for p in range(count)])

    full = twice(up_taps(2 * iota((half, half), 0) - (iota((half, half), 1) + RIM)))
    source = gauss_scr[:, 0:LEVELS].reshape(-1, half)
    up_scr[...] = dot(halves(source), full).reshape(up_scr.shape)

    narrow = twice(up_taps(2 * iota((LANES, half), 0) - iota((LANES, half), 1)))
    out = [gauss[PYR - 1][0][LEVELS]]
    for level in range(PYR - 2, 0, -1):
        columns = half if level == 1 else LANES
        table = narrow[:, 0:columns]
        coarse = gauss[level + 1]
        count = len(coarse)
        stacked = jnp.concatenate([plane[0:LEVELS] for plane in coarse], axis=0).reshape(-1, LANES)
        wider = dot(halves(stacked), table).reshape(count, LEVELS, SUB, columns)
        raised = rows_up([wider[p] for p in range(count)])
        base = dot(halves(jnp.concatenate(out, axis=0)), table).reshape(count, SUB, columns)
        base = rows_up([base[p] for p in range(count)])
        out = []
        for p in range(2 * count):
            here = gauss[level][p]
            index, rest = cell(here[LEVELS], LEVELS - 1)
            low, high = pick(index, lambda k: here[k] - raised[p][k])
            out.append(low + rest * (high - low) + base[p])

    base = dot(halves(jnp.concatenate(out, axis=0)), full).reshape(planes // 2, SUB, half)
    base = rows_up([base[p] for p in range(planes // 2)])
    columns_up = [up_scr[p // 2, :, p % 2] for p in range(planes // 2)]
    first, last = columns_up[0], columns_up[-1]
    padded = padded_for_up(columns_up)
    for p in range(planes):
        a, b, c = padded[p // 2], padded[p // 2 + 1], padded[p // 2 + 2]
        if p % 2 == 0:
            low, high = pick(index_ref[p], lambda k: (a[k] + c[k]) + 6.0 * b[k])
            detail = low + rest_ref[p] * (high - low)
        else:
            low, high = pick(index_ref[p], lambda k: b[k] + c[k])
            detail = 4.0 * (low + rest_ref[p] * (high - low))
        toned = (tone_ref[p] - detail) + base[p]
        for tile in range(half // LANES):
            out_ref[tile, pl.ds(p, SUB, stride=planes), :] = toned[:, tile * LANES:(tile + 1) * LANES]


def call(kernel, name, in_specs, out_shape, scratch, out_space=VMEM, **others):
    return pl.pallas_call(
        kernel,
        name=name,
        in_specs=in_specs,
        out_specs=jax.tree.map(lambda _: out_space, out_shape),
        out_shape=out_shape,
        scratch_shapes=scratch,
        compiler_params=PARAMS,
        **others,
    )


def body(image, curves):
    rows, width = image.shape
    half = width // 2
    own = half + RIM
    planes = rows // SUB
    lvl = lax.axis_index("lvl")
    tiles = lax.axis_size("tile")
    f32 = lambda *shape: jax.ShapeDtypeStruct(shape, jnp.float32)
    i32 = lambda *shape: jax.ShapeDtypeStruct(shape, jnp.int32)
    swap = [(0, 1), (1, 0)]

    other_curves = lax.ppermute(curves, "lvl", swap)
    whole, edge = call(
        stage_kernel, "stage", [HBM], [f32(width // LANES, rows, LANES), f32(rows, RIM)],
        [pltpu.SemaphoreType.DMA((width // LANES + 1,))],
    )(image)
    edge, other_curves = lax.optimization_barrier((edge, other_curves))
    pairs = []
    for tile in range(tiles):
        pairs.append((2 * tile + 1, 2 * ((tile + 1) % tiles)))
        pairs.append((2 * tile, 2 * ((tile - 1) % tiles) + 1))
    halo = lax.ppermute(edge, ("tile", "lvl"), pairs)

    gauss, tone, index, rest, tables = call(
        own_kernel, "own", [VMEM] * 3,
        [f32(planes // 4, COPIES, 2, SUB, half), f32(planes, SUB, half), i32(planes, SUB, half),
         f32(planes, SUB, half), f32(LEVELS, 4, SUB, LANES)],
        [pltpu.VMEM((planes, SUB, own), jnp.float32), pltpu.VMEM((planes, SUB, own), jnp.int32),
         pltpu.VMEM((planes, SUB, own), jnp.float32), pltpu.VMEM((planes, SUB, half), jnp.float32),
         pltpu.VMEM((planes, SUB, half), jnp.float32),
         pltpu.VMEM((planes // 4, COPIES, 2 * SUB, 2 * own), jnp.bfloat16),
         pltpu.VMEM((2 * own, half), jnp.bfloat16)],
    )(whole, curves, other_curves)
    mine = call(
        rest_kernel, "rest", [VMEM] * 6, f32(half // LANES, rows, LANES),
        [pltpu.VMEM((planes, SUB, RIM), jnp.float32), pltpu.VMEM((planes, SUB, RIM), jnp.int32),
         pltpu.VMEM((planes, SUB, RIM), jnp.float32),
         pltpu.VMEM((planes // 4, COPIES, 2 * SUB, 2 * RIM), jnp.bfloat16),
         pltpu.VMEM((planes // 4, COPIES, 2, SUB, half), jnp.float32),
         pltpu.VMEM((planes // 4, LEVELS, 2, SUB, half), jnp.float32)],
    )(halo, gauss, tone, index, rest, tables)
    theirs = lax.ppermute(mine, "lvl", swap)
    sems = [pltpu.SemaphoreType.DMA((half // LANES,))]
    begun = call(put_mine_kernel, "put_mine", [VMEM], f32(rows, width), sems, HBM)(mine)
    return call(
        put_theirs_kernel, "put_theirs", [VMEM, HBM], f32(rows, width), sems, HBM, input_output_aliases={1: 0}
    )(theirs, begun)


def solution(mesh):
    placed = (P("band", "tile"), P("lvl", None))
    return jax.shard_map(
        body, mesh=mesh, in_specs=placed, out_specs=P("band", "tile"), check_vma=False
    )
```

```python
import functools

import jax
import jax.numpy as jnp
from jax import lax
from jax.experimental import pallas as pl
from jax.experimental.pallas import tpu as pltpu
from jax.sharding import PartitionSpec as P

LEVELS = 16
KNOTS = 17
PYR = 6

SUB = 8
LANES = 128
RIM = 128
FIRST = 2
STACK = FIRST + LEVELS

VMEM = pl.BlockSpec(memory_space=pltpu.VMEM)
HBM = pl.BlockSpec(memory_space=pltpu.HBM)
PARAMS = pltpu.CompilerParams(vmem_limit_bytes=20 * 1024 * 1024)


def iota(shape, dim):
    return lax.broadcasted_iota(jnp.int32, shape, dim)


def down_taps(distance):
    size = jnp.abs(distance)
    value = jnp.where(size == 0, 6.0, jnp.where(size == 1, 4.0, jnp.where(size == 2, 1.0, 0.0)))
    return (value / 256.0).astype(jnp.bfloat16)


def up_taps(distance):
    size = jnp.abs(distance)
    value = jnp.where(size == 0, 0.75, jnp.where(size == 1, 0.5, jnp.where(size == 2, 0.125, 0.0)))
    return (value / 8.0).astype(jnp.bfloat16)


def twice(table):
    return jnp.concatenate([table, table], axis=0)


def halves(x):
    high = x.astype(jnp.bfloat16)
    low = (x - high.astype(jnp.float32)).astype(jnp.bfloat16)
    return jnp.concatenate([high, low], axis=-1)


def dot(x, table):
    return jnp.dot(x, table, preferred_element_type=jnp.float32)


def shift_down(x):
    return pltpu.roll(x, 1, axis=x.ndim - 2)


def shift_up(x):
    return pltpu.roll(x, SUB - 1, axis=x.ndim - 2)


def sublane(x):
    return iota(x.shape, x.ndim - 2)


def rows_down(planes, scaled=False):
    first, last = planes[0], planes[-1]
    top = sublane(first) == 0
    quad = (lambda x: x) if scaled else (lambda x: 4.0 * x)
    minus2 = jnp.where(top, first, shift_down(planes[-2]))
    minus1 = jnp.where(top, 4.0 * first if scaled else first, shift_down(last))
    plus = jnp.where(sublane(first) == SUB - 1, 0.25 * last if scaled else last, shift_up(first))
    padded = [minus2, minus1] + list(planes) + [plus]
    out = []
    for at in range(0, len(planes), 2):
        a, b, c, d, e = padded[at:at + 5]
        out.append((a + e) + quad(b + d) + 6.0 * c)
    return out


def padded_for_up(planes):
    first, last = planes[0], planes[-1]
    below = jnp.where(sublane(first) == 0, first, shift_down(last))
    above = jnp.where(sublane(first) == SUB - 1, last, shift_up(first))
    return [below] + list(planes) + [above]


def rows_up(planes):
    padded = padded_for_up(planes)
    out = []
    for at in range(len(planes)):
        a, b, c = padded[at:at + 3]
        out.append((a + c) + 6.0 * b)
        out.append(4.0 * (b + c))
    return out


GATHER = lax.GatherDimensionNumbers(
    offset_dims=(),
    collapsed_slice_dims=(0,),
    start_index_map=(0,),
    operand_batching_dims=(1,),
    start_indices_batching_dims=(1,),
)


def look_up(table, index):
    return lax.gather(
        table, index[..., None], GATHER, (1, 1), mode=lax.GatherScatterMode.PROMISE_IN_BOUNDS
    )


def cell(x, cells):
    scaled = x * float(cells)
    index = jnp.clip(scaled.astype(jnp.int32), 0, cells - 1)
    return index, scaled - index.astype(jnp.float32)


def curve_tables(curve_row, k):
    steps = (KNOTS - 1) // 2
    turn = steps * k // (LEVELS - 1)
    phase = (steps * k % (LEVELS - 1)) / (LEVELS - 1)
    width = curve_row.shape[-1]
    row = jnp.broadcast_to(curve_row, (SUB, width))
    offset = iota((SUB, width), 1) - iota((SUB, width), 0)

    def node(shift):
        at = jnp.where(offset == steps - turn + shift, row, 0.0)
        return jnp.sum(at, axis=1, keepdims=True)

    left, middle, right = node(-1), node(0), node(1)
    slope = middle - left
    bend = (right - middle) - slope
    start = (k / (LEVELS - 1) + middle) - phase * slope - phase * bend
    spread = lambda v: jnp.broadcast_to(v, (SUB, LANES))
    return spread(start), spread(slope), spread(bend), jnp.full((SUB, LANES), phase, jnp.float32)


def remap(tables, index, rest):
    start, slope, bend, phase = tables
    bent = jnp.maximum(rest, phase)
    return look_up(start, index) + look_up(slope, index) * rest + look_up(bend, index) * bent


def remap_pair(table_ref, first, planes, index_of, rest_of):
    even, odd = [], []
    for copy in range(2):
        start, slope, bend, phase = [table_ref[first + copy, kind] for kind in range(4)]
        even.append((start, slope, bend, phase))
        odd.append((4.0 * start, 4.0 * slope, 4.0 * bend, phase))
    mapped = [[], []]
    for p in range(planes):
        index, rest = index_of(p), rest_of(p)
        for copy in range(2):
            mapped[copy].append(remap((odd if p % 2 else even)[copy], index, rest))
    return mapped


def tone_tables(low, high):
    middle = (KNOTS - 1) // 2
    scale = middle / (LEVELS - 1)
    spread = lambda v: jnp.broadcast_to(v, (SUB, LANES))
    sub = iota((SUB, LANES), 0)

    def parts(curves, k):
        level = (sub + k).astype(jnp.float32) / (LEVELS - 1)
        left, centre, right = [spread(curves[:, at:at + 1]) for at in (middle - 1, middle, middle + 1)]
        return level + centre, scale * (right - centre), scale * (centre - left)

    def following(x, then):
        return jnp.where(sub == SUB - 1, spread(then[0:1, :]), shift_up(x))

    one, two = parts(low, 0), parts(high, LEVELS // 2)
    tables = []
    for here, then in ((one, two), (two, two)):
        base = here[0]
        tables.append((base, following(here[0], then[0]) - base, here[1] - following(here[2], then[2])))
    return tables


def tone(tables, x):
    index, rest = cell(x, LEVELS - 1)
    lower = index < SUB
    place = index & (SUB - 1)
    base, step, arc = [
        jnp.where(lower, look_up(one, place), look_up(two, place)) for one, two in zip(*tables)
    ]
    return base + rest * (step + (1.0 - rest) * arc)


def scaled_level(x):
    place = x * float(LEVELS - 1)
    half = 0.5 * place
    return place, jnp.abs(1.0 - 2.0 * (half - jnp.floor(half)))


def stage_kernel(image_ref, whole_ref, edge_ref, own_ref, rim_ref, wide_ref, small_ref, full_ref,
                 narrow_ref, sems):
    lvl = lax.axis_index("lvl")
    tiles = whole_ref.shape[0]
    start = pl.multiple_of(lvl * (tiles - 1) * LANES, LANES)
    copies = [pltpu.make_async_copy(image_ref.at[:, pl.ds(start, RIM)], edge_ref, sems.at[tiles])]
    for tile in range(tiles):
        source = image_ref.at[:, tile * LANES:(tile + 1) * LANES]
        copies.append(pltpu.make_async_copy(source, whole_ref.at[tile], sems.at[tile]))
    for copy in copies:
        copy.start()

    half = tiles * LANES // 2

    def put(ref, shape, value):
        table = value(iota(shape, 0), iota(shape, 1))
        ref[0:shape[0], :] = table
        ref[shape[0]:2 * shape[0], :] = table

    inner = jnp.where(lvl == 1, half + RIM, 0)
    outer = jnp.where(lvl == 0, -RIM, half)
    put(own_ref, (half + RIM, half),
        lambda i, j: down_taps(jnp.where(i >= half, i - inner, i) - 2 * (j - RIM // 2)))
    put(rim_ref, (RIM, LANES), lambda i, j: down_taps(i + outer - 2 * (j + lvl * LANES - RIM // 2)))
    put(wide_ref, (half, LANES), lambda i, j: down_taps(i - 2 * j))
    put(small_ref, (LANES, LANES), lambda i, j: down_taps(i - 2 * j))
    put(full_ref, (half, half), lambda i, j: up_taps(2 * i - (j + RIM)))
    put(narrow_ref, (LANES, half), lambda i, j: up_taps(2 * i - j))
    for copy in copies:
        copy.wait()


def put_kernel(half_ref, out_ref, sems, lvl):
    tiles = half_ref.shape[0]
    copies = []
    for tile in range(tiles):
        start = pl.multiple_of((lvl * tiles + tile) * LANES, LANES)
        target = out_ref.at[:, pl.ds(start, LANES)]
        copies.append(pltpu.make_async_copy(half_ref.at[tile], target, sems.at[tile]))
    for copy in copies:
        copy.start()
    for copy in copies:
        copy.wait()


def put_mine_kernel(mine_ref, out_ref, sems):
    put_kernel(mine_ref, out_ref, sems, lax.axis_index("lvl"))


def put_theirs_kernel(theirs_ref, begun_ref, out_ref, sems):
    put_kernel(theirs_ref, out_ref, sems, 1 - lax.axis_index("lvl"))


def pick(place, weight, values):
    even, odd = values(0), values(1)
    for k in range(2, LEVELS, 2):
        even = jnp.where(place >= float(k - 1), values(k), even)
        odd = jnp.where(place >= float(k), values(k + 1), odd)
    return odd + weight * (even - odd)


def split_store(ref, reduced, column, width):
    for pair in range(len(reduced) // 2):
        both = jnp.concatenate(reduced[2 * pair:2 * pair + 2], axis=0)
        high = both.astype(jnp.bfloat16)
        low = (both - high.astype(jnp.float32)).astype(jnp.bfloat16)
        ref[pair, :, column:column + LANES] = high
        ref[pair, :, width + column:width + column + LANES] = low


def scale_odd(planes):
    return [4.0 * x if p % 2 else x for p, x in enumerate(planes)]


def own_kernel(image_ref, mine_ref, other_ref, down_ref, gauss_ref, tone_ref, place_ref, weight_ref,
               table_ref, x_scr, cell_scr, rest_scr, part_scr):
    lvl = lax.axis_index("lvl")
    tiles, rows, _ = image_ref.shape
    planes = rows // SUB
    half = tiles * LANES // 2
    own = half + RIM
    pairs = LEVELS // 2

    first = jnp.where(lvl == 0, mine_ref[...], other_ref[...])
    second = jnp.where(lvl == 0, other_ref[...], mine_ref[...])
    for k in range(LEVELS):
        source = first if k < pairs else second
        row = k % pairs
        for kind, table in enumerate(curve_tables(source[row:row + 1, :], k)):
            table_ref[k, kind] = table
    tones = tone_tables(first, second)

    sources = [lvl * (tiles // 2) + tile for tile in range(tiles // 2)] + [tiles // 2 - lvl]
    for tile, source in enumerate(sources):
        span = slice(tile * LANES, (tile + 1) * LANES)
        for p in range(planes):
            x = image_ref[source, pl.ds(p, SUB, stride=planes), :]
            x_scr[p, :, span] = x
            cell_scr[p, :, span], rest_scr[p, :, span] = cell(x, (KNOTS - 1) // 2)
            if tile < tiles // 2:
                tone_ref[p, :, span] = tone(tones, x)
                place_ref[p, :, span], weight_ref[p, :, span] = scaled_level(x)

    def multiply(slot, target):
        part = part_scr[slot].reshape(-1, 2 * own)
        result = dot(part, down_ref[...]).reshape(2, planes // 4, 2, SUB, half)
        for copy in range(2):
            for tile in range(half // LANES):
                span = slice(tile * LANES, (tile + 1) * LANES)
                gauss_ref[tile, :, target + copy] = result[copy, :, :, :, span]

    for column in range(0, own, LANES):
        guide = scale_odd([x_scr[p, :, column:column + LANES] for p in range(planes)])
        reduced = rows_down(guide, scaled=True)
        for copy in range(2):
            split_store(part_scr.at[1, copy], reduced, column, own)

    def one_pair(step, carry):
        slot = lax.rem(step, 2)
        multiply(1 - slot, 2 * step)
        for column in range(0, own, LANES):
            span = slice(column, column + LANES)
            mapped = remap_pair(
                table_ref, 2 * step, planes, lambda p: cell_scr[p, :, span], lambda p: rest_scr[p, :, span]
            )
            for copy in range(2):
                split_store(part_scr.at[slot, copy], rows_down(mapped[copy], scaled=True), column, own)
        return carry

    lax.fori_loop(0, pairs, one_pair, 0)
    multiply((pairs - 1) % 2, 2 * pairs)


def rest_kernel(halo_ref, gauss_in_ref, tone_ref, place_ref, weight_ref, table_ref, rim_ref, wide_ref,
                small_ref, full_ref, narrow_ref, out_ref, gauss_ref, x_scr, cell_scr, rest_scr, part_scr,
                up_scr):
    lvl = lax.axis_index("lvl")
    rows = halo_ref.shape[0]
    planes = rows // SUB
    tiles = out_ref.shape[0]
    half = tiles * LANES
    pairs = LEVELS // 2

    for p in range(planes):
        x = halo_ref[pl.ds(p, SUB, stride=planes), :]
        x_scr[p] = x
        cell_scr[p], rest_scr[p] = cell(x, (KNOTS - 1) // 2)

    def multiply(slot, target):
        part = part_scr[slot].reshape(-1, 2 * RIM)
        result = dot(part, rim_ref[...]).reshape(2, planes // 4, 2, SUB, LANES)
        for copy in range(2):
            gauss_ref[lvl, :, target + copy] = gauss_in_ref[lvl, :, target + copy] + result[copy]

    reduced = rows_down(scale_odd([x_scr[p] for p in range(planes)]), scaled=True)
    for copy in range(2):
        split_store(part_scr.at[1, copy], reduced, 0, RIM)

    def one_pair(step, carry):
        slot = lax.rem(step, 2)
        multiply(1 - slot, 2 * step)
        mapped = remap_pair(table_ref, 2 * step, planes, lambda p: cell_scr[p], lambda p: rest_scr[p])
        for copy in range(2):
            split_store(part_scr.at[slot, copy], rows_down(mapped[copy], scaled=True), 0, RIM)
        return carry

    lax.fori_loop(0, pairs, one_pair, 0)
    multiply((pairs - 1) % 2, 2 * pairs)

    def level_one(p, start=0):
        parts = [gauss_ref[tile, p // 2, start:, p % 2] for tile in range(tiles)]
        return jnp.concatenate(parts, axis=-1)

    source = jnp.concatenate([level_one(p, FIRST) for p in range(planes // 2)], axis=0)
    up_scr[...] = dot(halves(source.reshape(-1, half)), full_ref[...]).reshape(up_scr.shape)

    gauss = [None, [level_one(p) for p in range(planes // 2)]]
    for level in range(1, PYR - 1):
        reduced = rows_down(gauss[level])
        count = len(reduced)
        stacked = jnp.concatenate(reduced, axis=0)
        stacked = stacked.reshape(-1, stacked.shape[-1])
        result = dot(halves(stacked), (wide_ref if level == 1 else small_ref)[...])
        result = result.reshape(count, STACK, SUB, LANES)
        gauss.append([result[p] for p in range(count)])

    out = [gauss[PYR - 1][0][0]]
    for level in range(PYR - 2, 0, -1):
        columns = half if level == 1 else LANES
        table = narrow_ref[:, 0:columns]
        coarse = gauss[level + 1]
        count = len(coarse)
        stacked = jnp.concatenate([plane[FIRST:] for plane in coarse], axis=0).reshape(-1, LANES)
        wider = dot(halves(stacked), table).reshape(count, LEVELS, SUB, columns)
        raised = rows_up([wider[p] for p in range(count)])
        base = dot(halves(jnp.concatenate(out, axis=0)), table).reshape(count, SUB, columns)
        base = rows_up([base[p] for p in range(count)])
        out = []
        for p in range(2 * count):
            here = gauss[level][p]
            place, weight = scaled_level(here[0])
            out.append(pick(place, weight, lambda k: here[FIRST + k] - raised[p][k]) + base[p])

    base = dot(halves(jnp.concatenate(out, axis=0)), full_ref[...]).reshape(planes // 2, SUB, half)
    base = rows_up([base[p] for p in range(planes // 2)])
    padded = padded_for_up([up_scr[p] for p in range(planes // 2)])
    for p in range(planes):
        a, b, c = padded[p // 2], padded[p // 2 + 1], padded[p // 2 + 2]
        if p % 2 == 0:
            detail = pick(place_ref[p], weight_ref[p], lambda k: (a[k] + c[k]) + 6.0 * b[k])
        else:
            detail = 4.0 * pick(place_ref[p], weight_ref[p], lambda k: b[k] + c[k])
        toned = (tone_ref[p] - detail) + base[p]
        for tile in range(tiles):
            out_ref[tile, pl.ds(p, SUB, stride=planes), :] = toned[:, tile * LANES:(tile + 1) * LANES]


def call(kernel, name, in_specs, out_shape, scratch, out_space=VMEM, **others):
    return pl.pallas_call(
        kernel,
        name=name,
        in_specs=in_specs,
        out_specs=jax.tree.map(lambda _: out_space, out_shape),
        out_shape=out_shape,
        scratch_shapes=scratch,
        compiler_params=PARAMS,
        **others,
    )


def body(image, curves):
    rows, width = image.shape
    half = width // 2
    own = half + RIM
    planes = rows // SUB
    tiles = half // LANES
    lvl = lax.axis_index("lvl")
    count = lax.axis_size("tile")
    f32 = lambda *shape: jax.ShapeDtypeStruct(shape, jnp.float32)
    b16 = lambda *shape: jax.ShapeDtypeStruct(shape, jnp.bfloat16)
    fast = lambda *shape: pltpu.VMEM(shape, jnp.float32)
    fast_int = lambda *shape: pltpu.VMEM(shape, jnp.int32)
    fast_half = lambda *shape: pltpu.VMEM(shape, jnp.bfloat16)
    swap = [(0, 1), (1, 0)]

    other_curves = lax.ppermute(curves, "lvl", swap)
    whole, edge, down, rim, wide, small, full, narrow = call(
        stage_kernel, "stage", [HBM],
        [f32(2 * tiles, rows, LANES), f32(rows, RIM), b16(2 * own, half), b16(2 * RIM, LANES),
         b16(2 * half, LANES), b16(2 * LANES, LANES), b16(2 * half, half), b16(2 * LANES, half)],
        [pltpu.SemaphoreType.DMA((2 * tiles + 1,))],
    )(pltpu.with_memory_space_constraint(image, pltpu.HBM))
    edge, other_curves = lax.optimization_barrier((edge, other_curves))
    pairs = []
    for tile in range(count):
        pairs.append((2 * tile + 1, 2 * ((tile + 1) % count)))
        pairs.append((2 * tile, 2 * ((tile - 1) % count) + 1))
    halo = lax.ppermute(edge, ("tile", "lvl"), pairs)

    gauss_shape = f32(tiles, planes // 4, STACK, 2, SUB, LANES)
    gauss, toned, place, weight, tables = call(
        own_kernel, "own", [VMEM] * 4,
        [gauss_shape, f32(planes, SUB, half), f32(planes, SUB, half), f32(planes, SUB, half),
         f32(LEVELS, 4, SUB, LANES)],
        [fast(planes, SUB, own), fast_int(planes, SUB, own), fast(planes, SUB, own),
         fast_half(2, 2, planes // 4, 2 * SUB, 2 * own)],
    )(whole, curves, other_curves, down)
    mine, _ = call(
        rest_kernel, "rest", [VMEM] * 11, [f32(tiles, rows, LANES), gauss_shape],
        [fast(planes, SUB, RIM), fast_int(planes, SUB, RIM), fast(planes, SUB, RIM),
         fast_half(2, 2, planes // 4, 2 * SUB, 2 * RIM), fast(planes // 2, LEVELS, SUB, half)],
        input_output_aliases={1: 1},
    )(halo, gauss, toned, place, weight, tables, rim, wide, small, full, narrow)
    theirs = lax.ppermute(mine, "lvl", swap)
    sems = [pltpu.SemaphoreType.DMA((tiles,))]
    begun = call(put_mine_kernel, "put_mine", [VMEM], f32(rows, width), sems, HBM)(mine)
    return call(
        put_theirs_kernel, "put_theirs", [VMEM, HBM], f32(rows, width), sems, HBM, input_output_aliases={1: 0}
    )(theirs, begun)


def solution(mesh):
    placed = (P("band", "tile"), P("lvl", None))
    return jax.shard_map(
        body, mesh=mesh, in_specs=placed, out_specs=P("band", "tile"), check_vma=False
    )
```

```python
import functools

import jax
import jax.numpy as jnp
from jax import lax
from jax.experimental import pallas as pl
from jax.experimental.pallas import tpu as pltpu
from jax.sharding import PartitionSpec as P

LEVELS = 16
KNOTS = 17
PYR = 6

SUB = 8
LANES = 128
RIM = 128
FIRST = 2
STACK = FIRST + LEVELS
FINE = (LEVELS - 1) * (KNOTS - 1) // 2
TABLES = 11

VMEM = pl.BlockSpec(memory_space=pltpu.VMEM)
HBM = pl.BlockSpec(memory_space=pltpu.HBM)
PARAMS = pltpu.CompilerParams(vmem_limit_bytes=20 * 1024 * 1024)


def iota(shape, dim):
    return lax.broadcasted_iota(jnp.int32, shape, dim)


def down_taps(distance):
    size = jnp.abs(distance)
    value = jnp.where(size == 0, 6.0, jnp.where(size == 1, 4.0, jnp.where(size == 2, 1.0, 0.0)))
    return (value / 256.0).astype(jnp.bfloat16)


def up_taps(distance):
    size = jnp.abs(distance)
    value = jnp.where(size == 0, 0.75, jnp.where(size == 1, 0.5, jnp.where(size == 2, 0.125, 0.0)))
    return (value / 2.0).astype(jnp.bfloat16)


def halves(x):
    high = x.astype(jnp.bfloat16)
    low = (x - high.astype(jnp.float32)).astype(jnp.bfloat16)
    return jnp.concatenate([high, low], axis=-1)


def dot(x, table):
    return jnp.dot(x, table, preferred_element_type=jnp.float32)


def shift_down(x):
    return pltpu.roll(x, 1, axis=x.ndim - 2)


def shift_up(x):
    return pltpu.roll(x, SUB - 1, axis=x.ndim - 2)


def sublane(x):
    return iota(x.shape, x.ndim - 2)


def rows_down(planes, scaled=False):
    first, last = planes[0], planes[-1]
    top = sublane(first) == 0
    quad = (lambda x: x) if scaled else (lambda x: 4.0 * x)
    minus2 = jnp.where(top, first, shift_down(planes[-2]))
    minus1 = jnp.where(top, 4.0 * first if scaled else first, shift_down(last))
    plus = jnp.where(sublane(first) == SUB - 1, 0.25 * last if scaled else last, shift_up(first))
    padded = [minus2, minus1] + list(planes) + [plus]
    out = []
    for at in range(0, len(planes), 2):
        a, b, c, d, e = padded[at:at + 5]
        out.append((a + e) + quad(b + d) + 6.0 * c)
    return out


def padded_for_up(planes):
    first, last = planes[0], planes[-1]
    below = jnp.where(sublane(first) == 0, first, shift_down(last))
    above = jnp.where(sublane(first) == SUB - 1, last, shift_up(first))
    return [below] + list(planes) + [above]


def rows_up(planes):
    padded = padded_for_up(planes)
    sums = [one + two for one, two in zip(padded[:-1], padded[1:])]
    out = []
    for at in range(len(planes)):
        out.append(0.25 * (sums[at] + sums[at + 1]) + planes[at])
        out.append(sums[at + 1])
    return out


def gather_along(dim):
    return lax.GatherDimensionNumbers(
        offset_dims=(),
        collapsed_slice_dims=(dim,),
        start_index_map=(dim,),
        operand_batching_dims=(1 - dim,),
        start_indices_batching_dims=(1 - dim,),
    )


def look_up(table, index, dim=0):
    return lax.gather(
        table, index[..., None], gather_along(dim), (1, 1), mode=lax.GatherScatterMode.PROMISE_IN_BOUNDS
    )


def cell(x, cells):
    scaled = x * float(cells)
    index = jnp.minimum(jnp.floor(scaled), float(cells - 1))
    return index.astype(jnp.int32), scaled - index


def by_lane(p):
    return p % 4 == 1


def curve_cell(p, x):
    return cell(x, FINE if by_lane(p) else (KNOTS - 1) // 2)


def curve_tables(curve_row, k):
    steps = (KNOTS - 1) // 2
    turn = steps * k // (LEVELS - 1)
    phase = (steps * k % (LEVELS - 1)) / (LEVELS - 1)
    width = curve_row.shape[-1]
    row = jnp.broadcast_to(curve_row, (SUB, width))
    offset = iota((SUB, width), 1) - iota((SUB, width), 0)

    def node(shift):
        at = jnp.where(offset == steps - turn + shift, row, 0.0)
        return jnp.sum(at, axis=1, keepdims=True)

    left, middle, right = node(-1), node(0), node(1)
    slope = middle - left
    bend = (right - middle) - slope
    start = (k / (LEVELS - 1) + middle) - phase * slope - phase * bend
    spread = lambda v: jnp.broadcast_to(v, (SUB, LANES))
    coarse = (spread(start), spread(slope), spread(bend))
    phase = jnp.full((SUB, LANES), phase, jnp.float32)

    lane = iota((SUB, LANES), 1)
    index = jnp.minimum(jnp.floor((lane.astype(jnp.float32) + 0.5) / (LEVELS - 1)), float(SUB - 1))
    index = index.astype(jnp.int32)
    within = (lane - (LEVELS - 1) * index).astype(jnp.float32)
    ends = [remap(coarse + (phase,), index, (within + side) / (LEVELS - 1)) for side in (0.0, 1.0)]
    fine = (ends[0], ends[1] - ends[0])
    return (phase,) + coarse + fine + tuple(4.0 * table for table in coarse + fine)


def remap(tables, index, rest):
    start, slope, bend, phase = tables
    bent = jnp.maximum(rest, phase)
    return look_up(start, index) + look_up(slope, index) * rest + look_up(bend, index) * bent


def remap_pair(table_ref, first, planes, index_of, rest_of):
    tables = [[table_ref[first + copy, kind] for kind in range(TABLES)] for copy in range(2)]
    mapped = [[], []]
    for p in range(planes):
        index, rest = index_of(p), rest_of(p)
        at = 6 if p % 2 else 1
        for copy in range(2):
            phase, (start, slope, bend, value, step) = tables[copy][0], tables[copy][at:at + 5]
            if by_lane(p):
                result = look_up(value, index, 1) + look_up(step, index, 1) * rest
            else:
                result = remap((start, slope, bend, phase), index, rest)
            mapped[copy].append(result)
    return mapped


def tone_tables(low, high):
    middle = (KNOTS - 1) // 2
    scale = middle / (LEVELS - 1)
    spread = lambda v: jnp.broadcast_to(v, (SUB, LANES))
    sub = iota((SUB, LANES), 0)

    def parts(curves, k):
        level = (sub + k).astype(jnp.float32) / (LEVELS - 1)
        left, centre, right = [spread(curves[:, at:at + 1]) for at in (middle - 1, middle, middle + 1)]
        return level + centre, scale * (right - centre), scale * (centre - left)

    def following(x, then):
        return jnp.where(sub == SUB - 1, spread(then[0:1, :]), shift_up(x))

    one, two = parts(low, 0), parts(high, LEVELS // 2)
    tables = []
    for here, then in ((one, two), (two, two)):
        base = here[0]
        tables.append((base, following(here[0], then[0]) - base, here[1] - following(here[2], then[2])))
    return tables


def tone(tables, x):
    index, rest = cell(x, LEVELS - 1)
    lower = index < SUB
    place = index & (SUB - 1)
    base, step, arc = [
        jnp.where(lower, look_up(one, place), look_up(two, place)) for one, two in zip(*tables)
    ]
    return base + rest * (step + (1.0 - rest) * arc)


def scaled_level(x):
    place = x * float(LEVELS - 1)
    half = 0.5 * place
    return place, jnp.abs(1.0 - 2.0 * (half - jnp.floor(half)))


def stage_kernel(image_ref, curves_ref, whole_ref, edge_ref, mine_ref, own_ref, rim_ref, wide_ref, small_ref, full_ref,
                 narrow_ref, sems):
    lvl = lax.axis_index("lvl")
    tiles = whole_ref.shape[0]
    start = pl.multiple_of(lvl * (tiles - 1) * LANES, LANES)
    copies = [
        pltpu.make_async_copy(image_ref.at[:, pl.ds(start, RIM)], edge_ref, sems.at[tiles]),
        pltpu.make_async_copy(curves_ref, mine_ref, sems.at[tiles + 1]),
    ]
    for tile in range(tiles):
        source = image_ref.at[:, tile * LANES:(tile + 1) * LANES]
        copies.append(pltpu.make_async_copy(source, whole_ref.at[tile], sems.at[tile]))
    for copy in copies:
        copy.start()

    half = tiles * LANES // 2

    def put(ref, shape, value):
        table = value(iota(shape, 0), iota(shape, 1))
        ref[0:shape[0], :] = table
        ref[shape[0]:2 * shape[0], :] = table

    inner = jnp.where(lvl == 1, half + RIM, 0)
    outer = jnp.where(lvl == 0, -RIM, half)
    put(own_ref, (half + RIM, half),
        lambda i, j: down_taps(jnp.where(i >= half, i - inner, i) - 2 * (j - RIM // 2)))
    put(rim_ref, (RIM, LANES), lambda i, j: down_taps(i + outer - 2 * (j + lvl * LANES - RIM // 2)))
    put(wide_ref, (half, LANES), lambda i, j: down_taps(i - 2 * j))
    put(small_ref, (LANES, LANES), lambda i, j: down_taps(i - 2 * j))
    put(full_ref, (half, half), lambda i, j: up_taps(2 * i - (j + RIM)))
    put(narrow_ref, (LANES, half), lambda i, j: up_taps(2 * i - j))
    for copy in copies:
        copy.wait()


def put_kernel(half_ref, out_ref, sems, lvl):
    tiles = half_ref.shape[0]
    copies = []
    for tile in range(tiles):
        start = pl.multiple_of((lvl * tiles + tile) * LANES, LANES)
        target = out_ref.at[:, pl.ds(start, LANES)]
        copies.append(pltpu.make_async_copy(half_ref.at[tile], target, sems.at[tile]))
    for copy in copies:
        copy.start()
    for copy in copies:
        copy.wait()


def put_mine_kernel(mine_ref, out_ref, sems):
    put_kernel(mine_ref, out_ref, sems, lax.axis_index("lvl"))


def put_theirs_kernel(theirs_ref, begun_ref, out_ref, sems):
    put_kernel(theirs_ref, out_ref, sems, 1 - lax.axis_index("lvl"))


def pick(place, weight, values):
    even, odd = values(0), values(1)
    for k in range(2, LEVELS, 2):
        even = jnp.where(place >= float(k - 1), values(k), even)
        odd = jnp.where(place >= float(k), values(k + 1), odd)
    return odd + weight * (even - odd)


def split_store(ref, reduced, column, width):
    for pair in range(len(reduced) // 2):
        both = jnp.concatenate(reduced[2 * pair:2 * pair + 2], axis=0)
        high = both.astype(jnp.bfloat16)
        low = (both - high.astype(jnp.float32)).astype(jnp.bfloat16)
        ref[pair, :, column:column + LANES] = high
        ref[pair, :, width + column:width + column + LANES] = low


def scale_odd(planes):
    return [4.0 * x if p % 2 else x for p, x in enumerate(planes)]


def own_kernel(image_ref, mine_ref, other_ref, down_ref, gauss_ref, tone_ref, place_ref, weight_ref,
               table_ref, x_scr, cell_scr, rest_scr, part_scr):
    lvl = lax.axis_index("lvl")
    tiles, rows, _ = image_ref.shape
    planes = rows // SUB
    half = tiles * LANES // 2
    own = half + RIM
    pairs = LEVELS // 2

    first = jnp.where(lvl == 0, mine_ref[...], other_ref[...])
    second = jnp.where(lvl == 0, other_ref[...], mine_ref[...])
    for k in range(LEVELS):
        source = first if k < pairs else second
        row = k % pairs
        for kind, table in enumerate(curve_tables(source[row:row + 1, :], k)):
            table_ref[k, kind] = table
    tones = tone_tables(first, second)

    sources = [lvl * (tiles // 2) + tile for tile in range(tiles // 2)] + [tiles // 2 - lvl]
    for tile, source in enumerate(sources):
        span = slice(tile * LANES, (tile + 1) * LANES)
        for p in range(planes):
            x = image_ref[source, pl.ds(p, SUB, stride=planes), :]
            x_scr[p, :, span] = x
            cell_scr[p, :, span], rest_scr[p, :, span] = curve_cell(p, x)
            if tile < tiles // 2:
                tone_ref[p, :, span] = tone(tones, x)
                place_ref[p, :, span], weight_ref[p, :, span] = scaled_level(x)

    def multiply(slot, target):
        part = part_scr[slot].reshape(-1, 2 * own)
        result = dot(part, down_ref[...]).reshape(2, planes // 4, 2, SUB, half)
        for copy in range(2):
            for tile in range(half // LANES):
                span = slice(tile * LANES, (tile + 1) * LANES)
                gauss_ref[tile, :, target + copy] = result[copy, :, :, :, span]

    for column in range(0, own, LANES):
        guide = scale_odd([x_scr[p, :, column:column + LANES] for p in range(planes)])
        reduced = rows_down(guide, scaled=True)
        for copy in range(2):
            split_store(part_scr.at[1, copy], reduced, column, own)

    def one_pair(step, carry):
        slot = lax.rem(step, 2)
        multiply(1 - slot, 2 * step)
        for column in range(0, own, LANES):
            span = slice(column, column + LANES)
            mapped = remap_pair(
                table_ref, 2 * step, planes, lambda p: cell_scr[p, :, span], lambda p: rest_scr[p, :, span]
            )
            for copy in range(2):
                split_store(part_scr.at[slot, copy], rows_down(mapped[copy], scaled=True), column, own)
        return carry

    lax.fori_loop(0, pairs, one_pair, 0, unroll=pairs)
    multiply((pairs - 1) % 2, 2 * pairs)


def rest_kernel(halo_ref, gauss_in_ref, tone_ref, place_ref, weight_ref, table_ref, rim_ref, wide_ref,
                small_ref, full_ref, narrow_ref, out_ref, gauss_ref, x_scr, cell_scr, rest_scr, part_scr,
                up_scr):
    lvl = lax.axis_index("lvl")
    rows = halo_ref.shape[0]
    planes = rows // SUB
    tiles = out_ref.shape[0]
    half = tiles * LANES
    pairs = LEVELS // 2

    for p in range(planes):
        x = halo_ref[pl.ds(p, SUB, stride=planes), :]
        x_scr[p] = x
        cell_scr[p], rest_scr[p] = curve_cell(p, x)

    def multiply(slot, target):
        part = part_scr[slot].reshape(-1, 2 * RIM)
        result = dot(part, rim_ref[...]).reshape(2, planes // 4, 2, SUB, LANES)
        for copy in range(2):
            gauss_ref[lvl, :, target + copy] = gauss_in_ref[lvl, :, target + copy] + result[copy]

    reduced = rows_down(scale_odd([x_scr[p] for p in range(planes)]), scaled=True)
    for copy in range(2):
        split_store(part_scr.at[1, copy], reduced, 0, RIM)

    def one_pair(step, carry):
        slot = lax.rem(step, 2)
        multiply(1 - slot, 2 * step)
        mapped = remap_pair(table_ref, 2 * step, planes, lambda p: cell_scr[p], lambda p: rest_scr[p])
        for copy in range(2):
            split_store(part_scr.at[slot, copy], rows_down(mapped[copy], scaled=True), 0, RIM)
        return carry

    lax.fori_loop(0, pairs, one_pair, 0, unroll=pairs)
    multiply((pairs - 1) % 2, 2 * pairs)

    def level_one(p, start=0):
        parts = [gauss_ref[tile, p // 2, start:, p % 2] for tile in range(tiles)]
        return jnp.concatenate(parts, axis=-1)

    source = jnp.concatenate([level_one(p, FIRST) for p in range(planes // 2)], axis=0)
    up_scr[...] = dot(halves(source.reshape(-1, half)), full_ref[...]).reshape(up_scr.shape)

    gauss = [None, [level_one(p) for p in range(planes // 2)]]
    for level in range(1, PYR - 1):
        reduced = rows_down(gauss[level])
        count = len(reduced)
        stacked = jnp.concatenate(reduced, axis=0)
        stacked = stacked.reshape(-1, stacked.shape[-1])
        result = dot(halves(stacked), (wide_ref if level == 1 else small_ref)[...])
        result = result.reshape(count, STACK, SUB, LANES)
        gauss.append([result[p] for p in range(count)])

    out = [gauss[PYR - 1][0][0]]
    for level in range(PYR - 2, 0, -1):
        columns = half if level == 1 else LANES
        table = narrow_ref[:, 0:columns]
        coarse = gauss[level + 1]
        count = len(coarse)
        stacked = jnp.concatenate([plane[FIRST:] for plane in coarse], axis=0).reshape(-1, LANES)
        wider = dot(halves(stacked), table).reshape(count, LEVELS, SUB, columns)
        raised = rows_up([wider[p] for p in range(count)])
        base = dot(halves(jnp.concatenate(out, axis=0)), table).reshape(count, SUB, columns)
        base = rows_up([base[p] for p in range(count)])
        out = []
        for p in range(2 * count):
            here = gauss[level][p]
            place, weight = scaled_level(here[0])
            out.append(pick(place, weight, lambda k: here[FIRST + k] - raised[p][k]) + base[p])

    base = dot(halves(jnp.concatenate(out, axis=0)), full_ref[...]).reshape(planes // 2, SUB, half)
    base = rows_up([base[p] for p in range(planes // 2)])
    rows = [up_scr[p] for p in range(planes // 2)]
    padded = padded_for_up(rows)
    sums = [one + two for one, two in zip(padded[:-1], padded[1:])]
    for p in range(planes):
        above, below, here = sums[p // 2], sums[p // 2 + 1], rows[p // 2]
        if p % 2 == 0:
            detail = pick(place_ref[p], weight_ref[p], lambda k: 0.25 * (above[k] + below[k]) + here[k])
        else:
            detail = pick(place_ref[p], weight_ref[p], lambda k: below[k])
        toned = (tone_ref[p] - detail) + base[p]
        for tile in range(tiles):
            out_ref[tile, pl.ds(p, SUB, stride=planes), :] = toned[:, tile * LANES:(tile + 1) * LANES]


def call(kernel, name, in_specs, out_shape, scratch, out_space=VMEM, **others):
    return pl.pallas_call(
        kernel,
        name=name,
        in_specs=in_specs,
        out_specs=jax.tree.map(lambda _: out_space, out_shape),
        out_shape=out_shape,
        scratch_shapes=scratch,
        compiler_params=PARAMS,
        **others,
    )


def body(image, curves):
    rows, width = image.shape
    half = width // 2
    own = half + RIM
    planes = rows // SUB
    tiles = half // LANES
    lvl = lax.axis_index("lvl")
    count = lax.axis_size("tile")
    f32 = lambda *shape: jax.ShapeDtypeStruct(shape, jnp.float32)
    b16 = lambda *shape: jax.ShapeDtypeStruct(shape, jnp.bfloat16)
    fast = lambda *shape: pltpu.VMEM(shape, jnp.float32)
    fast_int = lambda *shape: pltpu.VMEM(shape, jnp.int32)
    fast_half = lambda *shape: pltpu.VMEM(shape, jnp.bfloat16)
    swap = [(0, 1), (1, 0)]

    other_curves = lax.ppermute(curves, "lvl", swap)
    whole, edge, mine, down, rim, wide, small, full, narrow = call(
        stage_kernel, "stage", [HBM] * 2,
        [f32(2 * tiles, rows, LANES), f32(rows, RIM), f32(*curves.shape), b16(2 * own, half), b16(2 * RIM, LANES),
         b16(2 * half, LANES), b16(2 * LANES, LANES), b16(2 * half, half), b16(2 * LANES, half)],
        [pltpu.SemaphoreType.DMA((2 * tiles + 2,))],
    )(pltpu.with_memory_space_constraint(image, pltpu.HBM), pltpu.with_memory_space_constraint(curves, pltpu.HBM))
    edge, other_curves = lax.optimization_barrier((edge, other_curves))
    pairs = []
    for tile in range(count):
        pairs.append((2 * tile + 1, 2 * ((tile + 1) % count)))
        pairs.append((2 * tile, 2 * ((tile - 1) % count) + 1))
    halo = lax.ppermute(edge, ("tile", "lvl"), pairs)

    gauss_shape = f32(tiles, planes // 4, STACK, 2, SUB, LANES)
    gauss, toned, place, weight, tables = call(
        own_kernel, "own", [VMEM] * 4,
        [gauss_shape, f32(planes, SUB, half), f32(planes, SUB, half), f32(planes, SUB, half),
         f32(LEVELS, TABLES, SUB, LANES)],
        [fast(planes, SUB, own), fast_int(planes, SUB, own), fast(planes, SUB, own),
         fast_half(2, 2, planes // 4, 2 * SUB, 2 * own)],
    )(whole, mine, other_curves, down)
    mine, _ = call(
        rest_kernel, "rest", [VMEM] * 11, [f32(tiles, rows, LANES), gauss_shape],
        [fast(planes, SUB, RIM), fast_int(planes, SUB, RIM), fast(planes, SUB, RIM),
         fast_half(2, 2, planes // 4, 2 * SUB, 2 * RIM), fast(planes // 2, LEVELS, SUB, half)],
        input_output_aliases={1: 1},
    )(halo, gauss, toned, place, weight, tables, rim, wide, small, full, narrow)
    theirs = lax.ppermute(mine, "lvl", swap)
    sems = [pltpu.SemaphoreType.DMA((tiles,))]
    begun = call(put_mine_kernel, "put_mine", [VMEM], f32(rows, width), sems, HBM)(mine)
    return call(
        put_theirs_kernel, "put_theirs", [VMEM, HBM], f32(rows, width), sems, HBM, input_output_aliases={1: 0}
    )(theirs, begun)


def solution(mesh):
    placed = (P("band", "tile"), P("lvl", None))
    return jax.shard_map(
        body, mesh=mesh, in_specs=placed, out_specs=P("band", "tile"), check_vma=False
    )
```

```python
import functools

import jax
import jax.numpy as jnp
from jax import lax
from jax.experimental import pallas as pl
from jax.experimental.pallas import tpu as pltpu
from jax.sharding import PartitionSpec as P

LEVELS = 16
KNOTS = 17
PYR = 6

SUB = 8
LANES = 128
RIM = LANES
FIRST = 2
STACK = FIRST + LEVELS
LEFT, RIGHT = 2, 126
FINE = (LEVELS - 1) * (KNOTS - 1) // 2
TABLES = 11

VMEM = pl.BlockSpec(memory_space=pltpu.VMEM)
HBM = pl.BlockSpec(memory_space=pltpu.HBM)
PARAMS = pltpu.CompilerParams(vmem_limit_bytes=20 * 1024 * 1024)


def iota(shape, dim):
    return lax.broadcasted_iota(jnp.int32, shape, dim)


def down_taps(distance):
    size = jnp.abs(distance)
    value = jnp.where(size == 0, 6.0, jnp.where(size == 1, 4.0, jnp.where(size == 2, 1.0, 0.0)))
    return (value / 256.0).astype(jnp.bfloat16)


def up_taps(distance):
    size = jnp.abs(distance)
    value = jnp.where(size == 0, 0.75, jnp.where(size == 1, 0.5, jnp.where(size == 2, 0.125, 0.0)))
    return (value / 2.0).astype(jnp.bfloat16)


def halves(x):
    high = x.astype(jnp.bfloat16)
    low = (x - high.astype(jnp.float32)).astype(jnp.bfloat16)
    return jnp.concatenate([high, low], axis=-1)


def dot(x, table):
    return jnp.dot(x, table, preferred_element_type=jnp.float32)


def shift_down(x):
    return pltpu.roll(x, 1, axis=x.ndim - 2)


def shift_up(x):
    return pltpu.roll(x, SUB - 1, axis=x.ndim - 2)


def sublane(x):
    return iota(x.shape, x.ndim - 2)


def rows_down(planes, scaled=False):
    first, last = planes[0], planes[-1]
    top = sublane(first) == 0
    quad = (lambda x: x) if scaled else (lambda x: 4.0 * x)
    minus2 = jnp.where(top, first, shift_down(planes[-2]))
    minus1 = jnp.where(top, 4.0 * first if scaled else first, shift_down(last))
    plus = jnp.where(sublane(first) == SUB - 1, 0.25 * last if scaled else last, shift_up(first))
    padded = [minus2, minus1] + list(planes) + [plus]
    out = []
    for at in range(0, len(planes), 2):
        a, b, c, d, e = padded[at:at + 5]
        out.append((a + e) + quad(b + d) + 6.0 * c)
    return out


def padded_for_up(planes):
    first, last = planes[0], planes[-1]
    below = jnp.where(sublane(first) == 0, first, shift_down(last))
    above = jnp.where(sublane(first) == SUB - 1, last, shift_up(first))
    return [below] + list(planes) + [above]


def rows_up(planes):
    padded = padded_for_up(planes)
    sums = [one + two for one, two in zip(padded[:-1], padded[1:])]
    out = []
    for at in range(len(planes)):
        out.append(0.25 * (sums[at] + sums[at + 1]) + planes[at])
        out.append(sums[at + 1])
    return out


def gather_along(dim):
    return lax.GatherDimensionNumbers(
        offset_dims=(),
        collapsed_slice_dims=(dim,),
        start_index_map=(dim,),
        operand_batching_dims=(1 - dim,),
        start_indices_batching_dims=(1 - dim,),
    )


def look_up(table, index, dim=0):
    return lax.gather(
        table, index[..., None], gather_along(dim), (1, 1), mode=lax.GatherScatterMode.PROMISE_IN_BOUNDS
    )


def cell(x, cells):
    scaled = x * float(cells)
    index = jnp.minimum(jnp.floor(scaled), float(cells - 1))
    return index.astype(jnp.int32), scaled - index


def by_lane(p):
    return p % 4 == 1


def curve_cell(p, x):
    return cell(x, FINE if by_lane(p) else (KNOTS - 1) // 2)


def curve_tables(curve_row, k):
    steps = (KNOTS - 1) // 2
    turn = steps * k // (LEVELS - 1)
    phase = (steps * k % (LEVELS - 1)) / (LEVELS - 1)
    width = curve_row.shape[-1]
    row = jnp.broadcast_to(curve_row, (SUB, width))
    offset = iota((SUB, width), 1) - iota((SUB, width), 0)

    def node(shift):
        at = jnp.where(offset == steps - turn + shift, row, 0.0)
        return jnp.sum(at, axis=1, keepdims=True)

    left, middle, right = node(-1), node(0), node(1)
    slope = middle - left
    bend = (right - middle) - slope
    start = (k / (LEVELS - 1) + middle) - phase * slope - phase * bend
    spread = lambda v: jnp.broadcast_to(v, (SUB, LANES))
    coarse = (spread(start), spread(slope), spread(bend))
    phase = jnp.full((SUB, LANES), phase, jnp.float32)

    lane = iota((SUB, LANES), 1)
    index = jnp.minimum(jnp.floor((lane.astype(jnp.float32) + 0.5) / (LEVELS - 1)), float(SUB - 1))
    index = index.astype(jnp.int32)
    within = (lane - (LEVELS - 1) * index).astype(jnp.float32)
    ends = [remap(coarse + (phase,), index, (within + side) / (LEVELS - 1)) for side in (0.0, 1.0)]
    fine = (ends[0], ends[1] - ends[0])
    return (phase,) + coarse + fine + tuple(4.0 * table for table in coarse + fine)


def remap(tables, index, rest):
    start, slope, bend, phase = tables
    bent = jnp.maximum(rest, phase)
    return look_up(start, index) + look_up(slope, index) * rest + look_up(bend, index) * bent


def remap_pair(table_ref, first, planes, index_of, rest_of):
    tables = [[table_ref[first + copy, kind] for kind in range(TABLES)] for copy in range(2)]
    mapped = [[], []]
    for p in range(planes):
        index, rest = index_of(p), rest_of(p)
        at = 6 if p % 2 else 1
        for copy in range(2):
            phase, (start, slope, bend, value, step) = tables[copy][0], tables[copy][at:at + 5]
            if by_lane(p):
                result = look_up(value, index, 1) + look_up(step, index, 1) * rest
            else:
                result = remap((start, slope, bend, phase), index, rest)
            mapped[copy].append(result)
    return mapped


def tone_tables(low, high):
    middle = (KNOTS - 1) // 2
    scale = middle / (LEVELS - 1)
    spread = lambda v: jnp.broadcast_to(v, (SUB, LANES))
    sub = iota((SUB, LANES), 0)

    def parts(curves, k):
        level = (sub + k).astype(jnp.float32) / (LEVELS - 1)
        left, centre, right = [spread(curves[:, at:at + 1]) for at in (middle - 1, middle, middle + 1)]
        return level + centre, scale * (right - centre), scale * (centre - left)

    def following(x, then):
        return jnp.where(sub == SUB - 1, spread(then[0:1, :]), shift_up(x))

    one, two = parts(low, 0), parts(high, LEVELS // 2)
    lane = iota((SUB, LANES), 1)
    tables = []
    for kind in range(3):
        rows = []
        for here, then in ((one, two), (two, two)):
            if kind == 0:
                rows.append(here[0])
            elif kind == 1:
                rows.append(following(here[0], then[0]) - here[0])
            else:
                rows.append(here[1] - following(here[2], then[2]))
        along = jnp.where(lane == sub, rows[0], jnp.where(lane == sub + SUB, rows[1], 0.0))
        tables.append(spread(jnp.sum(along, axis=0, keepdims=True)))
    return tables


def tone(tables, x):
    index, rest = cell(x, LEVELS - 1)
    base, step, arc = [look_up(table, index, 1) for table in tables]
    return base + rest * (step + (1.0 - rest) * arc)


def scaled_level(x):
    place = x * float(LEVELS - 1)
    half = 0.5 * place
    return place, jnp.abs(1.0 - 2.0 * (half - jnp.floor(half)))


def start_all(pairs, sems):
    copies = [pltpu.make_async_copy(one, two, sems.at[at]) for at, (one, two) in enumerate(pairs)]
    for copy in copies:
        copy.start()
    return copies


def wait_all(copies):
    for copy in copies:
        copy.wait()


def near_column(lvl, lane):
    return lane + jnp.where(lvl == 0, LEFT, RIGHT)


def away_column(lvl, lane):
    return lane + jnp.where(lvl == 0, RIGHT, LEFT)


def level_one_column(lvl, at):
    return jnp.where(at < LANES, near_column(lvl, at), away_column(lvl, at - LANES))


def stage_kernel(image_ref, curves_ref, edge_ref, inner_ref, mine_ref, own_ref, rim_ref, wide_ref,
                 small_ref, near_ref, away_ref, narrow_ref, raise_ref, sems):
    lvl = lax.axis_index("lvl")
    planes = edge_ref.shape[0]
    half = 2 * LANES
    outermost = pl.multiple_of(lvl * 3 * LANES, LANES)
    pairs = [(curves_ref, mine_ref)]
    for q in range(SUB):
        rows = pl.ds(q * planes, planes)
        pairs.append((image_ref.at[rows, pl.ds(outermost, LANES)], edge_ref.at[:, q, :]))
        for tile in range(2):
            source = image_ref.at[rows, (tile + 1) * LANES:(tile + 2) * LANES]
            pairs.append((source, inner_ref.at[tile, :, q, :]))
    copies = start_all(pairs, sems)

    def put(ref, shape, value):
        table = value(iota(shape, 0), iota(shape, 1))
        ref[0:shape[0], :] = table
        ref[shape[0]:2 * shape[0], :] = table

    def place(i):
        tile = i // LANES
        return jnp.where(lvl == 0, i, i - 2 * tile * LANES + LANES)

    def rim_place(i):
        return i + jnp.where(lvl == 0, -RIM, half)

    def out_place(far, j):
        return j + jnp.where(lvl == far, 0, LANES)

    def wide(i, j):
        column = level_one_column(lvl, i)
        left = (i < LANES) == (lvl == 0)
        return jnp.where(left == (j < LANES // 2), down_taps(column - 2 * j), 0.0)

    def up_pair(column, far):
        def value(i, j):
            lane = j & (LANES - 1)
            taps = up_taps(2 * column(lvl, i) - (out_place(far, lane) + RIM))
            return jnp.where(j < LANES, taps, 0.25 * taps)
        return value

    put(own_ref, (3 * LANES, half),
        lambda i, j: down_taps(place(i) - 2 * (level_one_column(lvl, j) - RIM // 2)))
    put(rim_ref, (RIM, LANES), lambda i, j: down_taps(rim_place(i) - 2 * (near_column(lvl, j) - RIM // 2)))
    put(wide_ref, (half, LANES), wide)
    put(small_ref, (LANES, LANES), lambda i, j: down_taps(i - 2 * j))
    put(near_ref, (LANES, half), up_pair(near_column, 0))
    put(away_ref, (LANES, half), up_pair(away_column, 1))
    put(narrow_ref, (LANES, half), lambda i, j: up_taps(2 * i - level_one_column(lvl, j)))
    put(raise_ref, (LANES, LANES), lambda i, j: up_taps(2 * i - j))
    wait_all(copies)


def put_kernel(half_ref, out_ref, sems, lvl):
    planes = half_ref.shape[1]
    pairs = []
    for tile, at in enumerate((3 * lvl, 1 + lvl)):
        columns = pl.ds(pl.multiple_of(at * LANES, LANES), LANES)
        for q in range(SUB):
            pairs.append((half_ref.at[tile, :, q, :], out_ref.at[pl.ds(q * planes, planes), columns]))
    wait_all(start_all(pairs, sems))


def put_mine_kernel(mine_ref, out_ref, sems):
    put_kernel(mine_ref, out_ref, sems, lax.axis_index("lvl"))


def put_theirs_kernel(theirs_ref, begun_ref, out_ref, sems):
    put_kernel(theirs_ref, out_ref, sems, 1 - lax.axis_index("lvl"))


def pick(place, weight, values):
    even, odd = values(0), values(1)
    for k in range(2, LEVELS, 2):
        even = jnp.where(place >= float(k - 1), values(k), even)
        odd = jnp.where(place >= float(k), values(k + 1), odd)
    return odd + weight * (even - odd)


def split_store(ref, reduced, column, width):
    for pair in range(len(reduced) // 2):
        both = jnp.concatenate(reduced[2 * pair:2 * pair + 2], axis=0)
        high = both.astype(jnp.bfloat16)
        low = (both - high.astype(jnp.float32)).astype(jnp.bfloat16)
        ref[pair, :, column:column + LANES] = high
        ref[pair, :, width + column:width + column + LANES] = low


def scale_odd(planes):
    return [4.0 * x if p % 2 else x for p, x in enumerate(planes)]


def own_kernel(edge_ref, inner_ref, mine_ref, other_ref, down_ref, gauss_ref, last_ref, tone_ref, place_ref,
               weight_ref, table_ref, cell_scr, rest_scr, part_scr):
    lvl = lax.axis_index("lvl")
    planes = edge_ref.shape[0]
    own = 3 * LANES
    half = 2 * LANES
    pairs = LEVELS // 2

    first = jnp.where(lvl == 0, mine_ref[...], other_ref[...])
    second = jnp.where(lvl == 0, other_ref[...], mine_ref[...])
    for k in range(LEVELS):
        source = first if k < pairs else second
        row = k % pairs
        for kind, table in enumerate(curve_tables(source[row:row + 1, :], k)):
            table_ref[k, kind] = table
    tones = tone_tables(first, second)

    def image(tile, p):
        return edge_ref[p] if tile == 0 else inner_ref[lvl if tile == 1 else 1 - lvl, p]

    for tile in range(3):
        for p in range(planes):
            x = image(tile, p)
            cell_scr[tile, p], rest_scr[tile, p] = curve_cell(p, x)
            if tile < 2:
                tone_ref[tile, p] = tone(tones, x)
                place_ref[tile, p], weight_ref[tile, p] = scaled_level(x)

    def multiply(slot, target):
        part = part_scr[slot].reshape(-1, 2 * own)
        result = dot(part, down_ref[...]).reshape(2, planes // 4, 2, SUB, half)
        for copy in range(2):
            for tile in range(2):
                span = slice(tile * LANES, (tile + 1) * LANES)
                gauss_ref[tile, :, target + copy] = result[copy, :, :, :, span]

    for tile in range(3):
        reduced = rows_down(scale_odd([image(tile, p) for p in range(planes)]), scaled=True)
        for copy in range(2):
            split_store(part_scr.at[1, copy], reduced, tile * LANES, own)

    for step in range(pairs):
        slot = step % 2
        multiply(1 - slot, 2 * step)
        ref = last_ref if step == pairs - 1 else part_scr.at[slot]
        for tile in range(3):
            mapped = remap_pair(
                table_ref, 2 * step, planes, lambda p: cell_scr[tile, p], lambda p: rest_scr[tile, p]
            )
            for copy in range(2):
                split_store(ref.at[copy], rows_down(mapped[copy], scaled=True), tile * LANES, own)


def rest_kernel(halo_ref, gauss_in_ref, last_ref, tone_ref, place_ref, weight_ref, table_ref, down_ref,
                rim_ref, wide_ref, small_ref, near_ref, away_ref, narrow_ref, raise_ref, out_ref, gauss_ref,
                cell_scr, rest_scr, part_scr, up_scr):
    planes = halo_ref.shape[0]
    half = 2 * LANES
    pairs = LEVELS // 2

    result = dot(last_ref[...].reshape(-1, 6 * LANES), down_ref[...]).reshape(2, planes // 4, 2, SUB, half)
    for copy in range(2):
        gauss_ref[0, :, LEVELS + copy] = result[copy, :, :, :, 0:LANES]
        gauss_ref[1, :, LEVELS + copy] = result[copy, :, :, :, LANES:half]

    def columns_up(tile):
        source = jnp.concatenate([gauss_ref[tile, p // 2, FIRST:, p % 2] for p in range(planes // 2)], axis=0)
        result = dot(halves(source.reshape(-1, LANES)), tables_up[tile][...])
        up_scr[tile] = result.reshape(planes // 2, LEVELS, SUB, half)

    tables_up = (near_ref, away_ref)
    for p in range(planes):
        cell_scr[p], rest_scr[p] = curve_cell(p, halo_ref[p])

    def multiply(slot, target):
        part = part_scr[slot].reshape(-1, 2 * RIM)
        result = dot(part, rim_ref[...]).reshape(2, planes // 4, 2, SUB, LANES)
        before = gauss_ref if target == LEVELS else gauss_in_ref
        for copy in range(2):
            gauss_ref[0, :, target + copy] = before[0, :, target + copy] + result[copy]

    reduced = rows_down(scale_odd([halo_ref[p] for p in range(planes)]), scaled=True)
    for copy in range(2):
        split_store(part_scr.at[1, copy], reduced, 0, RIM)
    for step in range(pairs):
        slot = step % 2
        multiply(1 - slot, 2 * step)
        mapped = remap_pair(table_ref, 2 * step, planes, lambda p: cell_scr[p], lambda p: rest_scr[p])
        for copy in range(2):
            split_store(part_scr.at[slot, copy], rows_down(mapped[copy], scaled=True), 0, RIM)
    multiply((pairs - 1) % 2, 2 * pairs)

    sums = {}

    def quarter_sum(tile, at):
        if (tile, at) not in sums:
            count = planes // 2
            edge = lambda p: up_scr[tile, p, :, :, LANES:half]
            if at == 0:
                before = jnp.where(sublane(edge(0)) == 0, edge(0), shift_down(edge(count - 1)))
            else:
                before = edge(at - 1)
            if at == count:
                after = jnp.where(sublane(edge(0)) == SUB - 1, edge(count - 1), shift_up(edge(0)))
            else:
                after = edge(at)
            sums[tile, at] = before + after
        return sums[tile, at]

    def level_zero(tile, p):
        above, below = quarter_sum(tile, p // 2), quarter_sum(tile, p // 2 + 1)
        at = (place_ref[tile, p], weight_ref[tile, p])
        if p % 2 == 0:
            detail = pick(*at, lambda k: (above[k] + below[k]) + up_scr[tile, p // 2, k, :, 0:LANES])
        else:
            detail = 4.0 * pick(*at, lambda k: below[k])
        out_ref[tile, p] = tone_ref[tile, p] - detail

    waiting = [(tile, p) for tile in (1, 0) for p in range(planes)]

    def meanwhile(count):
        for _ in range(min(count, len(waiting))):
            level_zero(*waiting.pop(0))

    def level_one(p):
        return jnp.concatenate([gauss_ref[tile, p // 2, :, p % 2] for tile in range(2)], axis=-1)

    def next_level(coarse, table):
        reduced = rows_down(coarse)
        stacked = jnp.concatenate(reduced, axis=0)
        result = dot(halves(stacked.reshape(-1, stacked.shape[-1])), table)
        result = result.reshape(len(reduced), STACK, SUB, LANES)
        return [result[p] for p in range(len(reduced))]

    def raise_columns(stacks, table):
        stacked = jnp.concatenate(stacks, axis=0)
        result = dot(halves(stacked.reshape(-1, LANES)), table)
        return result.reshape((len(stacks), -1, SUB, table.shape[1]))

    def raise_stack(coarse, table):
        result = raise_columns([plane[FIRST:] for plane in coarse], table)
        return rows_up([result[p] for p in range(len(coarse))])

    def raise_one(planes_of, table):
        result = raise_columns([plane[None] for plane in planes_of], table)
        return rows_up([result[p, 0] for p in range(len(planes_of))])

    def coefficient(level, raised, p):
        here = gauss[level][p]
        return pick(*scaled_level(here[0]), lambda k: here[FIRST + k] - raised[p][k])

    lift = raise_ref[...]
    gauss = [None, [level_one(p) for p in range(planes // 2)]]
    gauss.append(next_level(gauss[1], wide_ref[...]))
    raised = [None, raise_stack(gauss[2], narrow_ref[...])]
    columns_up(1)
    columns_up(0)
    coeffs = [None, []]
    quarter = planes // 8
    for level in range(2, PYR - 1):
        gauss.append(next_level(gauss[level], small_ref[...]))
        coeffs[1] += [coefficient(1, raised[1], p) for p in range(quarter * (level - 2), quarter * (level - 1))]
        raised.append(raise_stack(gauss[level + 1], lift))
    base = raise_one([gauss[PYR - 1][0][0]], lift)
    coeffs[1] += [coefficient(1, raised[1], p) for p in range(3 * quarter, planes // 2)]
    for level in range(2, PYR - 1):
        coeffs.append([coefficient(level, raised[level], p) for p in range(len(gauss[level]))])
    for level in range(PYR - 2, 0, -1):
        out = [one + two for one, two in zip(coeffs[level], base)]
        if level > 1:
            base = raise_one(out, narrow_ref[...] if level == 2 else lift)
        else:
            base = []
            for tile in range(2):
                span = slice(tile * LANES, (tile + 1) * LANES)
                base.append(raise_one([plane[:, span] for plane in out], tables_up[tile][:, 0:LANES]))
        meanwhile(planes // 2)
    meanwhile(2 * planes)
    for tile in range(2):
        for p in range(planes):
            out_ref[tile, p] = out_ref[tile, p] + base[tile][p]


def call(kernel, name, in_specs, out_shape, scratch, out_space=VMEM, **others):
    return pl.pallas_call(
        kernel,
        name=name,
        in_specs=in_specs,
        out_specs=jax.tree.map(lambda _: out_space, out_shape),
        out_shape=out_shape,
        scratch_shapes=scratch,
        compiler_params=PARAMS,
        **others,
    )


def body(image, curves):
    rows, width = image.shape
    planes = rows // SUB
    half = width // 2
    count = lax.axis_size("tile")
    f32 = lambda *shape: jax.ShapeDtypeStruct(shape, jnp.float32)
    b16 = lambda *shape: jax.ShapeDtypeStruct(shape, jnp.bfloat16)
    fast = lambda *shape: pltpu.VMEM(shape, jnp.float32)
    fast_int = lambda *shape: pltpu.VMEM(shape, jnp.int32)
    fast_half = lambda *shape: pltpu.VMEM(shape, jnp.bfloat16)
    in_hbm = lambda x: pltpu.with_memory_space_constraint(x, pltpu.HBM)
    swap = [(0, 1), (1, 0)]

    other_curves = lax.ppermute(curves, "lvl", swap)
    edge, inner, mine, down, rim, wide, small, near, away, narrow, lift = call(
        stage_kernel, "stage", [HBM] * 2,
        [f32(planes, SUB, LANES), f32(2, planes, SUB, LANES), f32(*curves.shape), b16(6 * LANES, half),
         b16(2 * RIM, LANES), b16(2 * half, LANES), b16(2 * LANES, LANES), b16(2 * LANES, half),
         b16(2 * LANES, half), b16(2 * LANES, half), b16(2 * LANES, LANES)],
        [pltpu.SemaphoreType.DMA((3 * SUB + 1,))],
    )(in_hbm(image), in_hbm(curves))
    sent, other_curves = lax.optimization_barrier((edge, other_curves))
    pairs = []
    for tile in range(count):
        pairs.append((2 * tile + 1, 2 * ((tile + 1) % count)))
        pairs.append((2 * tile, 2 * ((tile - 1) % count) + 1))
    halo = lax.ppermute(sent, ("tile", "lvl"), pairs)

    gauss_shape = f32(2, planes // 4, STACK, 2, SUB, LANES)
    out_shape = f32(2, planes, SUB, LANES)
    last_shape = b16(2, planes // 4, 2 * SUB, 6 * LANES)
    gauss, last, toned, place, weight, tables = call(
        own_kernel, "own", [VMEM] * 5,
        [gauss_shape, last_shape, out_shape, out_shape, out_shape, f32(LEVELS, TABLES, SUB, LANES)],
        [fast_int(3, planes, SUB, LANES), fast(3, planes, SUB, LANES), fast_half(2, *last_shape.shape)],
    )(sent, inner, mine, other_curves, down)
    mine, _ = call(
        rest_kernel, "rest", [VMEM] * 15, [out_shape, gauss_shape],
        [fast_int(planes, SUB, RIM), fast(planes, SUB, RIM),
         fast_half(2, 2, planes // 4, 2 * SUB, 2 * RIM), fast(2, planes // 2, LEVELS, SUB, half)],
        input_output_aliases={1: 1},
    )(halo, gauss, last, toned, place, weight, tables, down, rim, wide, small, near, away, narrow, lift)
    theirs = lax.ppermute(mine, "lvl", swap)
    sems = [pltpu.SemaphoreType.DMA((2 * SUB,))]
    begun = call(put_mine_kernel, "put_mine", [VMEM], f32(rows, width), sems, HBM)(mine)
    return call(
        put_theirs_kernel, "put_theirs", [VMEM, HBM], f32(rows, width), sems, HBM, input_output_aliases={1: 0}
    )(theirs, begun)


def solution(mesh):
    placed = (P("band", "tile"), P("lvl", None))
    return jax.shard_map(
        body, mesh=mesh, in_specs=placed, out_specs=P("band", "tile"), check_vma=False
    )
```

```python
import functools

import jax
import jax.numpy as jnp
from jax import lax
from jax.experimental import pallas as pl
from jax.experimental.pallas import tpu as pltpu
from jax.sharding import PartitionSpec as P

LEVELS = 16
KNOTS = 17
PYR = 6

SUB = 8
LANES = 128
PIECE = LANES // 4
RIM = LANES
FIRST = 2
STACK = FIRST + LEVELS
LEFT, RIGHT = 2, 126
FINE = (LEVELS - 1) * (KNOTS - 1) // 2
TABLES = 11

VMEM = pl.BlockSpec(memory_space=pltpu.VMEM)
HBM = pl.BlockSpec(memory_space=pltpu.HBM)
PARAMS = pltpu.CompilerParams(vmem_limit_bytes=20 * 1024 * 1024)


def iota(shape, dim):
    return lax.broadcasted_iota(jnp.int32, shape, dim)


def down_taps(distance):
    size = jnp.abs(distance)
    value = jnp.where(size == 0, 6.0, jnp.where(size == 1, 4.0, jnp.where(size == 2, 1.0, 0.0)))
    return (value / 256.0).astype(jnp.bfloat16)


def up_taps(distance):
    size = jnp.abs(distance)
    value = jnp.where(size == 0, 0.75, jnp.where(size == 1, 0.5, jnp.where(size == 2, 0.125, 0.0)))
    return (value / 2.0).astype(jnp.bfloat16)


def halves(x):
    high = x.astype(jnp.bfloat16)
    low = (x - high.astype(jnp.float32)).astype(jnp.bfloat16)
    return jnp.concatenate([high, low], axis=-1)


def dot(x, table):
    return jnp.dot(x, table, preferred_element_type=jnp.float32)


def shift_down(x):
    return pltpu.roll(x, 1, axis=x.ndim - 2)


def shift_up(x):
    return pltpu.roll(x, SUB - 1, axis=x.ndim - 2)


def sublane(x):
    return iota(x.shape, x.ndim - 2)


def rows_down(planes, scaled=False):
    first, last = planes[0], planes[-1]
    top = sublane(first) == 0
    quad = (lambda x: x) if scaled else (lambda x: 4.0 * x)
    minus2 = jnp.where(top, first, shift_down(planes[-2]))
    minus1 = jnp.where(top, 4.0 * first if scaled else first, shift_down(last))
    plus = jnp.where(sublane(first) == SUB - 1, 0.25 * last if scaled else last, shift_up(first))
    padded = [minus2, minus1] + list(planes) + [plus]
    out = []
    for at in range(0, len(planes), 2):
        a, b, c, d, e = padded[at:at + 5]
        out.append((a + e) + quad(b + d) + 6.0 * c)
    return out


def padded_for_up(planes):
    first, last = planes[0], planes[-1]
    below = jnp.where(sublane(first) == 0, first, shift_down(last))
    above = jnp.where(sublane(first) == SUB - 1, last, shift_up(first))
    return [below] + list(planes) + [above]


def rows_up(planes):
    padded = padded_for_up(planes)
    sums = [one + two for one, two in zip(padded[:-1], padded[1:])]
    out = []
    for at in range(len(planes)):
        out.append(0.25 * (sums[at] + sums[at + 1]) + planes[at])
        out.append(sums[at + 1])
    return out


def gather_along(dim):
    return lax.GatherDimensionNumbers(
        offset_dims=(),
        collapsed_slice_dims=(dim,),
        start_index_map=(dim,),
        operand_batching_dims=(1 - dim,),
        start_indices_batching_dims=(1 - dim,),
    )


def look_up(table, index, dim=0):
    return lax.gather(
        table, index[..., None], gather_along(dim), (1, 1), mode=lax.GatherScatterMode.PROMISE_IN_BOUNDS
    )


def cell(x, cells):
    scaled = x * float(cells)
    index = jnp.minimum(jnp.floor(scaled), float(cells - 1))
    return index.astype(jnp.int32), scaled - index


def by_lane(p):
    return p % 4 == 1


def curve_cell(p, x):
    return cell(x, FINE if by_lane(p) else (KNOTS - 1) // 2)


def curve_tables(curve_row, k):
    steps = (KNOTS - 1) // 2
    turn = lax.div(steps * k, LEVELS - 1)
    phase = (steps * k - (LEVELS - 1) * turn).astype(jnp.float32) / (LEVELS - 1)
    width = curve_row.shape[-1]
    row = jnp.broadcast_to(curve_row, (SUB, width))
    offset = iota((SUB, width), 1) - iota((SUB, width), 0)

    def node(shift):
        at = jnp.where(offset == steps - turn + shift, row, 0.0)
        return jnp.sum(at, axis=1, keepdims=True)

    left, middle, right = node(-1), node(0), node(1)
    slope = middle - left
    bend = (right - middle) - slope
    start = (k.astype(jnp.float32) / (LEVELS - 1) + middle) - phase * slope - phase * bend
    spread = lambda v: jnp.broadcast_to(v, (SUB, LANES))
    coarse = (spread(start), spread(slope), spread(bend))
    phase = spread(phase)

    lane = iota((SUB, LANES), 1)
    index = jnp.minimum(jnp.floor((lane.astype(jnp.float32) + 0.5) / (LEVELS - 1)), float(SUB - 1))
    index = index.astype(jnp.int32)
    within = (lane - (LEVELS - 1) * index).astype(jnp.float32)
    ends = [remap(coarse + (phase,), index, (within + side) / (LEVELS - 1)) for side in (0.0, 1.0)]
    fine = (ends[0], ends[1] - ends[0])
    return (phase,) + coarse + fine + tuple(4.0 * table for table in coarse + fine)


def remap(tables, index, rest):
    start, slope, bend, phase = tables
    bent = jnp.maximum(rest, phase)
    return look_up(start, index) + look_up(slope, index) * rest + look_up(bend, index) * bent


def remap_pair(table_ref, first, planes, index_of, rest_of):
    tables = [[table_ref[first + copy, kind] for kind in range(TABLES)] for copy in range(2)]
    mapped = [[], []]
    for p in range(planes):
        index, rest = index_of(p), rest_of(p)
        at = 6 if p % 2 else 1
        for copy in range(2):
            phase, (start, slope, bend, value, step) = tables[copy][0], tables[copy][at:at + 5]
            if by_lane(p):
                result = look_up(value, index, 1) + look_up(step, index, 1) * rest
            else:
                result = remap((start, slope, bend, phase), index, rest)
            mapped[copy].append(result)
    return mapped


def tone_tables(low, high):
    middle = (KNOTS - 1) // 2
    scale = middle / (LEVELS - 1)
    spread = lambda v: jnp.broadcast_to(v, (SUB, LANES))
    sub = iota((SUB, LANES), 0)

    def parts(curves, k):
        level = (sub + k).astype(jnp.float32) / (LEVELS - 1)
        left, centre, right = [spread(curves[:, at:at + 1]) for at in (middle - 1, middle, middle + 1)]
        return level + centre, scale * (right - centre), scale * (centre - left)

    def following(x, then):
        return jnp.where(sub == SUB - 1, spread(then[0:1, :]), shift_up(x))

    one, two = parts(low, 0), parts(high, LEVELS // 2)
    lane = iota((SUB, LANES), 1)
    tables = []
    for kind in range(3):
        rows = []
        for here, then in ((one, two), (two, two)):
            if kind == 0:
                rows.append(here[0])
            elif kind == 1:
                rows.append(following(here[0], then[0]) - here[0])
            else:
                rows.append(here[1] - following(here[2], then[2]))
        along = jnp.where(lane == sub, rows[0], jnp.where(lane == sub + SUB, rows[1], 0.0))
        tables.append(spread(jnp.sum(along, axis=0, keepdims=True)))
    return tables


def tone(tables, x):
    index, rest = cell(x, LEVELS - 1)
    base, step, arc = [look_up(table, index, 1) for table in tables]
    return base + rest * (step + (1.0 - rest) * arc)


def scaled_level(x):
    place = x * float(LEVELS - 1)
    half = 0.5 * place
    return place, jnp.abs(1.0 - 2.0 * (half - jnp.floor(half)))


def start_all(pairs, sems):
    copies = [pltpu.make_async_copy(one, two, sems.at[at]) for at, (one, two) in enumerate(pairs)]
    for copy in copies:
        copy.start()
    return copies


def wait_all(copies):
    for copy in copies:
        copy.wait()


def kept_lanes(lvl):
    lane = iota((SUB, LANES), 1)
    return (lane >= PIECE * lvl) & (lane < LANES - PIECE * (1 - lvl))


def unpack(sent, lvl):
    lane = iota((SUB, LANES), 1)
    planes = []
    for group in range(len(sent) // 3):
        three = sent[3 * group:3 * group + 3]
        one, two, three_on = [pltpu.roll(x, PIECE * (at + 1), axis=1) for at, x in enumerate(three)]
        later = jnp.where(lane < PIECE * (2 + lvl), two, three_on)
        planes += three + [jnp.where(lane < PIECE * (1 + lvl), one, later)]
    return planes


def near_column(lvl, lane):
    return lane + jnp.where(lvl == 0, LEFT, RIGHT)


def away_column(lvl, lane):
    return lane + jnp.where(lvl == 0, RIGHT, LEFT)


def level_one_column(lvl, at):
    return jnp.where(at < LANES, near_column(lvl, at), away_column(lvl, at - LANES))


def stage_kernel(image_ref, curves_ref, edge_ref, inner_ref, sent_ref, mine_ref, own_ref, rim_ref, wide_ref,
                 small_ref, near_ref, away_ref, narrow_ref, raise_ref, sems):
    lvl = lax.axis_index("lvl")
    planes = edge_ref.shape[0]
    half = 2 * LANES
    outermost = pl.multiple_of(lvl * 3 * LANES, LANES)
    pairs = [(curves_ref, mine_ref)]
    for q in range(SUB):
        rows = pl.ds(q * planes, planes)
        pairs.append((image_ref.at[rows, pl.ds(outermost, LANES)], edge_ref.at[:, q, :]))
        for tile in range(2):
            source = image_ref.at[rows, (tile + 1) * LANES:(tile + 2) * LANES]
            pairs.append((source, inner_ref.at[tile, :, q, :]))
    copies = start_all(pairs, sems)

    def put(ref, shape, value):
        table = value(iota(shape, 0), iota(shape, 1))
        ref[0:shape[0], :] = table
        ref[shape[0]:2 * shape[0], :] = table

    def place(i):
        tile = i // LANES
        return jnp.where(lvl == 0, i, i - 2 * tile * LANES + LANES)

    def rim_place(i):
        return i + jnp.where(lvl == 0, -RIM, half)

    def out_place(far, j):
        return j + jnp.where(lvl == far, 0, LANES)

    def wide(i, j):
        column = level_one_column(lvl, i)
        left = (i < LANES) == (lvl == 0)
        return jnp.where(left == (j < LANES // 2), down_taps(column - 2 * j), 0.0)

    def up_pair(column, far):
        def value(i, j):
            lane = j & (LANES - 1)
            taps = up_taps(2 * column(lvl, i) - (out_place(far, lane) + RIM))
            return jnp.where(j < LANES, taps, 0.25 * taps)
        return value

    put(own_ref, (3 * LANES, half),
        lambda i, j: down_taps(place(i) - 2 * (level_one_column(lvl, j) - RIM // 2)))
    put(rim_ref, (RIM, LANES), lambda i, j: down_taps(rim_place(i) - 2 * (near_column(lvl, j) - RIM // 2)))
    put(wide_ref, (half, LANES), wide)
    put(small_ref, (LANES, LANES), lambda i, j: down_taps(i - 2 * j))
    put(near_ref, (LANES, half), up_pair(near_column, 0))
    put(away_ref, (LANES, half), up_pair(away_column, 1))
    put(narrow_ref, (LANES, half), lambda i, j: up_taps(2 * i - level_one_column(lvl, j)))
    put(raise_ref, (LANES, LANES), lambda i, j: up_taps(2 * i - j))
    wait_all(copies)
    kept = kept_lanes(lvl)
    for group in range(planes // 4):
        *three, fourth = [edge_ref[4 * group + at] for at in range(4)]
        for at, x in enumerate(three):
            sent_ref[3 * group + at] = jnp.where(kept, x, pltpu.roll(fourth, LANES - PIECE * (at + 1), axis=1))


def put_kernel(half_ref, out_ref, sems, lvl):
    planes = half_ref.shape[1]
    pairs = []
    for tile, at in enumerate((3 * lvl, 1 + lvl)):
        columns = pl.ds(pl.multiple_of(at * LANES, LANES), LANES)
        for q in range(SUB):
            pairs.append((half_ref.at[tile, :, q, :], out_ref.at[pl.ds(q * planes, planes), columns]))
    wait_all(start_all(pairs, sems))


def put_mine_kernel(mine_ref, out_ref, sems):
    put_kernel(mine_ref, out_ref, sems, lax.axis_index("lvl"))


def put_theirs_kernel(theirs_ref, begun_ref, out_ref, sems):
    put_kernel(theirs_ref, out_ref, sems, 1 - lax.axis_index("lvl"))


def pick(place, weight, values):
    even, odd = values(0), values(1)
    for k in range(2, LEVELS, 2):
        even = jnp.where(place >= float(k - 1), values(k), even)
        odd = jnp.where(place >= float(k), values(k + 1), odd)
    return odd + weight * (even - odd)


def split_store(ref, reduced, column, width):
    for pair in range(len(reduced) // 2):
        both = jnp.concatenate(reduced[2 * pair:2 * pair + 2], axis=0)
        high = both.astype(jnp.bfloat16)
        low = (both - high.astype(jnp.float32)).astype(jnp.bfloat16)
        ref[pair, :, column:column + LANES] = high
        ref[pair, :, width + column:width + column + LANES] = low


def scale_odd(planes):
    return [4.0 * x if p % 2 else x for p, x in enumerate(planes)]


def all_tables(table_ref, curves_ref, first):
    for row in range(LEVELS // 2):
        for kind, table in enumerate(curve_tables(curves_ref[row:row + 1, :], first + row)):
            table_ref[first + row, kind] = table


def image_of(edge_ref, inner_ref, tile, p):
    lvl = lax.axis_index("lvl")
    return edge_ref[p] if tile == 0 else inner_ref[lvl if tile == 1 else 1 - lvl, p]


def multiply_own(part_ref, down_ref, gauss_ref, target):
    part = part_ref[...].reshape(-1, 6 * LANES)
    result = dot(part, down_ref[...]).reshape(2, part_ref.shape[1], 2, SUB, 2 * LANES)
    for copy in range(2):
        for tile in range(2):
            span = slice(tile * LANES, (tile + 1) * LANES)
            gauss_ref[tile, :, target + copy] = result[copy, :, :, :, span]


def own_pairs(table_ref, first, cell_ref, fraction_ref, down_ref, gauss_ref, last_ref, part_scr, before):
    planes = cell_ref.shape[1]
    pairs = LEVELS // 4
    waiting = before
    for step in range(pairs):
        multiply_own(waiting[0], down_ref, gauss_ref, waiting[1])
        ref = last_ref if step == pairs - 1 else part_scr.at[step % 2]
        for tile in range(3):
            mapped = remap_pair(
                table_ref, first + 2 * step, planes, lambda p: cell_ref[tile, p], lambda p: fraction_ref[tile, p]
            )
            for copy in range(2):
                split_store(ref.at[copy], rows_down(mapped[copy], scaled=True), tile * LANES, 3 * LANES)
        waiting = (ref, FIRST + first + 2 * step)


def waits_longest():
    return (lax.axis_index("band") == 0) & (lax.axis_index("tile") == 0) & (lax.axis_index("lvl") == 0)


def early_kernel(*refs):
    @pl.when(waits_longest())
    def _():
        mine_part(*refs)


def late_kernel(*refs):
    @pl.when(jnp.logical_not(waits_longest()))
    def _():
        mine_part(*refs[:4], *refs[11:])


def mine_part(edge_ref, inner_ref, mine_ref, down_ref, gauss_ref, last_ref, place_ref, weight_ref,
                table_ref, cell_ref, fraction_ref, part_scr):
    planes = edge_ref.shape[0]
    first = lax.axis_index("lvl") * (LEVELS // 2)
    all_tables(table_ref, mine_ref, first)
    image = functools.partial(image_of, edge_ref, inner_ref)
    for tile in range(3):
        for p in range(planes):
            x = image(tile, p)
            cell_ref[tile, p], fraction_ref[tile, p] = curve_cell(p, x)
            if tile < 2:
                place_ref[tile, p], weight_ref[tile, p] = scaled_level(x)
        reduced = rows_down(scale_odd([image(tile, p) for p in range(planes)]), scaled=True)
        for copy in range(2):
            split_store(part_scr.at[1, copy], reduced, tile * LANES, 3 * LANES)
    before = (part_scr.at[1], 0)
    own_pairs(table_ref, first, cell_ref, fraction_ref, down_ref, gauss_ref, last_ref, part_scr, before)


def other_kernel(edge_ref, inner_ref, mine_ref, other_ref, down_ref, cell_ref, fraction_ref, last_in_ref,
                 gauss_in_ref, table_in_ref, gauss_ref, table_ref, last_ref, tone_ref, part_scr):
    lvl = lax.axis_index("lvl")
    first = (1 - lvl) * (LEVELS // 2)
    all_tables(table_ref, other_ref, first)
    low = jnp.where(lvl == 0, mine_ref[...], other_ref[...])
    high = jnp.where(lvl == 0, other_ref[...], mine_ref[...])
    tones = tone_tables(low, high)
    for tile in range(2):
        for p in range(edge_ref.shape[0]):
            tone_ref[tile, p] = tone(tones, image_of(edge_ref, inner_ref, tile, p))
    before = (last_in_ref, FIRST + lvl * (LEVELS // 2) + LEVELS // 2 - 2)
    own_pairs(table_ref, first, cell_ref, fraction_ref, down_ref, gauss_ref, last_ref, part_scr, before)


def rest_kernel(halo_ref, gauss_in_ref, last_ref, tone_ref, place_ref, weight_ref, table_ref, down_ref,
                rim_ref, wide_ref, small_ref, near_ref, away_ref, narrow_ref, raise_ref, out_ref, gauss_ref,
                cell_scr, rest_scr, part_scr, up_scr):
    lvl = lax.axis_index("lvl")
    halo = unpack([halo_ref[at] for at in range(halo_ref.shape[0])], 1 - lvl)
    planes = len(halo)
    half = 2 * LANES
    pairs = LEVELS // 2

    multiply_own(last_ref, down_ref, gauss_ref, FIRST + (1 - lvl) * (LEVELS // 2) + LEVELS // 2 - 2)

    def columns_up(tile):
        source = jnp.concatenate([gauss_ref[tile, p // 2, FIRST:, p % 2] for p in range(planes // 2)], axis=0)
        result = dot(halves(source.reshape(-1, LANES)), tables_up[tile][...])
        up_scr[tile] = result.reshape(planes // 2, LEVELS, SUB, half)

    tables_up = (near_ref, away_ref)
    for p in range(planes):
        cell_scr[p], rest_scr[p] = curve_cell(p, halo[p])

    def multiply(slot, target):
        part = part_scr[slot].reshape(-1, 2 * RIM)
        result = dot(part, rim_ref[...]).reshape(2, planes // 4, 2, SUB, LANES)
        for copy in range(2):
            gauss_ref[0, :, target + copy] = gauss_ref[0, :, target + copy] + result[copy]

    reduced = rows_down(scale_odd(halo), scaled=True)
    for copy in range(2):
        split_store(part_scr.at[1, copy], reduced, 0, RIM)
    for step in range(pairs):
        slot = step % 2
        multiply(1 - slot, 2 * step)
        mapped = remap_pair(table_ref, 2 * step, planes, lambda p: cell_scr[p], lambda p: rest_scr[p])
        for copy in range(2):
            split_store(part_scr.at[slot, copy], rows_down(mapped[copy], scaled=True), 0, RIM)
    multiply((pairs - 1) % 2, 2 * pairs)

    sums = {}

    def quarter_sum(tile, at):
        if (tile, at) not in sums:
            count = planes // 2
            edge = lambda p: up_scr[tile, p, :, :, LANES:half]
            if at == 0:
                before = jnp.where(sublane(edge(0)) == 0, edge(0), shift_down(edge(count - 1)))
            else:
                before = edge(at - 1)
            if at == count:
                after = jnp.where(sublane(edge(0)) == SUB - 1, edge(count - 1), shift_up(edge(0)))
            else:
                after = edge(at)
            sums[tile, at] = before + after
        return sums[tile, at]

    def level_zero(tile, p):
        above, below = quarter_sum(tile, p // 2), quarter_sum(tile, p // 2 + 1)
        at = (place_ref[tile, p], weight_ref[tile, p])
        if p % 2 == 0:
            detail = pick(*at, lambda k: (above[k] + below[k]) + up_scr[tile, p // 2, k, :, 0:LANES])
        else:
            detail = 4.0 * pick(*at, lambda k: below[k])
        out_ref[tile, p] = tone_ref[tile, p] - detail

    waiting = [(tile, p) for tile in (1, 0) for p in range(planes)]

    def meanwhile(count):
        for _ in range(min(count, len(waiting))):
            level_zero(*waiting.pop(0))

    def level_one(p):
        return jnp.concatenate([gauss_ref[tile, p // 2, :, p % 2] for tile in range(2)], axis=-1)

    def next_level(coarse, table):
        reduced = rows_down(coarse)
        stacked = jnp.concatenate(reduced, axis=0)
        result = dot(halves(stacked.reshape(-1, stacked.shape[-1])), table)
        result = result.reshape(len(reduced), STACK, SUB, LANES)
        return [result[p] for p in range(len(reduced))]

    def raise_columns(stacks, table):
        stacked = jnp.concatenate(stacks, axis=0)
        result = dot(halves(stacked.reshape(-1, LANES)), table)
        return result.reshape((len(stacks), -1, SUB, table.shape[1]))

    def raise_stack(coarse, table):
        result = raise_columns([plane[FIRST:] for plane in coarse], table)
        return rows_up([result[p] for p in range(len(coarse))])

    def raise_one(planes_of, table):
        result = raise_columns([plane[None] for plane in planes_of], table)
        return rows_up([result[p, 0] for p in range(len(planes_of))])

    def coefficient(level, raised, p):
        here = gauss[level][p]
        return pick(*scaled_level(here[0]), lambda k: here[FIRST + k] - raised[p][k])

    lift = raise_ref[...]
    gauss = [None, [level_one(p) for p in range(planes // 2)]]
    gauss.append(next_level(gauss[1], wide_ref[...]))
    raised = [None, raise_stack(gauss[2], narrow_ref[...])]
    columns_up(1)
    columns_up(0)
    coeffs = [None, []]
    quarter = planes // 8
    for level in range(2, PYR - 1):
        gauss.append(next_level(gauss[level], small_ref[...]))
        coeffs[1] += [coefficient(1, raised[1], p) for p in range(quarter * (level - 2), quarter * (level - 1))]
        raised.append(raise_stack(gauss[level + 1], lift))
    base = raise_one([gauss[PYR - 1][0][0]], lift)
    coeffs[1] += [coefficient(1, raised[1], p) for p in range(3 * quarter, planes // 2)]
    for level in range(2, PYR - 1):
        coeffs.append([coefficient(level, raised[level], p) for p in range(len(gauss[level]))])
    for level in range(PYR - 2, 0, -1):
        out = [one + two for one, two in zip(coeffs[level], base)]
        if level > 1:
            base = raise_one(out, narrow_ref[...] if level == 2 else lift)
        else:
            base = []
            for tile in range(2):
                span = slice(tile * LANES, (tile + 1) * LANES)
                base.append(raise_one([plane[:, span] for plane in out], tables_up[tile][:, 0:LANES]))
        meanwhile(planes // 2)
    meanwhile(2 * planes)
    for tile in range(2):
        for p in range(planes):
            out_ref[tile, p] = out_ref[tile, p] + base[tile][p]


def call(kernel, name, in_specs, out_shape, scratch, out_space=VMEM, **others):
    return pl.pallas_call(
        kernel,
        name=name,
        in_specs=in_specs,
        out_specs=jax.tree.map(lambda _: out_space, out_shape),
        out_shape=out_shape,
        scratch_shapes=scratch,
        compiler_params=PARAMS,
        **others,
    )


def body(image, curves):
    rows, width = image.shape
    planes = rows // SUB
    half = width // 2
    count = lax.axis_size("tile")
    f32 = lambda *shape: jax.ShapeDtypeStruct(shape, jnp.float32)
    b16 = lambda *shape: jax.ShapeDtypeStruct(shape, jnp.bfloat16)
    fast = lambda *shape: pltpu.VMEM(shape, jnp.float32)
    i32 = lambda *shape: jax.ShapeDtypeStruct(shape, jnp.int32)
    fast_int = lambda *shape: pltpu.VMEM(shape, jnp.int32)
    fast_half = lambda *shape: pltpu.VMEM(shape, jnp.bfloat16)
    in_hbm = lambda x: pltpu.with_memory_space_constraint(x, pltpu.HBM)
    swap = [(0, 1), (1, 0)]

    edge, inner, sent, mine, down, rim, wide, small, near, away, narrow, lift = call(
        stage_kernel, "stage", [HBM] * 2,
        [f32(planes, SUB, LANES), f32(2, planes, SUB, LANES), f32(planes * 3 // 4, SUB, LANES), f32(*curves.shape), b16(6 * LANES, half),
         b16(2 * RIM, LANES), b16(2 * half, LANES), b16(2 * LANES, LANES), b16(2 * LANES, half),
         b16(2 * LANES, half), b16(2 * LANES, half), b16(2 * LANES, LANES)],
        [pltpu.SemaphoreType.DMA((3 * SUB + 1,))],
    )(in_hbm(image), in_hbm(curves))
    pairs = []
    for tile in range(count):
        pairs.append((2 * tile + 1, 2 * ((tile + 1) % count)))
        pairs.append((2 * tile, 2 * ((tile - 1) % count) + 1))

    gauss_shape = f32(2, planes // 4, STACK, 2, SUB, LANES)
    out_shape = f32(2, planes, SUB, LANES)
    last_shape = b16(2, planes // 4, 2 * SUB, 6 * LANES)
    table_shape = f32(LEVELS, TABLES, SUB, LANES)
    strip = (3, planes, SUB, LANES)
    part = [fast_half(2, *last_shape.shape)]
    own_shapes = [gauss_shape, last_shape, out_shape, out_shape, table_shape, i32(*strip), f32(*strip)]
    begun = call(early_kernel, "early", [VMEM] * 4, own_shapes, part)(edge, inner, mine, down)
    sent, begun = lax.optimization_barrier((sent, begun))
    halo = lax.ppermute(sent, ("tile", "lvl"), pairs)
    gauss, last, place, weight, tables, cells, fractions = call(
        late_kernel, "late", [VMEM] * 11, own_shapes, part,
        input_output_aliases={4 + at: at for at in range(7)},
    )(edge, inner, mine, down, *begun)
    swapped, last = lax.optimization_barrier((mine, last))
    other_curves = lax.ppermute(swapped, "lvl", swap)
    gauss, tables, last, toned = call(
        other_kernel, "other", [VMEM] * 10, [gauss_shape, table_shape, last_shape, out_shape], part,
        input_output_aliases={8: 0, 9: 1},
    )(edge, inner, mine, other_curves, down, cells, fractions, last, gauss, tables)
    mine, _ = call(
        rest_kernel, "rest", [VMEM] * 15, [out_shape, gauss_shape],
        [fast_int(planes, SUB, RIM), fast(planes, SUB, RIM),
         fast_half(2, 2, planes // 4, 2 * SUB, 2 * RIM), fast(2, planes // 2, LEVELS, SUB, half)],
        input_output_aliases={1: 1},
    )(halo, gauss, last, toned, place, weight, tables, down, rim, wide, small, near, away, narrow, lift)
    theirs = lax.ppermute(mine, "lvl", swap)
    sems = [pltpu.SemaphoreType.DMA((2 * SUB,))]
    begun = call(put_mine_kernel, "put_mine", [VMEM], f32(rows, width), sems, HBM)(mine)
    return call(
        put_theirs_kernel, "put_theirs", [VMEM, HBM], f32(rows, width), sems, HBM, input_output_aliases={1: 0}
    )(theirs, begun)


def solution(mesh):
    placed = (P("band", "tile"), P("lvl", None))
    return jax.shard_map(
        body, mesh=mesh, in_specs=placed, out_specs=P("band", "tile"), check_vma=False
    )
```

```python
import functools

import jax
import jax.numpy as jnp
from jax import lax
from jax.experimental import pallas as pl
from jax.experimental.pallas import tpu as pltpu
from jax.sharding import PartitionSpec as P

LEVELS = 16
KNOTS = 17
PYR = 6

SUB = 8
LANES = 128
PIECE = LANES // 4
RIM = LANES
FIRST = 2
STACK = FIRST + LEVELS
LEFT, RIGHT = 2, 126
FINE = (LEVELS - 1) * (KNOTS - 1) // 2
TABLES = 11

VMEM = pl.BlockSpec(memory_space=pltpu.VMEM)
HBM = pl.BlockSpec(memory_space=pltpu.HBM)
PARAMS = pltpu.CompilerParams(vmem_limit_bytes=20 * 1024 * 1024)


def iota(shape, dim):
    return lax.broadcasted_iota(jnp.int32, shape, dim)


def down_taps(distance):
    size = jnp.abs(distance)
    value = jnp.where(size == 0, 6.0, jnp.where(size == 1, 4.0, jnp.where(size == 2, 1.0, 0.0)))
    return (value / 256.0).astype(jnp.bfloat16)


def up_taps(distance):
    size = jnp.abs(distance)
    value = jnp.where(size == 0, 0.75, jnp.where(size == 1, 0.5, jnp.where(size == 2, 0.125, 0.0)))
    return (value / 2.0).astype(jnp.bfloat16)


def halves(x):
    high = x.astype(jnp.bfloat16)
    low = (x - high.astype(jnp.float32)).astype(jnp.bfloat16)
    return jnp.concatenate([high, low], axis=-1)


def dot(x, table):
    return jnp.dot(x, table, preferred_element_type=jnp.float32)


def shift_down(x):
    return pltpu.roll(x, 1, axis=x.ndim - 2)


def shift_up(x):
    return pltpu.roll(x, SUB - 1, axis=x.ndim - 2)


def sublane(x):
    return iota(x.shape, x.ndim - 2)


def rows_down(planes, scaled=False):
    first, last = planes[0], planes[-1]
    top = sublane(first) == 0
    quad = (lambda x: x) if scaled else (lambda x: 4.0 * x)
    minus2 = jnp.where(top, first, shift_down(planes[-2]))
    minus1 = jnp.where(top, 4.0 * first if scaled else first, shift_down(last))
    plus = jnp.where(sublane(first) == SUB - 1, 0.25 * last if scaled else last, shift_up(first))
    padded = [minus2, minus1] + list(planes) + [plus]
    out = []
    for at in range(0, len(planes), 2):
        a, b, c, d, e = padded[at:at + 5]
        out.append((a + e) + quad(b + d) + 6.0 * c)
    return out


def padded_for_up(planes):
    first, last = planes[0], planes[-1]
    below = jnp.where(sublane(first) == 0, first, shift_down(last))
    above = jnp.where(sublane(first) == SUB - 1, last, shift_up(first))
    return [below] + list(planes) + [above]


def rows_up(planes):
    padded = padded_for_up(planes)
    sums = [one + two for one, two in zip(padded[:-1], padded[1:])]
    out = []
    for at in range(len(planes)):
        out.append(0.25 * (sums[at] + sums[at + 1]) + planes[at])
        out.append(sums[at + 1])
    return out


def gather_along(dim):
    return lax.GatherDimensionNumbers(
        offset_dims=(),
        collapsed_slice_dims=(dim,),
        start_index_map=(dim,),
        operand_batching_dims=(1 - dim,),
        start_indices_batching_dims=(1 - dim,),
    )


def look_up(table, index, dim=0):
    return lax.gather(
        table, index[..., None], gather_along(dim), (1, 1), mode=lax.GatherScatterMode.PROMISE_IN_BOUNDS
    )


def cell(x, cells):
    scaled = x * float(cells)
    index = jnp.minimum(jnp.floor(scaled), float(cells - 1))
    return index.astype(jnp.int32), scaled - index


def by_lane(p):
    return p % 4 == 1


def curve_cell(p, x):
    return cell(x, FINE if by_lane(p) else (KNOTS - 1) // 2)


def curve_tables(curve_row, k):
    steps = (KNOTS - 1) // 2
    turn = lax.div(steps * k, LEVELS - 1)
    phase = (steps * k - (LEVELS - 1) * turn).astype(jnp.float32) / (LEVELS - 1)
    width = curve_row.shape[-1]
    row = jnp.broadcast_to(curve_row, (SUB, width))
    offset = iota((SUB, width), 1) - iota((SUB, width), 0)

    def node(shift):
        at = jnp.where(offset == steps - turn + shift, row, 0.0)
        return jnp.sum(at, axis=1, keepdims=True)

    left, middle, right = node(-1), node(0), node(1)
    slope = middle - left
    bend = (right - middle) - slope
    start = (k.astype(jnp.float32) / (LEVELS - 1) + middle) - phase * slope - phase * bend
    spread = lambda v: jnp.broadcast_to(v, (SUB, LANES))
    coarse = (spread(start), spread(slope), spread(bend))
    phase = spread(phase)

    lane = iota((SUB, LANES), 1)
    index = jnp.minimum(jnp.floor((lane.astype(jnp.float32) + 0.5) / (LEVELS - 1)), float(SUB - 1))
    index = index.astype(jnp.int32)
    within = (lane - (LEVELS - 1) * index).astype(jnp.float32)
    ends = [remap(coarse + (phase,), index, (within + side) / (LEVELS - 1)) for side in (0.0, 1.0)]
    fine = (ends[0], ends[1] - ends[0])
    return (phase,) + coarse + fine + tuple(4.0 * table for table in coarse + fine)


def remap(tables, index, rest):
    start, slope, bend, phase = tables
    bent = jnp.maximum(rest, phase)
    return look_up(start, index) + look_up(slope, index) * rest + look_up(bend, index) * bent


def remap_pair(table_ref, first, planes, index_of, rest_of):
    tables = [[table_ref[first + copy, kind] for kind in range(TABLES)] for copy in range(2)]
    mapped = [[], []]
    for p in range(planes):
        index, rest = index_of(p), rest_of(p)
        at = 6 if p % 2 else 1
        for copy in range(2):
            phase, (start, slope, bend, value, step) = tables[copy][0], tables[copy][at:at + 5]
            if by_lane(p):
                result = look_up(value, index, 1) + look_up(step, index, 1) * rest
            else:
                result = remap((start, slope, bend, phase), index, rest)
            mapped[copy].append(result)
    return mapped


def tone_tables(low, high):
    middle = (KNOTS - 1) // 2
    scale = middle / (LEVELS - 1)
    spread = lambda v: jnp.broadcast_to(v, (SUB, LANES))
    sub = iota((SUB, LANES), 0)

    def parts(curves, k):
        level = (sub + k).astype(jnp.float32) / (LEVELS - 1)
        left, centre, right = [spread(curves[:, at:at + 1]) for at in (middle - 1, middle, middle + 1)]
        return level + centre, scale * (right - centre), scale * (centre - left)

    def following(x, then):
        return jnp.where(sub == SUB - 1, spread(then[0:1, :]), shift_up(x))

    one, two = parts(low, 0), parts(high, LEVELS // 2)
    lane = iota((SUB, LANES), 1)
    tables = []
    for kind in range(3):
        rows = []
        for here, then in ((one, two), (two, two)):
            if kind == 0:
                rows.append(here[0])
            elif kind == 1:
                rows.append(following(here[0], then[0]) - here[0])
            else:
                rows.append(here[1] - following(here[2], then[2]))
        along = jnp.where(lane == sub, rows[0], jnp.where(lane == sub + SUB, rows[1], 0.0))
        tables.append(spread(jnp.sum(along, axis=0, keepdims=True)))
    return tables


def tone(tables, x):
    index, rest = cell(x, LEVELS - 1)
    base, step, arc = [look_up(table, index, 1) for table in tables]
    return base + rest * (step + (1.0 - rest) * arc)


def scaled_level(x):
    place = x * float(LEVELS - 1)
    half = 0.5 * place
    return place, jnp.abs(1.0 - 2.0 * (half - jnp.floor(half)))


def start_all(pairs, sems):
    copies = [pltpu.make_async_copy(one, two, sems.at[at]) for at, (one, two) in enumerate(pairs)]
    for copy in copies:
        copy.start()
    return copies


def wait_all(copies):
    for copy in copies:
        copy.wait()


def kept_lanes(lvl):
    lane = iota((SUB, LANES), 1)
    return (lane >= PIECE * lvl) & (lane < LANES - PIECE * (1 - lvl))


def unpack(sent, lvl):
    lane = iota((SUB, LANES), 1)
    planes = []
    for group in range(len(sent) // 3):
        three = sent[3 * group:3 * group + 3]
        one, two, three_on = [pltpu.roll(x, PIECE * (at + 1), axis=1) for at, x in enumerate(three)]
        later = jnp.where(lane < PIECE * (2 + lvl), two, three_on)
        planes += three + [jnp.where(lane < PIECE * (1 + lvl), one, later)]
    return planes


def near_column(lvl, lane):
    return lane + jnp.where(lvl == 0, LEFT, RIGHT)


def away_column(lvl, lane):
    return lane + jnp.where(lvl == 0, RIGHT, LEFT)


def level_one_column(lvl, at):
    return jnp.where(at < LANES, near_column(lvl, at), away_column(lvl, at - LANES))


def stage_kernel(image_ref, curves_ref, edge_ref, inner_ref, sent_ref, mine_ref, own_ref, rim_ref, wide_ref,
                 small_ref, near_ref, away_ref, narrow_ref, raise_ref, sems):
    lvl = lax.axis_index("lvl")
    planes = edge_ref.shape[0]
    half = 2 * LANES
    outermost = pl.multiple_of(lvl * 3 * LANES, LANES)
    pairs = [(curves_ref, mine_ref)]
    for q in range(SUB):
        rows = pl.ds(q * planes, planes)
        pairs.append((image_ref.at[rows, pl.ds(outermost, LANES)], edge_ref.at[:, q, :]))
        for tile in range(2):
            source = image_ref.at[rows, (tile + 1) * LANES:(tile + 2) * LANES]
            pairs.append((source, inner_ref.at[tile, :, q, :]))
    copies = start_all(pairs, sems)

    def put(ref, shape, value):
        table = value(iota(shape, 0), iota(shape, 1))
        ref[0:shape[0], :] = table
        ref[shape[0]:2 * shape[0], :] = table

    def place(i):
        tile = i // LANES
        return jnp.where(lvl == 0, i, i - 2 * tile * LANES + LANES)

    def rim_place(i):
        return i + jnp.where(lvl == 0, -RIM, half)

    def out_place(far, j):
        return j + jnp.where(lvl == far, 0, LANES)

    def wide(i, j):
        column = level_one_column(lvl, i)
        left = (i < LANES) == (lvl == 0)
        return jnp.where(left == (j < LANES // 2), down_taps(column - 2 * j), 0.0)

    def up_pair(column, far):
        def value(i, j):
            lane = j & (LANES - 1)
            taps = up_taps(2 * column(lvl, i) - (out_place(far, lane) + RIM))
            return jnp.where(j < LANES, taps, 0.25 * taps)
        return value

    put(own_ref, (3 * LANES, half),
        lambda i, j: down_taps(place(i) - 2 * (level_one_column(lvl, j) - RIM // 2)))
    put(rim_ref, (RIM, LANES), lambda i, j: down_taps(rim_place(i) - 2 * (near_column(lvl, j) - RIM // 2)))
    put(wide_ref, (half, LANES), wide)
    put(small_ref, (LANES, LANES), lambda i, j: down_taps(i - 2 * j))
    put(near_ref, (LANES, half), up_pair(near_column, 0))
    put(away_ref, (LANES, half), up_pair(away_column, 1))
    put(narrow_ref, (LANES, half), lambda i, j: up_taps(2 * i - level_one_column(lvl, j)))
    put(raise_ref, (LANES, LANES), lambda i, j: up_taps(2 * i - j))
    wait_all(copies)
    kept = kept_lanes(lvl)
    for group in range(planes // 4):
        *three, fourth = [edge_ref[4 * group + at] for at in range(4)]
        for at, x in enumerate(three):
            sent_ref[3 * group + at] = jnp.where(kept, x, pltpu.roll(fourth, LANES - PIECE * (at + 1), axis=1))


def put_kernel(half_ref, out_ref, sems, lvl):
    planes = half_ref.shape[1]
    pairs = []
    for tile, at in enumerate((3 * lvl, 1 + lvl)):
        columns = pl.ds(pl.multiple_of(at * LANES, LANES), LANES)
        for q in range(SUB):
            pairs.append((half_ref.at[tile, :, q, :], out_ref.at[pl.ds(q * planes, planes), columns]))
    wait_all(start_all(pairs, sems))


def put_mine_kernel(mine_ref, out_ref, sems):
    put_kernel(mine_ref, out_ref, sems, lax.axis_index("lvl"))


def put_theirs_kernel(theirs_ref, begun_ref, out_ref, sems):
    put_kernel(theirs_ref, out_ref, sems, 1 - lax.axis_index("lvl"))


def pick(place, weight, values):
    even, odd = values(0), values(1)
    for k in range(2, LEVELS, 2):
        even = jnp.where(place >= float(k - 1), values(k), even)
        odd = jnp.where(place >= float(k), values(k + 1), odd)
    return odd + weight * (even - odd)


def split_store(ref, reduced, column, width):
    for pair in range(len(reduced) // 2):
        both = jnp.concatenate(reduced[2 * pair:2 * pair + 2], axis=0)
        high = both.astype(jnp.bfloat16)
        low = (both - high.astype(jnp.float32)).astype(jnp.bfloat16)
        ref[pair, :, column:column + LANES] = high
        ref[pair, :, width + column:width + column + LANES] = low


def scale_odd(planes):
    return [4.0 * x if p % 2 else x for p, x in enumerate(planes)]


def all_tables(table_ref, curves_ref, first):
    for row in range(LEVELS // 2):
        for kind, table in enumerate(curve_tables(curves_ref[row:row + 1, :], first + row)):
            table_ref[first + row, kind] = table


def image_of(edge_ref, inner_ref, tile, p):
    lvl = lax.axis_index("lvl")
    return edge_ref[p] if tile == 0 else inner_ref[lvl if tile == 1 else 1 - lvl, p]


def multiply_own(part_ref, down_ref, gauss_ref, target):
    part = part_ref[...].reshape(-1, 6 * LANES)
    result = dot(part, down_ref[...]).reshape(2, part_ref.shape[1], 2, SUB, 2 * LANES)
    for copy in range(2):
        for tile in range(2):
            span = slice(tile * LANES, (tile + 1) * LANES)
            gauss_ref[tile, :, target + copy] = result[copy, :, :, :, span]


def own_pairs(table_ref, first, cell_ref, fraction_ref, down_ref, gauss_ref, last_ref, part_scr, before):
    planes = cell_ref.shape[1]
    pairs = LEVELS // 4
    waiting = before
    for step in range(pairs):
        multiply_own(waiting[0], down_ref, gauss_ref, waiting[1])
        ref = last_ref if step == pairs - 1 else part_scr.at[step % 2]
        for tile in range(3):
            mapped = remap_pair(
                table_ref, first + 2 * step, planes, lambda p: cell_ref[tile, p], lambda p: fraction_ref[tile, p]
            )
            for copy in range(2):
                split_store(ref.at[copy], rows_down(mapped[copy], scaled=True), tile * LANES, 3 * LANES)
        waiting = (ref, FIRST + first + 2 * step)


def waits_longest():
    foremost = (lax.axis_index("band") == 0) | (lax.axis_index("lvl") == 1)
    return (lax.axis_index("tile") == 0) & foremost


def early_kernel(*refs):
    @pl.when(waits_longest())
    def _():
        mine_part(*refs)


def late_kernel(*refs):
    @pl.when(jnp.logical_not(waits_longest()))
    def _():
        mine_part(*refs[:4], *refs[11:])


def mine_part(edge_ref, inner_ref, mine_ref, down_ref, gauss_ref, last_ref, place_ref, weight_ref,
                table_ref, cell_ref, fraction_ref, part_scr):
    planes = edge_ref.shape[0]
    first = lax.axis_index("lvl") * (LEVELS // 2)
    all_tables(table_ref, mine_ref, first)
    image = functools.partial(image_of, edge_ref, inner_ref)
    for tile in range(3):
        for p in range(planes):
            x = image(tile, p)
            cell_ref[tile, p], fraction_ref[tile, p] = curve_cell(p, x)
            if tile < 2:
                place_ref[tile, p], weight_ref[tile, p] = scaled_level(x)
        reduced = rows_down(scale_odd([image(tile, p) for p in range(planes)]), scaled=True)
        for copy in range(2):
            split_store(part_scr.at[1, copy], reduced, tile * LANES, 3 * LANES)
    before = (part_scr.at[1], 0)
    own_pairs(table_ref, first, cell_ref, fraction_ref, down_ref, gauss_ref, last_ref, part_scr, before)


def other_kernel(edge_ref, inner_ref, mine_ref, other_ref, down_ref, cell_ref, fraction_ref, last_in_ref,
                 gauss_in_ref, table_in_ref, gauss_ref, table_ref, last_ref, tone_ref, part_scr):
    lvl = lax.axis_index("lvl")
    first = (1 - lvl) * (LEVELS // 2)
    all_tables(table_ref, other_ref, first)
    low = jnp.where(lvl == 0, mine_ref[...], other_ref[...])
    high = jnp.where(lvl == 0, other_ref[...], mine_ref[...])
    tones = tone_tables(low, high)
    for tile in range(2):
        for p in range(edge_ref.shape[0]):
            tone_ref[tile, p] = tone(tones, image_of(edge_ref, inner_ref, tile, p))
    before = (last_in_ref, FIRST + lvl * (LEVELS // 2) + LEVELS // 2 - 2)
    own_pairs(table_ref, first, cell_ref, fraction_ref, down_ref, gauss_ref, last_ref, part_scr, before)


def rest_kernel(halo_ref, gauss_in_ref, last_ref, tone_ref, place_ref, weight_ref, table_ref, down_ref,
                rim_ref, wide_ref, small_ref, near_ref, away_ref, narrow_ref, raise_ref, out_ref, gauss_ref,
                cell_scr, rest_scr, part_scr, up_scr):
    lvl = lax.axis_index("lvl")
    halo = unpack([halo_ref[at] for at in range(halo_ref.shape[0])], 1 - lvl)
    planes = len(halo)
    half = 2 * LANES
    pairs = LEVELS // 2

    multiply_own(last_ref, down_ref, gauss_ref, FIRST + (1 - lvl) * (LEVELS // 2) + LEVELS // 2 - 2)

    def columns_up(tile):
        source = jnp.concatenate([gauss_ref[tile, p // 2, FIRST:, p % 2] for p in range(planes // 2)], axis=0)
        result = dot(halves(source.reshape(-1, LANES)), tables_up[tile][...])
        up_scr[tile] = result.reshape(planes // 2, LEVELS, SUB, half)

    tables_up = (near_ref, away_ref)
    for p in range(planes):
        cell_scr[p], rest_scr[p] = curve_cell(p, halo[p])

    def multiply(slot, target):
        part = part_scr[slot].reshape(-1, 2 * RIM)
        result = dot(part, rim_ref[...]).reshape(2, planes // 4, 2, SUB, LANES)
        for copy in range(2):
            gauss_ref[0, :, target + copy] = gauss_ref[0, :, target + copy] + result[copy]

    reduced = rows_down(scale_odd(halo), scaled=True)
    for copy in range(2):
        split_store(part_scr.at[1, copy], reduced, 0, RIM)
    for step in range(pairs):
        slot = step % 2
        multiply(1 - slot, 2 * step)
        mapped = remap_pair(table_ref, 2 * step, planes, lambda p: cell_scr[p], lambda p: rest_scr[p])
        for copy in range(2):
            split_store(part_scr.at[slot, copy], rows_down(mapped[copy], scaled=True), 0, RIM)
    multiply((pairs - 1) % 2, 2 * pairs)

    sums = {}

    def quarter_sum(tile, at):
        if (tile, at) not in sums:
            count = planes // 2
            edge = lambda p: up_scr[tile, p, :, :, LANES:half]
            if at == 0:
                before = jnp.where(sublane(edge(0)) == 0, edge(0), shift_down(edge(count - 1)))
            else:
                before = edge(at - 1)
            if at == count:
                after = jnp.where(sublane(edge(0)) == SUB - 1, edge(count - 1), shift_up(edge(0)))
            else:
                after = edge(at)
            sums[tile, at] = before + after
        return sums[tile, at]

    def level_zero(tile, p):
        above, below = quarter_sum(tile, p // 2), quarter_sum(tile, p // 2 + 1)
        at = (place_ref[tile, p], weight_ref[tile, p])
        if p % 2 == 0:
            detail = pick(*at, lambda k: (above[k] + below[k]) + up_scr[tile, p // 2, k, :, 0:LANES])
        else:
            detail = 4.0 * pick(*at, lambda k: below[k])
        out_ref[tile, p] = tone_ref[tile, p] - detail

    waiting = [(tile, p) for tile in (1, 0) for p in range(planes)]

    def meanwhile(count):
        for _ in range(min(count, len(waiting))):
            level_zero(*waiting.pop(0))

    def level_one(p):
        return jnp.concatenate([gauss_ref[tile, p // 2, :, p % 2] for tile in range(2)], axis=-1)

    def next_level(coarse, table):
        reduced = rows_down(coarse)
        stacked = jnp.concatenate(reduced, axis=0)
        result = dot(halves(stacked.reshape(-1, stacked.shape[-1])), table)
        result = result.reshape(len(reduced), STACK, SUB, LANES)
        return [result[p] for p in range(len(reduced))]

    def raise_columns(stacks, table):
        stacked = jnp.concatenate(stacks, axis=0)
        result = dot(halves(stacked.reshape(-1, LANES)), table)
        return result.reshape((len(stacks), -1, SUB, table.shape[1]))

    def raise_stack(coarse, table):
        result = raise_columns([plane[FIRST:] for plane in coarse], table)
        return rows_up([result[p] for p in range(len(coarse))])

    def raise_one(planes_of, table):
        result = raise_columns([plane[None] for plane in planes_of], table)
        return rows_up([result[p, 0] for p in range(len(planes_of))])

    def coefficient(level, raised, p):
        here = gauss[level][p]
        return pick(*scaled_level(here[0]), lambda k: here[FIRST + k] - raised[p][k])

    lift = raise_ref[...]
    gauss = [None, [level_one(p) for p in range(planes // 2)]]
    gauss.append(next_level(gauss[1], wide_ref[...]))
    raised = [None, raise_stack(gauss[2], narrow_ref[...])]
    columns_up(1)
    columns_up(0)
    coeffs = [None, []]
    quarter = planes // 8
    for level in range(2, PYR - 1):
        gauss.append(next_level(gauss[level], small_ref[...]))
        coeffs[1] += [coefficient(1, raised[1], p) for p in range(quarter * (level - 2), quarter * (level - 1))]
        raised.append(raise_stack(gauss[level + 1], lift))
    base = raise_one([gauss[PYR - 1][0][0]], lift)
    coeffs[1] += [coefficient(1, raised[1], p) for p in range(3 * quarter, planes // 2)]
    for level in range(2, PYR - 1):
        coeffs.append([coefficient(level, raised[level], p) for p in range(len(gauss[level]))])
    for level in range(PYR - 2, 0, -1):
        out = [one + two for one, two in zip(coeffs[level], base)]
        if level > 1:
            base = raise_one(out, narrow_ref[...] if level == 2 else lift)
        else:
            base = []
            for tile in range(2):
                span = slice(tile * LANES, (tile + 1) * LANES)
                base.append(raise_one([plane[:, span] for plane in out], tables_up[tile][:, 0:LANES]))
        meanwhile(planes // 2)
    meanwhile(2 * planes)
    for tile in range(2):
        for p in range(planes):
            out_ref[tile, p] = out_ref[tile, p] + base[tile][p]


def call(kernel, name, in_specs, out_shape, scratch, out_space=VMEM, **others):
    return pl.pallas_call(
        kernel,
        name=name,
        in_specs=in_specs,
        out_specs=jax.tree.map(lambda _: out_space, out_shape),
        out_shape=out_shape,
        scratch_shapes=scratch,
        compiler_params=PARAMS,
        **others,
    )


def body(image, curves):
    rows, width = image.shape
    planes = rows // SUB
    half = width // 2
    count = lax.axis_size("tile")
    f32 = lambda *shape: jax.ShapeDtypeStruct(shape, jnp.float32)
    b16 = lambda *shape: jax.ShapeDtypeStruct(shape, jnp.bfloat16)
    fast = lambda *shape: pltpu.VMEM(shape, jnp.float32)
    i32 = lambda *shape: jax.ShapeDtypeStruct(shape, jnp.int32)
    fast_int = lambda *shape: pltpu.VMEM(shape, jnp.int32)
    fast_half = lambda *shape: pltpu.VMEM(shape, jnp.bfloat16)
    in_hbm = lambda x: pltpu.with_memory_space_constraint(x, pltpu.HBM)
    swap = [(0, 1), (1, 0)]

    edge, inner, sent, mine, down, rim, wide, small, near, away, narrow, lift = call(
        stage_kernel, "stage", [HBM] * 2,
        [f32(planes, SUB, LANES), f32(2, planes, SUB, LANES), f32(planes * 3 // 4, SUB, LANES), f32(*curves.shape), b16(6 * LANES, half),
         b16(2 * RIM, LANES), b16(2 * half, LANES), b16(2 * LANES, LANES), b16(2 * LANES, half),
         b16(2 * LANES, half), b16(2 * LANES, half), b16(2 * LANES, LANES)],
        [pltpu.SemaphoreType.DMA((3 * SUB + 1,))],
    )(in_hbm(image), in_hbm(curves))
    pairs = []
    for tile in range(count):
        pairs.append((2 * tile + 1, 2 * ((tile + 1) % count)))
        pairs.append((2 * tile, 2 * ((tile - 1) % count) + 1))

    gauss_shape = f32(2, planes // 4, STACK, 2, SUB, LANES)
    out_shape = f32(2, planes, SUB, LANES)
    last_shape = b16(2, planes // 4, 2 * SUB, 6 * LANES)
    table_shape = f32(LEVELS, TABLES, SUB, LANES)
    strip = (3, planes, SUB, LANES)
    part = [fast_half(2, *last_shape.shape)]
    own_shapes = [gauss_shape, last_shape, out_shape, out_shape, table_shape, i32(*strip), f32(*strip)]
    begun = call(early_kernel, "early", [VMEM] * 4, own_shapes, part)(edge, inner, mine, down)
    sent, mine, begun = lax.optimization_barrier((sent, mine, begun))
    halo = lax.ppermute(sent, ("tile", "lvl"), pairs)
    other_curves = lax.ppermute(mine, "lvl", swap)
    gauss, last, place, weight, tables, cells, fractions = call(
        late_kernel, "late", [VMEM] * 11, own_shapes, part,
        input_output_aliases={4 + at: at for at in range(7)},
    )(edge, inner, mine, down, *begun)
    gauss, tables, last, toned = call(
        other_kernel, "other", [VMEM] * 10, [gauss_shape, table_shape, last_shape, out_shape], part,
        input_output_aliases={8: 0, 9: 1},
    )(edge, inner, mine, other_curves, down, cells, fractions, last, gauss, tables)
    mine, _ = call(
        rest_kernel, "rest", [VMEM] * 15, [out_shape, gauss_shape],
        [fast_int(planes, SUB, RIM), fast(planes, SUB, RIM),
         fast_half(2, 2, planes // 4, 2 * SUB, 2 * RIM), fast(2, planes // 2, LEVELS, SUB, half)],
        input_output_aliases={1: 1},
    )(halo, gauss, last, toned, place, weight, tables, down, rim, wide, small, near, away, narrow, lift)
    theirs = lax.ppermute(mine, "lvl", swap)
    sems = [pltpu.SemaphoreType.DMA((2 * SUB,))]
    begun = call(put_mine_kernel, "put_mine", [VMEM], f32(rows, width), sems, HBM)(mine)
    return call(
        put_theirs_kernel, "put_theirs", [VMEM, HBM], f32(rows, width), sems, HBM, input_output_aliases={1: 0}
    )(theirs, begun)


def solution(mesh):
    placed = (P("band", "tile"), P("lvl", None))
    return jax.shard_map(
        body, mesh=mesh, in_specs=placed, out_specs=P("band", "tile"), check_vma=False
    )
```

```python
import functools

import jax
import jax.numpy as jnp
from jax import lax
from jax.experimental import pallas as pl
from jax.experimental.pallas import tpu as pltpu
from jax.sharding import PartitionSpec as P

LEVELS = 16
KNOTS = 17
PYR = 6

SUB = 8
LANES = 128
PIECE = LANES // 4
RIM = LANES
FIRST = 2
STACK = FIRST + LEVELS
LEFT, RIGHT = 2, 126
FINE = (LEVELS - 1) * (KNOTS - 1) // 2
TABLES = 11

VMEM = pl.BlockSpec(memory_space=pltpu.VMEM)
HBM = pl.BlockSpec(memory_space=pltpu.HBM)
PARAMS = pltpu.CompilerParams(vmem_limit_bytes=20 * 1024 * 1024)


def iota(shape, dim):
    return lax.broadcasted_iota(jnp.int32, shape, dim)


def down_taps(distance):
    size = jnp.abs(distance)
    value = jnp.where(size == 0, 6.0, jnp.where(size == 1, 4.0, jnp.where(size == 2, 1.0, 0.0)))
    return (value / 256.0).astype(jnp.bfloat16)


def up_taps(distance):
    size = jnp.abs(distance)
    value = jnp.where(size == 0, 0.75, jnp.where(size == 1, 0.5, jnp.where(size == 2, 0.125, 0.0)))
    return (value / 2.0).astype(jnp.bfloat16)


def halves(x):
    high = x.astype(jnp.bfloat16)
    low = (x - high.astype(jnp.float32)).astype(jnp.bfloat16)
    return jnp.concatenate([high, low], axis=-1)


def dot(x, table):
    return jnp.dot(x, table, preferred_element_type=jnp.float32)


def shift_down(x):
    return pltpu.roll(x, 1, axis=x.ndim - 2)


def shift_up(x):
    return pltpu.roll(x, SUB - 1, axis=x.ndim - 2)


def sublane(x):
    return iota(x.shape, x.ndim - 2)


def rows_down(planes, scaled=False):
    first, last = planes[0], planes[-1]
    top = sublane(first) == 0
    quad = (lambda x: x) if scaled else (lambda x: 4.0 * x)
    minus2 = jnp.where(top, first, shift_down(planes[-2]))
    minus1 = jnp.where(top, 4.0 * first if scaled else first, shift_down(last))
    plus = jnp.where(sublane(first) == SUB - 1, 0.25 * last if scaled else last, shift_up(first))
    padded = [minus2, minus1] + list(planes) + [plus]
    out = []
    for at in range(0, len(planes), 2):
        a, b, c, d, e = padded[at:at + 5]
        out.append((a + e) + quad(b + d) + 6.0 * c)
    return out


def padded_for_up(planes):
    first, last = planes[0], planes[-1]
    below = jnp.where(sublane(first) == 0, first, shift_down(last))
    above = jnp.where(sublane(first) == SUB - 1, last, shift_up(first))
    return [below] + list(planes) + [above]


def rows_up(planes):
    padded = padded_for_up(planes)
    sums = [one + two for one, two in zip(padded[:-1], padded[1:])]
    out = []
    for at in range(len(planes)):
        out.append(0.25 * (sums[at] + sums[at + 1]) + planes[at])
        out.append(sums[at + 1])
    return out


def gather_along(dim):
    return lax.GatherDimensionNumbers(
        offset_dims=(),
        collapsed_slice_dims=(dim,),
        start_index_map=(dim,),
        operand_batching_dims=(1 - dim,),
        start_indices_batching_dims=(1 - dim,),
    )


def look_up(table, index, dim=0):
    return lax.gather(
        table, index[..., None], gather_along(dim), (1, 1), mode=lax.GatherScatterMode.PROMISE_IN_BOUNDS
    )


def cell(x, cells):
    scaled = x * float(cells)
    index = jnp.minimum(jnp.floor(scaled), float(cells - 1))
    return index.astype(jnp.int32), scaled - index


def by_lane(p):
    return p % 4 == 2


def curve_cell(p, x):
    return cell(x, FINE if by_lane(p) else (KNOTS - 1) // 2)


def curve_tables(curve_row, k):
    steps = (KNOTS - 1) // 2
    turn = lax.div(steps * k, LEVELS - 1)
    phase = (steps * k - (LEVELS - 1) * turn).astype(jnp.float32) / (LEVELS - 1)
    width = curve_row.shape[-1]
    row = jnp.broadcast_to(curve_row, (SUB, width))
    offset = iota((SUB, width), 1) - iota((SUB, width), 0)

    def node(shift):
        at = jnp.where(offset == steps - turn + shift, row, 0.0)
        return jnp.sum(at, axis=1, keepdims=True)

    left, middle, right = node(-1), node(0), node(1)
    slope = middle - left
    bend = (right - middle) - slope
    start = (k.astype(jnp.float32) / (LEVELS - 1) + middle) - phase * slope - phase * bend
    spread = lambda v: jnp.broadcast_to(v, (SUB, LANES))
    coarse = (spread(start), spread(slope), spread(bend))
    phase = spread(phase)

    lane = iota((SUB, LANES), 1)
    index = jnp.minimum(jnp.floor((lane.astype(jnp.float32) + 0.5) / (LEVELS - 1)), float(SUB - 1))
    index = index.astype(jnp.int32)
    within = (lane - (LEVELS - 1) * index).astype(jnp.float32)
    ends = [remap(coarse + (phase,), index, (within + side) / (LEVELS - 1)) for side in (0.0, 1.0)]
    fine = (ends[0], ends[1] - ends[0])
    return (phase,) + coarse + fine + tuple(4.0 * table for table in coarse + fine)


def remap(tables, index, rest):
    start, slope, bend, phase = tables
    bent = jnp.maximum(rest, phase)
    return look_up(start, index) + look_up(slope, index) * rest + look_up(bend, index) * bent


def remap_pair(table_ref, first, planes, index_of, rest_of):
    tables = [[table_ref[first + copy, kind] for kind in range(TABLES)] for copy in range(2)]
    mapped = [[], []]
    for p in range(planes):
        index, rest = index_of(p), rest_of(p)
        at = 6 if p % 2 else 1
        for copy in range(2):
            phase, (start, slope, bend, value, step) = tables[copy][0], tables[copy][at:at + 5]
            if by_lane(p):
                result = look_up(value, index, 1) + look_up(step, index, 1) * rest
            else:
                result = remap((start, slope, bend, phase), index, rest)
            mapped[copy].append(result)
    return mapped


def tone_tables(low, high):
    middle = (KNOTS - 1) // 2
    scale = middle / (LEVELS - 1)
    spread = lambda v: jnp.broadcast_to(v, (SUB, LANES))
    sub = iota((SUB, LANES), 0)

    def parts(curves, k):
        level = (sub + k).astype(jnp.float32) / (LEVELS - 1)
        left, centre, right = [spread(curves[:, at:at + 1]) for at in (middle - 1, middle, middle + 1)]
        return level + centre, scale * (right - centre), scale * (centre - left)

    def following(x, then):
        return jnp.where(sub == SUB - 1, spread(then[0:1, :]), shift_up(x))

    one, two = parts(low, 0), parts(high, LEVELS // 2)
    lane = iota((SUB, LANES), 1)
    tables = []
    for kind in range(3):
        rows = []
        for here, then in ((one, two), (two, two)):
            if kind == 0:
                rows.append(here[0])
            elif kind == 1:
                rows.append(following(here[0], then[0]) - here[0])
            else:
                rows.append(here[1] - following(here[2], then[2]))
        along = jnp.where(lane == sub, rows[0], jnp.where(lane == sub + SUB, rows[1], 0.0))
        tables.append(spread(jnp.sum(along, axis=0, keepdims=True)))
    return tables


def tone(tables, x):
    index, rest = cell(x, LEVELS - 1)
    base, step, arc = [look_up(table, index, 1) for table in tables]
    return base + rest * (step + (1.0 - rest) * arc)


def scaled_level(x):
    place = x * float(LEVELS - 1)
    half = 0.5 * place
    return place, jnp.abs(1.0 - 2.0 * (half - jnp.floor(half)))


def start_all(pairs, sems):
    copies = [pltpu.make_async_copy(one, two, sems.at[at]) for at, (one, two) in enumerate(pairs)]
    for copy in copies:
        copy.start()
    return copies


def wait_all(copies):
    for copy in copies:
        copy.wait()


def kept_lanes(lvl):
    lane = iota((SUB, LANES), 1)
    return (lane >= PIECE * lvl) & (lane < LANES - PIECE * (1 - lvl))


def unpack(sent, lvl):
    lane = iota((SUB, LANES), 1)
    planes = []
    for group in range(len(sent) // 3):
        three = sent[3 * group:3 * group + 3]
        one, two, three_on = [pltpu.roll(x, PIECE * (at + 1), axis=1) for at, x in enumerate(three)]
        later = jnp.where(lane < PIECE * (2 + lvl), two, three_on)
        planes += three + [jnp.where(lane < PIECE * (1 + lvl), one, later)]
    return planes


def near_column(lvl, lane):
    return lane + jnp.where(lvl == 0, LEFT, RIGHT)


def away_column(lvl, lane):
    return lane + jnp.where(lvl == 0, RIGHT, LEFT)


def level_one_column(lvl, at):
    return jnp.where(at < LANES, near_column(lvl, at), away_column(lvl, at - LANES))


def stage_kernel(image_ref, curves_ref, edge_ref, inner_ref, sent_ref, mine_ref, own_ref, rim_ref, wide_ref,
                 small_ref, near_ref, away_ref, narrow_ref, raise_ref, sems):
    lvl = lax.axis_index("lvl")
    planes = edge_ref.shape[0]
    half = 2 * LANES
    outermost = pl.multiple_of(lvl * 3 * LANES, LANES)
    rows = [pl.ds(q * planes, planes) for q in range(SUB)]
    pairs = [(image_ref.at[rows[q], pl.ds(outermost, LANES)], edge_ref.at[:, q, :]) for q in range(SUB)]
    pairs.append((curves_ref, mine_ref))
    for tile in range(2):
        columns = slice((tile + 1) * LANES, (tile + 2) * LANES)
        pairs += [(image_ref.at[rows[q], columns], inner_ref.at[tile, :, q, :]) for q in range(SUB)]
    copies = start_all(pairs, sems)

    def put(ref, shape, value):
        table = value(iota(shape, 0), iota(shape, 1))
        ref[0:shape[0], :] = table
        ref[shape[0]:2 * shape[0], :] = table

    def place(i):
        tile = i // LANES
        return jnp.where(lvl == 0, i, i - 2 * tile * LANES + LANES)

    def rim_place(i):
        return i + jnp.where(lvl == 0, -RIM, half)

    def out_place(far, j):
        return j + jnp.where(lvl == far, 0, LANES)

    def wide(i, j):
        column = level_one_column(lvl, i)
        left = (i < LANES) == (lvl == 0)
        return jnp.where(left == (j < LANES // 2), down_taps(column - 2 * j), 0.0)

    def up_pair(column, far):
        def value(i, j):
            lane = j & (LANES - 1)
            taps = up_taps(2 * column(lvl, i) - (out_place(far, lane) + RIM))
            return jnp.where(j < LANES, taps, 0.25 * taps)
        return value

    put(own_ref, (3 * LANES, half),
        lambda i, j: down_taps(place(i) - 2 * (level_one_column(lvl, j) - RIM // 2)))
    put(rim_ref, (RIM, LANES), lambda i, j: down_taps(rim_place(i) - 2 * (near_column(lvl, j) - RIM // 2)))
    put(wide_ref, (half, LANES), wide)
    put(small_ref, (LANES, LANES), lambda i, j: down_taps(i - 2 * j))
    put(near_ref, (LANES, half), up_pair(near_column, 0))
    put(away_ref, (LANES, half), up_pair(away_column, 1))
    put(narrow_ref, (LANES, half), lambda i, j: up_taps(2 * i - level_one_column(lvl, j)))
    put(raise_ref, (LANES, LANES), lambda i, j: up_taps(2 * i - j))
    wait_all(copies[:SUB])
    kept = kept_lanes(lvl)
    for group in range(planes // 4):
        *three, fourth = [edge_ref[4 * group + at] for at in range(4)]
        for at, x in enumerate(three):
            sent_ref[3 * group + at] = jnp.where(kept, x, pltpu.roll(fourth, LANES - PIECE * (at + 1), axis=1))
    wait_all(copies[SUB:])


def put_kernel(half_ref, out_ref, sems, lvl):
    planes = half_ref.shape[1]
    pairs = []
    for tile, at in enumerate((3 * lvl, 1 + lvl)):
        columns = pl.ds(pl.multiple_of(at * LANES, LANES), LANES)
        for q in range(SUB):
            pairs.append((half_ref.at[tile, :, q, :], out_ref.at[pl.ds(q * planes, planes), columns]))
    wait_all(start_all(pairs, sems))


def put_mine_kernel(mine_ref, out_ref, sems):
    put_kernel(mine_ref, out_ref, sems, lax.axis_index("lvl"))


def put_theirs_kernel(theirs_ref, begun_ref, out_ref, sems):
    put_kernel(theirs_ref, out_ref, sems, 1 - lax.axis_index("lvl"))


def pick(place, weight, values):
    even, odd = values(0), values(1)
    for k in range(2, LEVELS, 2):
        even = jnp.where(place >= float(k - 1), values(k), even)
        odd = jnp.where(place >= float(k), values(k + 1), odd)
    return odd + weight * (even - odd)


def split_store(ref, reduced, column, width):
    for pair in range(len(reduced) // 2):
        both = jnp.concatenate(reduced[2 * pair:2 * pair + 2], axis=0)
        high = both.astype(jnp.bfloat16)
        low = (both - high.astype(jnp.float32)).astype(jnp.bfloat16)
        ref[pair, :, column:column + LANES] = high
        ref[pair, :, width + column:width + column + LANES] = low


def scale_odd(planes):
    return [4.0 * x if p % 2 else x for p, x in enumerate(planes)]


def all_tables(table_ref, curves_ref, first):
    for row in range(LEVELS // 2):
        for kind, table in enumerate(curve_tables(curves_ref[row:row + 1, :], first + row)):
            table_ref[first + row, kind] = table


def image_of(edge_ref, inner_ref, tile, p):
    lvl = lax.axis_index("lvl")
    return edge_ref[p] if tile == 0 else inner_ref[lvl if tile == 1 else 1 - lvl, p]


def multiply_own(part_ref, down_ref, gauss_ref, target):
    part = part_ref[...].reshape(-1, 6 * LANES)
    result = dot(part, down_ref[...]).reshape(2, part_ref.shape[1], 2, SUB, 2 * LANES)
    for copy in range(2):
        for tile in range(2):
            span = slice(tile * LANES, (tile + 1) * LANES)
            gauss_ref[tile, :, target + copy] = result[copy, :, :, :, span]


def own_pairs(table_ref, first, cell_ref, fraction_ref, down_ref, gauss_ref, last_ref, part_scr, before):
    planes = cell_ref.shape[1]
    pairs = LEVELS // 4
    waiting = before
    for step in range(pairs):
        multiply_own(waiting[0], down_ref, gauss_ref, waiting[1])
        ref = last_ref if step == pairs - 1 else part_scr.at[step % 2]
        for tile in range(3):
            mapped = remap_pair(
                table_ref, first + 2 * step, planes, lambda p: cell_ref[tile, p], lambda p: fraction_ref[tile, p]
            )
            for copy in range(2):
                split_store(ref.at[copy], rows_down(mapped[copy], scaled=True), tile * LANES, 3 * LANES)
        waiting = (ref, FIRST + first + 2 * step)


def waits_longest():
    foremost = (lax.axis_index("band") == 0) | (lax.axis_index("lvl") == 1)
    return (lax.axis_index("tile") == 0) & foremost


def early_kernel(*refs):
    @pl.when(waits_longest())
    def _():
        mine_part(*refs)


def late_kernel(*refs):
    @pl.when(jnp.logical_not(waits_longest()))
    def _():
        mine_part(*refs[:4], *refs[11:])


def mine_part(edge_ref, inner_ref, mine_ref, down_ref, gauss_ref, last_ref, place_ref, weight_ref,
                table_ref, cell_ref, fraction_ref, part_scr):
    planes = edge_ref.shape[0]
    first = lax.axis_index("lvl") * (LEVELS // 2)
    all_tables(table_ref, mine_ref, first)
    image = functools.partial(image_of, edge_ref, inner_ref)
    for tile in range(3):
        for p in range(planes):
            x = image(tile, p)
            cell_ref[tile, p], fraction_ref[tile, p] = curve_cell(p, x)
            if tile < 2:
                place_ref[tile, p], weight_ref[tile, p] = scaled_level(x)
        reduced = rows_down(scale_odd([image(tile, p) for p in range(planes)]), scaled=True)
        for copy in range(2):
            split_store(part_scr.at[1, copy], reduced, tile * LANES, 3 * LANES)
    before = (part_scr.at[1], 0)
    own_pairs(table_ref, first, cell_ref, fraction_ref, down_ref, gauss_ref, last_ref, part_scr, before)


def other_kernel(edge_ref, inner_ref, mine_ref, other_ref, down_ref, cell_ref, fraction_ref, last_in_ref,
                 gauss_in_ref, table_in_ref, gauss_ref, table_ref, last_ref, tone_ref, part_scr):
    lvl = lax.axis_index("lvl")
    first = (1 - lvl) * (LEVELS // 2)
    all_tables(table_ref, other_ref, first)
    low = jnp.where(lvl == 0, mine_ref[...], other_ref[...])
    high = jnp.where(lvl == 0, other_ref[...], mine_ref[...])
    tones = tone_tables(low, high)
    for tile in range(2):
        for p in range(edge_ref.shape[0]):
            tone_ref[tile, p] = tone(tones, image_of(edge_ref, inner_ref, tile, p))
    before = (last_in_ref, FIRST + lvl * (LEVELS // 2) + LEVELS // 2 - 2)
    own_pairs(table_ref, first, cell_ref, fraction_ref, down_ref, gauss_ref, last_ref, part_scr, before)


def rest_kernel(halo_ref, gauss_in_ref, last_ref, tone_ref, place_ref, weight_ref, table_ref, down_ref,
                rim_ref, wide_ref, small_ref, near_ref, away_ref, narrow_ref, raise_ref, out_ref, gauss_ref,
                cell_scr, rest_scr, part_scr, up_scr):
    lvl = lax.axis_index("lvl")
    halo = unpack([halo_ref[at] for at in range(halo_ref.shape[0])], 1 - lvl)
    planes = len(halo)
    half = 2 * LANES
    pairs = LEVELS // 2

    multiply_own(last_ref, down_ref, gauss_ref, FIRST + (1 - lvl) * (LEVELS // 2) + LEVELS // 2 - 2)

    def columns_up(tile):
        source = jnp.concatenate([gauss_ref[tile, p // 2, FIRST:, p % 2] for p in range(planes // 2)], axis=0)
        result = dot(halves(source.reshape(-1, LANES)), tables_up[tile][...])
        up_scr[tile] = result.reshape(planes // 2, LEVELS, SUB, half)

    tables_up = (near_ref, away_ref)
    for p in range(planes):
        cell_scr[p], rest_scr[p] = curve_cell(p, halo[p])

    def multiply(slot, target):
        part = part_scr[slot].reshape(-1, 2 * RIM)
        result = dot(part, rim_ref[...]).reshape(2, planes // 4, 2, SUB, LANES)
        for copy in range(2):
            gauss_ref[0, :, target + copy] = gauss_ref[0, :, target + copy] + result[copy]

    reduced = rows_down(scale_odd(halo), scaled=True)
    for copy in range(2):
        split_store(part_scr.at[1, copy], reduced, 0, RIM)
    for step in range(pairs):
        slot = step % 2
        multiply(1 - slot, 2 * step)
        mapped = remap_pair(table_ref, 2 * step, planes, lambda p: cell_scr[p], lambda p: rest_scr[p])
        for copy in range(2):
            split_store(part_scr.at[slot, copy], rows_down(mapped[copy], scaled=True), 0, RIM)
    multiply((pairs - 1) % 2, 2 * pairs)

    sums = {}

    def quarter_sum(tile, at):
        if (tile, at) not in sums:
            count = planes // 2
            edge = lambda p: up_scr[tile, p, :, :, LANES:half]
            if at == 0:
                before = jnp.where(sublane(edge(0)) == 0, edge(0), shift_down(edge(count - 1)))
            else:
                before = edge(at - 1)
            if at == count:
                after = jnp.where(sublane(edge(0)) == SUB - 1, edge(count - 1), shift_up(edge(0)))
            else:
                after = edge(at)
            sums[tile, at] = before + after
        return sums[tile, at]

    def level_zero(tile, p):
        above, below = quarter_sum(tile, p // 2), quarter_sum(tile, p // 2 + 1)
        at = (place_ref[tile, p], weight_ref[tile, p])
        if p % 2 == 0:
            detail = pick(*at, lambda k: (above[k] + below[k]) + up_scr[tile, p // 2, k, :, 0:LANES])
        else:
            detail = 4.0 * pick(*at, lambda k: below[k])
        out_ref[tile, p] = tone_ref[tile, p] - detail

    waiting = [(tile, p) for tile in (1, 0) for p in range(planes)]

    def meanwhile(count):
        for _ in range(min(count, len(waiting))):
            level_zero(*waiting.pop(0))

    def level_one(p):
        return jnp.concatenate([gauss_ref[tile, p // 2, :, p % 2] for tile in range(2)], axis=-1)

    def next_level(coarse, table):
        reduced = rows_down(coarse)
        stacked = jnp.concatenate(reduced, axis=0)
        result = dot(halves(stacked.reshape(-1, stacked.shape[-1])), table)
        result = result.reshape(len(reduced), STACK, SUB, LANES)
        return [result[p] for p in range(len(reduced))]

    def raise_columns(stacks, table):
        stacked = jnp.concatenate(stacks, axis=0)
        result = dot(halves(stacked.reshape(-1, LANES)), table)
        return result.reshape((len(stacks), -1, SUB, table.shape[1]))

    def raise_stack(coarse, table):
        result = raise_columns([plane[FIRST:] for plane in coarse], table)
        return rows_up([result[p] for p in range(len(coarse))])

    def raise_one(planes_of, table):
        result = raise_columns([plane[None] for plane in planes_of], table)
        return rows_up([result[p, 0] for p in range(len(planes_of))])

    def coefficient(level, raised, p):
        here = gauss[level][p]
        return pick(*scaled_level(here[0]), lambda k: here[FIRST + k] - raised[p][k])

    columns_up(1)
    lift = raise_ref[...]
    gauss = [None, [level_one(p) for p in range(planes // 2)]]
    gauss.append(next_level(gauss[1], wide_ref[...]))
    raised = [None, raise_stack(gauss[2], narrow_ref[...])]
    columns_up(0)
    coeffs = [None, []]
    quarter = planes // 8
    for level in range(2, PYR - 1):
        gauss.append(next_level(gauss[level], small_ref[...]))
        coeffs[1] += [coefficient(1, raised[1], p) for p in range(quarter * (level - 2), quarter * (level - 1))]
        raised.append(raise_stack(gauss[level + 1], lift))
    base = raise_one([gauss[PYR - 1][0][0]], lift)
    coeffs[1] += [coefficient(1, raised[1], p) for p in range(3 * quarter, planes // 2)]
    for level in range(2, PYR - 1):
        coeffs.append([coefficient(level, raised[level], p) for p in range(len(gauss[level]))])
    for level in range(PYR - 2, 0, -1):
        out = [one + two for one, two in zip(coeffs[level], base)]
        if level > 1:
            base = raise_one(out, narrow_ref[...] if level == 2 else lift)
        else:
            base = []
            for tile in range(2):
                span = slice(tile * LANES, (tile + 1) * LANES)
                base.append(raise_one([plane[:, span] for plane in out], tables_up[tile][:, 0:LANES]))
        meanwhile(planes // 2)
    meanwhile(2 * planes)
    for tile in range(2):
        for p in range(planes):
            out_ref[tile, p] = out_ref[tile, p] + base[tile][p]


def call(kernel, name, in_specs, out_shape, scratch, out_space=VMEM, **others):
    return pl.pallas_call(
        kernel,
        name=name,
        in_specs=in_specs,
        out_specs=jax.tree.map(lambda _: out_space, out_shape),
        out_shape=out_shape,
        scratch_shapes=scratch,
        compiler_params=PARAMS,
        **others,
    )


def body(image, curves):
    rows, width = image.shape
    planes = rows // SUB
    half = width // 2
    count = lax.axis_size("tile")
    f32 = lambda *shape: jax.ShapeDtypeStruct(shape, jnp.float32)
    b16 = lambda *shape: jax.ShapeDtypeStruct(shape, jnp.bfloat16)
    fast = lambda *shape: pltpu.VMEM(shape, jnp.float32)
    i32 = lambda *shape: jax.ShapeDtypeStruct(shape, jnp.int32)
    fast_int = lambda *shape: pltpu.VMEM(shape, jnp.int32)
    fast_half = lambda *shape: pltpu.VMEM(shape, jnp.bfloat16)
    in_hbm = lambda x: pltpu.with_memory_space_constraint(x, pltpu.HBM)
    swap = [(0, 1), (1, 0)]

    edge, inner, sent, mine, down, rim, wide, small, near, away, narrow, lift = call(
        stage_kernel, "stage", [HBM] * 2,
        [f32(planes, SUB, LANES), f32(2, planes, SUB, LANES), f32(planes * 3 // 4, SUB, LANES), f32(*curves.shape), b16(6 * LANES, half),
         b16(2 * RIM, LANES), b16(2 * half, LANES), b16(2 * LANES, LANES), b16(2 * LANES, half),
         b16(2 * LANES, half), b16(2 * LANES, half), b16(2 * LANES, LANES)],
        [pltpu.SemaphoreType.DMA((3 * SUB + 1,))],
    )(in_hbm(image), in_hbm(curves))
    pairs = []
    for tile in range(count):
        pairs.append((2 * tile + 1, 2 * ((tile + 1) % count)))
        pairs.append((2 * tile, 2 * ((tile - 1) % count) + 1))

    gauss_shape = f32(2, planes // 4, STACK, 2, SUB, LANES)
    out_shape = f32(2, planes, SUB, LANES)
    last_shape = b16(2, planes // 4, 2 * SUB, 6 * LANES)
    table_shape = f32(LEVELS, TABLES, SUB, LANES)
    strip = (3, planes, SUB, LANES)
    part = [fast_half(2, *last_shape.shape)]
    own_shapes = [gauss_shape, last_shape, out_shape, out_shape, table_shape, i32(*strip), f32(*strip)]
    begun = call(early_kernel, "early", [VMEM] * 4, own_shapes, part)(edge, inner, mine, down)
    sent, mine, begun = lax.optimization_barrier((sent, mine, begun))
    halo = lax.ppermute(sent, ("tile", "lvl"), pairs)
    other_curves = lax.ppermute(mine, "lvl", swap)
    gauss, last, place, weight, tables, cells, fractions = call(
        late_kernel, "late", [VMEM] * 11, own_shapes, part,
        input_output_aliases={4 + at: at for at in range(7)},
    )(edge, inner, mine, down, *begun)
    gauss, tables, last, toned = call(
        other_kernel, "other", [VMEM] * 10, [gauss_shape, table_shape, last_shape, out_shape], part,
        input_output_aliases={8: 0, 9: 1},
    )(edge, inner, mine, other_curves, down, cells, fractions, last, gauss, tables)
    mine, _ = call(
        rest_kernel, "rest", [VMEM] * 15, [out_shape, gauss_shape],
        [fast_int(planes, SUB, RIM), fast(planes, SUB, RIM),
         fast_half(2, 2, planes // 4, 2 * SUB, 2 * RIM), fast(2, planes // 2, LEVELS, SUB, half)],
        input_output_aliases={1: 1},
    )(halo, gauss, last, toned, place, weight, tables, down, rim, wide, small, near, away, narrow, lift)
    theirs = lax.ppermute(mine, "lvl", swap)
    sems = [pltpu.SemaphoreType.DMA((2 * SUB,))]
    begun = call(put_mine_kernel, "put_mine", [VMEM], f32(rows, width), sems, HBM)(mine)
    return call(
        put_theirs_kernel, "put_theirs", [VMEM, HBM], f32(rows, width), sems, HBM, input_output_aliases={1: 0}
    )(theirs, begun)


def solution(mesh):
    placed = (P("band", "tile"), P("lvl", None))
    return jax.shard_map(
        body, mesh=mesh, in_specs=placed, out_specs=P("band", "tile"), check_vma=False
    )
```

```python
import functools

import jax
import jax.numpy as jnp
from jax import lax
from jax.experimental import pallas as pl
from jax.experimental.pallas import tpu as pltpu
from jax.sharding import PartitionSpec as P

LEVELS = 16
KNOTS = 17
PYR = 6

SUB = 8
LANES = 128
PIECE = LANES // 4
RIM = LANES
FIRST = 2
STACK = FIRST + LEVELS
LEFT, RIGHT = 2, 126
FINE = (LEVELS - 1) * (KNOTS - 1) // 2
TABLES = 11

VMEM = pl.BlockSpec(memory_space=pltpu.VMEM)
HBM = pl.BlockSpec(memory_space=pltpu.HBM)
PARAMS = pltpu.CompilerParams(vmem_limit_bytes=20 * 1024 * 1024)


def iota(shape, dim):
    return lax.broadcasted_iota(jnp.int32, shape, dim)


def down_taps(distance):
    size = jnp.abs(distance)
    value = jnp.where(size == 0, 6.0, jnp.where(size == 1, 4.0, jnp.where(size == 2, 1.0, 0.0)))
    return (value / 256.0).astype(jnp.bfloat16)


def up_taps(distance):
    size = jnp.abs(distance)
    value = jnp.where(size == 0, 0.75, jnp.where(size == 1, 0.5, jnp.where(size == 2, 0.125, 0.0)))
    return (value / 2.0).astype(jnp.bfloat16)


def halves(x):
    high = x.astype(jnp.bfloat16)
    low = (x - high.astype(jnp.float32)).astype(jnp.bfloat16)
    return jnp.concatenate([high, low], axis=-1)


def dot(x, table):
    return jnp.dot(x, table, preferred_element_type=jnp.float32)


def shift_down(x):
    return pltpu.roll(x, 1, axis=x.ndim - 2)


def shift_up(x):
    return pltpu.roll(x, SUB - 1, axis=x.ndim - 2)


def sublane(x):
    return iota(x.shape, x.ndim - 2)


def rows_down(planes, scaled=False):
    first, last = planes[0], planes[-1]
    top = sublane(first) == 0
    quad = (lambda x: x) if scaled else (lambda x: 4.0 * x)
    minus2 = jnp.where(top, first, shift_down(planes[-2]))
    minus1 = jnp.where(top, 4.0 * first if scaled else first, shift_down(last))
    plus = jnp.where(sublane(first) == SUB - 1, 0.25 * last if scaled else last, shift_up(first))
    padded = [minus2, minus1] + list(planes) + [plus]
    out = []
    for at in range(0, len(planes), 2):
        a, b, c, d, e = padded[at:at + 5]
        out.append((a + e) + quad(b + d) + 6.0 * c)
    return out


def padded_for_up(planes):
    first, last = planes[0], planes[-1]
    below = jnp.where(sublane(first) == 0, first, shift_down(last))
    above = jnp.where(sublane(first) == SUB - 1, last, shift_up(first))
    return [below] + list(planes) + [above]


def rows_up(planes):
    padded = padded_for_up(planes)
    sums = [one + two for one, two in zip(padded[:-1], padded[1:])]
    out = []
    for at in range(len(planes)):
        out.append(0.25 * (sums[at] + sums[at + 1]) + planes[at])
        out.append(sums[at + 1])
    return out


def gather_along(dim):
    return lax.GatherDimensionNumbers(
        offset_dims=(),
        collapsed_slice_dims=(dim,),
        start_index_map=(dim,),
        operand_batching_dims=(1 - dim,),
        start_indices_batching_dims=(1 - dim,),
    )


def look_up(table, index, dim=0):
    return lax.gather(
        table, index[..., None], gather_along(dim), (1, 1), mode=lax.GatherScatterMode.PROMISE_IN_BOUNDS
    )


def cell(x, cells):
    scaled = x * float(cells)
    index = jnp.minimum(jnp.floor(scaled), float(cells - 1))
    return index.astype(jnp.int32), scaled - index


def by_lane(p):
    return p % 4 == 2


def curve_cell(p, x):
    return cell(x, FINE if by_lane(p) else (KNOTS - 1) // 2)


def curve_tables(curve_row, k):
    steps = (KNOTS - 1) // 2
    turn = lax.div(steps * k, LEVELS - 1)
    phase = (steps * k - (LEVELS - 1) * turn).astype(jnp.float32) / (LEVELS - 1)
    width = curve_row.shape[-1]
    row = jnp.broadcast_to(curve_row, (SUB, width))
    offset = iota((SUB, width), 1) - iota((SUB, width), 0)

    def node(shift):
        at = jnp.where(offset == steps - turn + shift, row, 0.0)
        return jnp.sum(at, axis=1, keepdims=True)

    left, middle, right = node(-1), node(0), node(1)
    slope = middle - left
    bend = (right - middle) - slope
    start = (k.astype(jnp.float32) / (LEVELS - 1) + middle) - phase * slope - phase * bend
    spread = lambda v: jnp.broadcast_to(v, (SUB, LANES))
    coarse = (spread(start), spread(slope), spread(bend))
    phase = spread(phase)

    lane = iota((SUB, LANES), 1)
    index = jnp.minimum(jnp.floor((lane.astype(jnp.float32) + 0.5) / (LEVELS - 1)), float(SUB - 1))
    index = index.astype(jnp.int32)
    within = (lane - (LEVELS - 1) * index).astype(jnp.float32)
    ends = [remap(coarse + (phase,), index, (within + side) / (LEVELS - 1)) for side in (0.0, 1.0)]
    fine = (ends[0], ends[1] - ends[0])
    return (phase,) + coarse + fine + tuple(4.0 * table for table in coarse + fine)


def remap(tables, index, rest):
    start, slope, bend, phase = tables
    bent = jnp.maximum(rest, phase)
    return look_up(start, index) + look_up(slope, index) * rest + look_up(bend, index) * bent


def remap_pair(table_ref, first, planes, index_of, rest_of):
    tables = [[table_ref[first + copy, kind] for kind in range(TABLES)] for copy in range(2)]
    mapped = [[], []]
    for p in range(planes):
        index, rest = index_of(p), rest_of(p)
        at = 6 if p % 2 else 1
        for copy in range(2):
            phase, (start, slope, bend, value, step) = tables[copy][0], tables[copy][at:at + 5]
            if by_lane(p):
                result = look_up(value, index, 1) + look_up(step, index, 1) * rest
            else:
                result = remap((start, slope, bend, phase), index, rest)
            mapped[copy].append(result)
    return mapped


def tone_tables(low, high):
    middle = (KNOTS - 1) // 2
    scale = middle / (LEVELS - 1)
    spread = lambda v: jnp.broadcast_to(v, (SUB, LANES))
    sub = iota((SUB, LANES), 0)

    def parts(curves, k):
        level = (sub + k).astype(jnp.float32) / (LEVELS - 1)
        left, centre, right = [spread(curves[:, at:at + 1]) for at in (middle - 1, middle, middle + 1)]
        return level + centre, scale * (right - centre), scale * (centre - left)

    def following(x, then):
        return jnp.where(sub == SUB - 1, spread(then[0:1, :]), shift_up(x))

    one, two = parts(low, 0), parts(high, LEVELS // 2)
    lane = iota((SUB, LANES), 1)
    tables = []
    for kind in range(3):
        rows = []
        for here, then in ((one, two), (two, two)):
            if kind == 0:
                rows.append(here[0])
            elif kind == 1:
                rows.append(following(here[0], then[0]) - here[0])
            else:
                rows.append(here[1] - following(here[2], then[2]))
        along = jnp.where(lane == sub, rows[0], jnp.where(lane == sub + SUB, rows[1], 0.0))
        tables.append(spread(jnp.sum(along, axis=0, keepdims=True)))
    return tables


def tone(tables, x):
    index, rest = cell(x, LEVELS - 1)
    base, step, arc = [look_up(table, index, 1) for table in tables]
    return base + rest * (step + (1.0 - rest) * arc)


def scaled_level(x):
    place = x * float(LEVELS - 1)
    half = 0.5 * place
    return place, jnp.abs(1.0 - 2.0 * (half - jnp.floor(half)))


def start_all(pairs, sems):
    copies = [pltpu.make_async_copy(one, two, sems.at[at]) for at, (one, two) in enumerate(pairs)]
    for copy in copies:
        copy.start()
    return copies


def wait_all(copies):
    for copy in copies:
        copy.wait()


def kept_lanes(lvl):
    lane = iota((SUB, LANES), 1)
    return (lane >= PIECE * lvl) & (lane < LANES - PIECE * (1 - lvl))


def unpack(sent, lvl):
    lane = iota((SUB, LANES), 1)
    planes = []
    for group in range(len(sent) // 3):
        three = sent[3 * group:3 * group + 3]
        one, two, three_on = [pltpu.roll(x, PIECE * (at + 1), axis=1) for at, x in enumerate(three)]
        later = jnp.where(lane < PIECE * (2 + lvl), two, three_on)
        planes += three + [jnp.where(lane < PIECE * (1 + lvl), one, later)]
    return planes


def near_column(lvl, lane):
    return lane + jnp.where(lvl == 0, LEFT, RIGHT)


def away_column(lvl, lane):
    return lane + jnp.where(lvl == 0, RIGHT, LEFT)


def level_one_column(lvl, at):
    return jnp.where(at < LANES, near_column(lvl, at), away_column(lvl, at - LANES))


def stage_kernel(image_ref, curves_ref, edge_ref, inner_ref, sent_ref, mine_ref, own_ref, rim_ref, wide_ref,
                 small_ref, near_ref, away_ref, narrow_ref, raise_ref, sems):
    lvl = lax.axis_index("lvl")
    planes = edge_ref.shape[0]
    half = 2 * LANES
    outermost = pl.multiple_of(lvl * 3 * LANES, LANES)
    rows = [pl.ds(q * planes, planes) for q in range(SUB)]
    pairs = [(image_ref.at[rows[q], pl.ds(outermost, LANES)], edge_ref.at[:, q, :]) for q in range(SUB)]
    pairs.append((curves_ref, mine_ref))
    for tile in range(2):
        columns = slice((tile + 1) * LANES, (tile + 2) * LANES)
        pairs += [(image_ref.at[rows[q], columns], inner_ref.at[tile, :, q, :]) for q in range(SUB)]
    copies = start_all(pairs, sems)

    def put(ref, shape, value):
        table = value(iota(shape, 0), iota(shape, 1))
        ref[0:shape[0], :] = table
        ref[shape[0]:2 * shape[0], :] = table

    def place(i):
        tile = i // LANES
        return jnp.where(lvl == 0, i, i - 2 * tile * LANES + LANES)

    def rim_place(i):
        return i + jnp.where(lvl == 0, -RIM, half)

    def out_place(far, j):
        return j + jnp.where(lvl == far, 0, LANES)

    def wide(i, j):
        column = level_one_column(lvl, i)
        left = (i < LANES) == (lvl == 0)
        return jnp.where(left == (j < LANES // 2), down_taps(column - 2 * j), 0.0)

    def up_pair(column, far):
        def value(i, j):
            lane = j & (LANES - 1)
            taps = up_taps(2 * column(lvl, i) - (out_place(far, lane) + RIM))
            return jnp.where(j < LANES, taps, 0.25 * taps)
        return value

    put(own_ref, (3 * LANES, half),
        lambda i, j: down_taps(place(i) - 2 * (level_one_column(lvl, j) - RIM // 2)))
    put(rim_ref, (RIM, LANES), lambda i, j: down_taps(rim_place(i) - 2 * (near_column(lvl, j) - RIM // 2)))
    put(wide_ref, (half, LANES), wide)
    put(small_ref, (LANES, LANES), lambda i, j: down_taps(i - 2 * j))
    put(near_ref, (LANES, half), up_pair(near_column, 0))
    put(away_ref, (LANES, half), up_pair(away_column, 1))
    put(narrow_ref, (LANES, half), lambda i, j: up_taps(2 * i - level_one_column(lvl, j)))
    put(raise_ref, (LANES, LANES), lambda i, j: up_taps(2 * i - j))
    wait_all(copies[:SUB])
    kept = kept_lanes(lvl)
    for group in range(planes // 4):
        *three, fourth = [edge_ref[4 * group + at] for at in range(4)]
        for at, x in enumerate(three):
            sent_ref[3 * group + at] = jnp.where(kept, x, pltpu.roll(fourth, LANES - PIECE * (at + 1), axis=1))
    wait_all(copies[SUB:])


def put_kernel(half_ref, out_ref, sems, lvl):
    planes = half_ref.shape[1]
    pairs = []
    for tile, at in enumerate((3 * lvl, 1 + lvl)):
        columns = pl.ds(pl.multiple_of(at * LANES, LANES), LANES)
        for q in range(SUB):
            pairs.append((half_ref.at[tile, :, q, :], out_ref.at[pl.ds(q * planes, planes), columns]))
    wait_all(start_all(pairs, sems))


def put_mine_kernel(mine_ref, out_ref, sems):
    put_kernel(mine_ref, out_ref, sems, lax.axis_index("lvl"))


def put_theirs_kernel(theirs_ref, begun_ref, out_ref, sems):
    put_kernel(theirs_ref, out_ref, sems, 1 - lax.axis_index("lvl"))


def pick(place, weight, values):
    even, odd = values(0), values(1)
    for k in range(2, LEVELS, 2):
        even = jnp.where(place >= float(k - 1), values(k), even)
        odd = jnp.where(place >= float(k), values(k + 1), odd)
    return odd + weight * (even - odd)


def split_store(ref, reduced, column, width):
    for pair in range(len(reduced) // 2):
        both = jnp.concatenate(reduced[2 * pair:2 * pair + 2], axis=0)
        high = both.astype(jnp.bfloat16)
        low = (both - high.astype(jnp.float32)).astype(jnp.bfloat16)
        ref[pair, :, column:column + LANES] = high
        ref[pair, :, width + column:width + column + LANES] = low


def scale_odd(planes):
    return [4.0 * x if p % 2 else x for p, x in enumerate(planes)]


def all_tables(table_ref, curves_ref, first):
    for row in range(LEVELS // 2):
        for kind, table in enumerate(curve_tables(curves_ref[row:row + 1, :], first + row)):
            table_ref[first + row, kind] = table


def image_of(edge_ref, inner_ref, tile, p):
    lvl = lax.axis_index("lvl")
    return edge_ref[p] if tile == 0 else inner_ref[lvl if tile == 1 else 1 - lvl, p]


def multiply_own(part_ref, down_ref, gauss_ref, target):
    part = part_ref[...].reshape(-1, 6 * LANES)
    result = dot(part, down_ref[...]).reshape(2, part_ref.shape[1], 2, SUB, 2 * LANES)
    for copy in range(2):
        for tile in range(2):
            span = slice(tile * LANES, (tile + 1) * LANES)
            gauss_ref[tile, :, target + copy] = result[copy, :, :, :, span]


def own_pairs(steps, table_ref, first, cell_ref, fraction_ref, down_ref, gauss_ref, last_ref, part_scr, before):
    planes = cell_ref.shape[1]
    waiting = before
    for step in steps:
        multiply_own(waiting[0], down_ref, gauss_ref, waiting[1])
        ref = last_ref if step == steps[-1] else part_scr.at[step % 2]
        for tile in range(3):
            mapped = remap_pair(
                table_ref, first + 2 * step, planes, lambda p: cell_ref[tile, p], lambda p: fraction_ref[tile, p]
            )
            for copy in range(2):
                split_store(ref.at[copy], rows_down(mapped[copy], scaled=True), tile * LANES, 3 * LANES)
        waiting = (ref, FIRST + first + 2 * step)


def waits_longest():
    foremost = (lax.axis_index("band") == 0) | (lax.axis_index("lvl") == 1)
    return (lax.axis_index("tile") == 0) & foremost


def waits_for_both():
    return waits_longest() & (lax.axis_index("lvl") == 1)


def early_kernel(*refs):
    @pl.when(waits_longest())
    def _():
        mine_begin(*refs)

    @pl.when(waits_for_both())
    def _():
        mine_end(*refs)


def late_kernel(*refs):
    refs = refs[:4] + refs[11:]

    @pl.when(jnp.logical_not(waits_longest()))
    def _():
        mine_begin(*refs)

    @pl.when(jnp.logical_not(waits_for_both()))
    def _():
        mine_end(*refs)


def mine_end(edge_ref, inner_ref, mine_ref, down_ref, gauss_ref, last_ref, place_ref, weight_ref,
             table_ref, cell_ref, fraction_ref, part_scr):
    first = lax.axis_index("lvl") * (LEVELS // 2)
    steps = range(LEVELS // 8, LEVELS // 4)
    before = (last_ref, FIRST + first + 2 * (steps[0] - 1))
    own_pairs(steps, table_ref, first, cell_ref, fraction_ref, down_ref, gauss_ref, last_ref, part_scr, before)


def mine_begin(edge_ref, inner_ref, mine_ref, down_ref, gauss_ref, last_ref, place_ref, weight_ref,
               table_ref, cell_ref, fraction_ref, part_scr):
    planes = edge_ref.shape[0]
    first = lax.axis_index("lvl") * (LEVELS // 2)
    all_tables(table_ref, mine_ref, first)
    image = functools.partial(image_of, edge_ref, inner_ref)
    for tile in range(3):
        for p in range(planes):
            x = image(tile, p)
            cell_ref[tile, p], fraction_ref[tile, p] = curve_cell(p, x)
            if tile < 2:
                place_ref[tile, p], weight_ref[tile, p] = scaled_level(x)
        reduced = rows_down(scale_odd([image(tile, p) for p in range(planes)]), scaled=True)
        for copy in range(2):
            split_store(part_scr.at[1, copy], reduced, tile * LANES, 3 * LANES)
    before = (part_scr.at[1], 0)
    steps = range(LEVELS // 8)
    own_pairs(steps, table_ref, first, cell_ref, fraction_ref, down_ref, gauss_ref, last_ref, part_scr, before)


def other_kernel(edge_ref, inner_ref, mine_ref, other_ref, down_ref, cell_ref, fraction_ref, last_in_ref,
                 gauss_in_ref, table_in_ref, gauss_ref, table_ref, last_ref, tone_ref, part_scr):
    lvl = lax.axis_index("lvl")
    first = (1 - lvl) * (LEVELS // 2)
    all_tables(table_ref, other_ref, first)
    low = jnp.where(lvl == 0, mine_ref[...], other_ref[...])
    high = jnp.where(lvl == 0, other_ref[...], mine_ref[...])
    tones = tone_tables(low, high)
    for tile in range(2):
        for p in range(edge_ref.shape[0]):
            tone_ref[tile, p] = tone(tones, image_of(edge_ref, inner_ref, tile, p))
    before = (last_in_ref, FIRST + lvl * (LEVELS // 2) + LEVELS // 2 - 2)
    steps = range(LEVELS // 4)
    own_pairs(steps, table_ref, first, cell_ref, fraction_ref, down_ref, gauss_ref, last_ref, part_scr, before)


def rest_kernel(halo_ref, gauss_in_ref, last_ref, tone_ref, place_ref, weight_ref, table_ref, down_ref,
                rim_ref, wide_ref, small_ref, near_ref, away_ref, narrow_ref, raise_ref, out_ref, gauss_ref,
                cell_scr, rest_scr, part_scr, up_scr):
    lvl = lax.axis_index("lvl")
    halo = unpack([halo_ref[at] for at in range(halo_ref.shape[0])], 1 - lvl)
    planes = len(halo)
    half = 2 * LANES
    pairs = LEVELS // 2

    multiply_own(last_ref, down_ref, gauss_ref, FIRST + (1 - lvl) * (LEVELS // 2) + LEVELS // 2 - 2)

    def columns_up(tile):
        source = jnp.concatenate([gauss_ref[tile, p // 2, FIRST:, p % 2] for p in range(planes // 2)], axis=0)
        result = dot(halves(source.reshape(-1, LANES)), tables_up[tile][...])
        up_scr[tile] = result.reshape(planes // 2, LEVELS, SUB, half)

    tables_up = (near_ref, away_ref)
    for p in range(planes):
        cell_scr[p], rest_scr[p] = curve_cell(p, halo[p])

    def multiply(slot, target):
        part = part_scr[slot].reshape(-1, 2 * RIM)
        result = dot(part, rim_ref[...]).reshape(2, planes // 4, 2, SUB, LANES)
        for copy in range(2):
            gauss_ref[0, :, target + copy] = gauss_ref[0, :, target + copy] + result[copy]

    reduced = rows_down(scale_odd(halo), scaled=True)
    for copy in range(2):
        split_store(part_scr.at[1, copy], reduced, 0, RIM)
    for step in range(pairs):
        slot = step % 2
        multiply(1 - slot, 2 * step)
        mapped = remap_pair(table_ref, 2 * step, planes, lambda p: cell_scr[p], lambda p: rest_scr[p])
        for copy in range(2):
            split_store(part_scr.at[slot, copy], rows_down(mapped[copy], scaled=True), 0, RIM)
    multiply((pairs - 1) % 2, 2 * pairs)

    sums = {}

    def quarter_sum(tile, at):
        if (tile, at) not in sums:
            count = planes // 2
            edge = lambda p: up_scr[tile, p, :, :, LANES:half]
            if at == 0:
                before = jnp.where(sublane(edge(0)) == 0, edge(0), shift_down(edge(count - 1)))
            else:
                before = edge(at - 1)
            if at == count:
                after = jnp.where(sublane(edge(0)) == SUB - 1, edge(count - 1), shift_up(edge(0)))
            else:
                after = edge(at)
            sums[tile, at] = before + after
        return sums[tile, at]

    def level_zero(tile, p):
        above, below = quarter_sum(tile, p // 2), quarter_sum(tile, p // 2 + 1)
        at = (place_ref[tile, p], weight_ref[tile, p])
        if p % 2 == 0:
            detail = pick(*at, lambda k: (above[k] + below[k]) + up_scr[tile, p // 2, k, :, 0:LANES])
        else:
            detail = 4.0 * pick(*at, lambda k: below[k])
        out_ref[tile, p] = tone_ref[tile, p] - detail

    waiting = [(tile, p) for tile in (1, 0) for p in range(planes)]

    def meanwhile(count):
        for _ in range(min(count, len(waiting))):
            level_zero(*waiting.pop(0))

    def level_one(p):
        return jnp.concatenate([gauss_ref[tile, p // 2, :, p % 2] for tile in range(2)], axis=-1)

    def next_level(coarse, table):
        reduced = rows_down(coarse)
        stacked = jnp.concatenate(reduced, axis=0)
        result = dot(halves(stacked.reshape(-1, stacked.shape[-1])), table)
        result = result.reshape(len(reduced), STACK, SUB, LANES)
        return [result[p] for p in range(len(reduced))]

    def raise_columns(stacks, table):
        stacked = jnp.concatenate(stacks, axis=0)
        result = dot(halves(stacked.reshape(-1, LANES)), table)
        return result.reshape((len(stacks), -1, SUB, table.shape[1]))

    def raise_stack(coarse, table):
        result = raise_columns([plane[FIRST:] for plane in coarse], table)
        return rows_up([result[p] for p in range(len(coarse))])

    def raise_one(planes_of, table):
        result = raise_columns([plane[None] for plane in planes_of], table)
        return rows_up([result[p, 0] for p in range(len(planes_of))])

    def coefficient(level, raised, p):
        here = gauss[level][p]
        return pick(*scaled_level(here[0]), lambda k: here[FIRST + k] - raised[p][k])

    columns_up(1)
    lift = raise_ref[...]
    gauss = [None, [level_one(p) for p in range(planes // 2)]]
    gauss.append(next_level(gauss[1], wide_ref[...]))
    raised = [None, raise_stack(gauss[2], narrow_ref[...])]
    columns_up(0)
    coeffs = [None, []]
    quarter = planes // 8
    for level in range(2, PYR - 1):
        gauss.append(next_level(gauss[level], small_ref[...]))
        coeffs[1] += [coefficient(1, raised[1], p) for p in range(quarter * (level - 2), quarter * (level - 1))]
        raised.append(raise_stack(gauss[level + 1], lift))
    base = raise_one([gauss[PYR - 1][0][0]], lift)
    coeffs[1] += [coefficient(1, raised[1], p) for p in range(3 * quarter, planes // 2)]
    for level in range(2, PYR - 1):
        coeffs.append([coefficient(level, raised[level], p) for p in range(len(gauss[level]))])
    for level in range(PYR - 2, 0, -1):
        out = [one + two for one, two in zip(coeffs[level], base)]
        if level > 1:
            base = raise_one(out, narrow_ref[...] if level == 2 else lift)
        else:
            base = []
            for tile in range(2):
                span = slice(tile * LANES, (tile + 1) * LANES)
                base.append(raise_one([plane[:, span] for plane in out], tables_up[tile][:, 0:LANES]))
        meanwhile(planes // 2)
    meanwhile(2 * planes)
    for tile in range(2):
        for p in range(planes):
            out_ref[tile, p] = out_ref[tile, p] + base[tile][p]


def call(kernel, name, in_specs, out_shape, scratch, out_space=VMEM, **others):
    return pl.pallas_call(
        kernel,
        name=name,
        in_specs=in_specs,
        out_specs=jax.tree.map(lambda _: out_space, out_shape),
        out_shape=out_shape,
        scratch_shapes=scratch,
        compiler_params=PARAMS,
        **others,
    )


def body(image, curves):
    rows, width = image.shape
    planes = rows // SUB
    half = width // 2
    count = lax.axis_size("tile")
    f32 = lambda *shape: jax.ShapeDtypeStruct(shape, jnp.float32)
    b16 = lambda *shape: jax.ShapeDtypeStruct(shape, jnp.bfloat16)
    fast = lambda *shape: pltpu.VMEM(shape, jnp.float32)
    i32 = lambda *shape: jax.ShapeDtypeStruct(shape, jnp.int32)
    fast_int = lambda *shape: pltpu.VMEM(shape, jnp.int32)
    fast_half = lambda *shape: pltpu.VMEM(shape, jnp.bfloat16)
    in_hbm = lambda x: pltpu.with_memory_space_constraint(x, pltpu.HBM)
    swap = [(0, 1), (1, 0)]

    edge, inner, sent, mine, down, rim, wide, small, near, away, narrow, lift = call(
        stage_kernel, "stage", [HBM] * 2,
        [f32(planes, SUB, LANES), f32(2, planes, SUB, LANES), f32(planes * 3 // 4, SUB, LANES), f32(*curves.shape), b16(6 * LANES, half),
         b16(2 * RIM, LANES), b16(2 * half, LANES), b16(2 * LANES, LANES), b16(2 * LANES, half),
         b16(2 * LANES, half), b16(2 * LANES, half), b16(2 * LANES, LANES)],
        [pltpu.SemaphoreType.DMA((3 * SUB + 1,))],
    )(in_hbm(image), in_hbm(curves))
    pairs = []
    for tile in range(count):
        pairs.append((2 * tile + 1, 2 * ((tile + 1) % count)))
        pairs.append((2 * tile, 2 * ((tile - 1) % count) + 1))

    gauss_shape = f32(2, planes // 4, STACK, 2, SUB, LANES)
    out_shape = f32(2, planes, SUB, LANES)
    last_shape = b16(2, planes // 4, 2 * SUB, 6 * LANES)
    table_shape = f32(LEVELS, TABLES, SUB, LANES)
    strip = (3, planes, SUB, LANES)
    part = [fast_half(2, *last_shape.shape)]
    own_shapes = [gauss_shape, last_shape, out_shape, out_shape, table_shape, i32(*strip), f32(*strip)]
    begun = call(early_kernel, "early", [VMEM] * 4, own_shapes, part)(edge, inner, mine, down)
    sent, mine, begun = lax.optimization_barrier((sent, mine, begun))
    halo = lax.ppermute(sent, ("tile", "lvl"), pairs)
    other_curves = lax.ppermute(mine, "lvl", swap)
    gauss, last, place, weight, tables, cells, fractions = call(
        late_kernel, "late", [VMEM] * 11, own_shapes, part,
        input_output_aliases={4 + at: at for at in range(7)},
    )(edge, inner, mine, down, *begun)
    gauss, tables, last, toned = call(
        other_kernel, "other", [VMEM] * 10, [gauss_shape, table_shape, last_shape, out_shape], part,
        input_output_aliases={8: 0, 9: 1},
    )(edge, inner, mine, other_curves, down, cells, fractions, last, gauss, tables)
    mine, _ = call(
        rest_kernel, "rest", [VMEM] * 15, [out_shape, gauss_shape],
        [fast_int(planes, SUB, RIM), fast(planes, SUB, RIM),
         fast_half(2, 2, planes // 4, 2 * SUB, 2 * RIM), fast(2, planes // 2, LEVELS, SUB, half)],
        input_output_aliases={1: 1},
    )(halo, gauss, last, toned, place, weight, tables, down, rim, wide, small, near, away, narrow, lift)
    theirs = lax.ppermute(mine, "lvl", swap)
    sems = [pltpu.SemaphoreType.DMA((2 * SUB,))]
    begun = call(put_mine_kernel, "put_mine", [VMEM], f32(rows, width), sems, HBM)(mine)
    return call(
        put_theirs_kernel, "put_theirs", [VMEM, HBM], f32(rows, width), sems, HBM, input_output_aliases={1: 0}
    )(theirs, begun)


def solution(mesh):
    placed = (P("band", "tile"), P("lvl", None))
    return jax.shard_map(
        body, mesh=mesh, in_specs=placed, out_specs=P("band", "tile"), check_vma=False
    )
```

```python
import functools

import jax
import jax.numpy as jnp
from jax import lax
from jax.experimental import pallas as pl
from jax.experimental.pallas import tpu as pltpu
from jax.sharding import PartitionSpec as P

LEVELS = 16
KNOTS = 17
PYR = 6

SUB = 8
LANES = 128
PIECE = LANES // 4
RIM = LANES
FIRST = 2
STACK = FIRST + LEVELS
LEFT, RIGHT = 2, 126
FINE = (LEVELS - 1) * (KNOTS - 1) // 2
TABLES = 11

VMEM = pl.BlockSpec(memory_space=pltpu.VMEM)
HBM = pl.BlockSpec(memory_space=pltpu.HBM)
PARAMS = pltpu.CompilerParams(vmem_limit_bytes=20 * 1024 * 1024)


def iota(shape, dim):
    return lax.broadcasted_iota(jnp.int32, shape, dim)


def down_taps(distance):
    size = jnp.abs(distance)
    value = jnp.where(size == 0, 6.0, jnp.where(size == 1, 4.0, jnp.where(size == 2, 1.0, 0.0)))
    return (value / 256.0).astype(jnp.bfloat16)


def up_taps(distance):
    size = jnp.abs(distance)
    value = jnp.where(size == 0, 0.75, jnp.where(size == 1, 0.5, jnp.where(size == 2, 0.125, 0.0)))
    return (value / 2.0).astype(jnp.bfloat16)


def halves(x):
    high = x.astype(jnp.bfloat16)
    low = (x - high.astype(jnp.float32)).astype(jnp.bfloat16)
    return jnp.concatenate([high, low], axis=-1)


def dot(x, table):
    return jnp.dot(x, table, preferred_element_type=jnp.float32)


def shift_down(x):
    return pltpu.roll(x, 1, axis=x.ndim - 2)


def shift_up(x):
    return pltpu.roll(x, SUB - 1, axis=x.ndim - 2)


def sublane(x):
    return iota(x.shape, x.ndim - 2)


def rows_down(planes, scaled=False):
    first, last = planes[0], planes[-1]
    top = sublane(first) == 0
    quad = (lambda x: x) if scaled else (lambda x: 4.0 * x)
    minus2 = jnp.where(top, first, shift_down(planes[-2]))
    minus1 = jnp.where(top, 4.0 * first if scaled else first, shift_down(last))
    plus = jnp.where(sublane(first) == SUB - 1, 0.25 * last if scaled else last, shift_up(first))
    padded = [minus2, minus1] + list(planes) + [plus]
    out = []
    for at in range(0, len(planes), 2):
        a, b, c, d, e = padded[at:at + 5]
        out.append((a + e) + quad(b + d) + 6.0 * c)
    return out


def padded_for_up(planes):
    first, last = planes[0], planes[-1]
    below = jnp.where(sublane(first) == 0, first, shift_down(last))
    above = jnp.where(sublane(first) == SUB - 1, last, shift_up(first))
    return [below] + list(planes) + [above]


def rows_up(planes):
    padded = padded_for_up(planes)
    sums = [one + two for one, two in zip(padded[:-1], padded[1:])]
    out = []
    for at in range(len(planes)):
        out.append(0.25 * (sums[at] + sums[at + 1]) + planes[at])
        out.append(sums[at + 1])
    return out


def gather_along(dim):
    return lax.GatherDimensionNumbers(
        offset_dims=(),
        collapsed_slice_dims=(dim,),
        start_index_map=(dim,),
        operand_batching_dims=(1 - dim,),
        start_indices_batching_dims=(1 - dim,),
    )


def look_up(table, index, dim=0):
    return lax.gather(
        table, index[..., None], gather_along(dim), (1, 1), mode=lax.GatherScatterMode.PROMISE_IN_BOUNDS
    )


def cell(x, cells):
    scaled = x * float(cells)
    index = jnp.minimum(jnp.floor(scaled), float(cells - 1))
    return index.astype(jnp.int32), scaled - index


def by_lane(p):
    return p % 4 == 2


def curve_cell(p, x):
    return cell(x, FINE if by_lane(p) else (KNOTS - 1) // 2)


def curve_tables(curve_row, k):
    steps = (KNOTS - 1) // 2
    turn = lax.div(steps * k, LEVELS - 1)
    phase = (steps * k - (LEVELS - 1) * turn).astype(jnp.float32) / (LEVELS - 1)
    width = curve_row.shape[-1]
    row = jnp.broadcast_to(curve_row, (SUB, width))
    offset = iota((SUB, width), 1) - iota((SUB, width), 0)

    def node(shift):
        at = jnp.where(offset == steps - turn + shift, row, 0.0)
        return jnp.sum(at, axis=1, keepdims=True)

    left, middle, right = node(-1), node(0), node(1)
    slope = middle - left
    bend = (right - middle) - slope
    start = (k.astype(jnp.float32) / (LEVELS - 1) + middle) - phase * slope - phase * bend
    spread = lambda v: jnp.broadcast_to(v, (SUB, LANES))
    coarse = (spread(start), spread(slope), spread(bend))
    phase = spread(phase)

    lane = iota((SUB, LANES), 1)
    index = jnp.minimum(jnp.floor((lane.astype(jnp.float32) + 0.5) / (LEVELS - 1)), float(SUB - 1))
    index = index.astype(jnp.int32)
    within = (lane - (LEVELS - 1) * index).astype(jnp.float32)
    ends = [remap(coarse + (phase,), index, (within + side) / (LEVELS - 1)) for side in (0.0, 1.0)]
    fine = (ends[0], ends[1] - ends[0])
    return (phase,) + coarse + fine + tuple(4.0 * table for table in coarse + fine)


def remap(tables, index, rest):
    start, slope, bend, phase = tables
    bent = jnp.maximum(rest, phase)
    return look_up(start, index) + look_up(slope, index) * rest + look_up(bend, index) * bent


def remap_pair(table_ref, first, planes, index_of, rest_of):
    tables = [[table_ref[first + copy, kind] for kind in range(TABLES)] for copy in range(2)]
    mapped = [[], []]
    for p in range(planes):
        index, rest = index_of(p), rest_of(p)
        at = 6 if p % 2 else 1
        for copy in range(2):
            phase, (start, slope, bend, value, step) = tables[copy][0], tables[copy][at:at + 5]
            if by_lane(p):
                result = look_up(value, index, 1) + look_up(step, index, 1) * rest
            else:
                result = remap((start, slope, bend, phase), index, rest)
            mapped[copy].append(result)
    return mapped


def tone_tables(low, high):
    middle = (KNOTS - 1) // 2
    scale = middle / (LEVELS - 1)
    spread = lambda v: jnp.broadcast_to(v, (SUB, LANES))
    sub = iota((SUB, LANES), 0)

    def parts(curves, k):
        level = (sub + k).astype(jnp.float32) / (LEVELS - 1)
        left, centre, right = [spread(curves[:, at:at + 1]) for at in (middle - 1, middle, middle + 1)]
        return level + centre, scale * (right - centre), scale * (centre - left)

    def following(x, then):
        return jnp.where(sub == SUB - 1, spread(then[0:1, :]), shift_up(x))

    one, two = parts(low, 0), parts(high, LEVELS // 2)
    lane = iota((SUB, LANES), 1)
    tables = []
    for kind in range(3):
        rows = []
        for here, then in ((one, two), (two, two)):
            if kind == 0:
                rows.append(here[0])
            elif kind == 1:
                rows.append(following(here[0], then[0]) - here[0])
            else:
                rows.append(here[1] - following(here[2], then[2]))
        along = jnp.where(lane == sub, rows[0], jnp.where(lane == sub + SUB, rows[1], 0.0))
        tables.append(spread(jnp.sum(along, axis=0, keepdims=True)))
    return tables


def tone(tables, x):
    index, rest = cell(x, LEVELS - 1)
    base, step, arc = [look_up(table, index, 1) for table in tables]
    return base + rest * (step + (1.0 - rest) * arc)


def scaled_level(x):
    place = x * float(LEVELS - 1)
    half = 0.5 * place
    return place, jnp.abs(1.0 - 2.0 * (half - jnp.floor(half)))


def start_all(pairs, sems):
    copies = [pltpu.make_async_copy(one, two, sems.at[at]) for at, (one, two) in enumerate(pairs)]
    for copy in copies:
        copy.start()
    return copies


def wait_all(copies):
    for copy in copies:
        copy.wait()


def kept_lanes(lvl):
    lane = iota((SUB, LANES), 1)
    return (lane >= PIECE * lvl) & (lane < LANES - PIECE * (1 - lvl))


def unpack(sent, lvl):
    lane = iota((SUB, LANES), 1)
    planes = []
    for group in range(len(sent) // 3):
        three = sent[3 * group:3 * group + 3]
        one, two, three_on = [pltpu.roll(x, PIECE * (at + 1), axis=1) for at, x in enumerate(three)]
        later = jnp.where(lane < PIECE * (2 + lvl), two, three_on)
        planes += three + [jnp.where(lane < PIECE * (1 + lvl), one, later)]
    return planes


def near_column(lvl, lane):
    return lane + jnp.where(lvl == 0, LEFT, RIGHT)


def away_column(lvl, lane):
    return lane + jnp.where(lvl == 0, RIGHT, LEFT)


def level_one_column(lvl, at):
    return jnp.where(at < LANES, near_column(lvl, at), away_column(lvl, at - LANES))


def stage_kernel(image_ref, curves_ref, edge_ref, inner_ref, sent_ref, mine_ref, own_ref, rim_ref, wide_ref,
                 small_ref, near_ref, away_ref, narrow_ref, raise_ref, sems):
    lvl = lax.axis_index("lvl")
    planes = edge_ref.shape[0]
    half = 2 * LANES
    outermost = pl.multiple_of(lvl * 3 * LANES, LANES)
    rows = [pl.ds(q * planes, planes) for q in range(SUB)]
    pairs = [(image_ref.at[rows[q], pl.ds(outermost, LANES)], edge_ref.at[:, q, :]) for q in range(SUB)]
    pairs.append((curves_ref, mine_ref))
    for tile in range(2):
        columns = slice((tile + 1) * LANES, (tile + 2) * LANES)
        pairs += [(image_ref.at[rows[q], columns], inner_ref.at[tile, :, q, :]) for q in range(SUB)]
    copies = start_all(pairs, sems)

    def put(ref, shape, value):
        table = value(iota(shape, 0), iota(shape, 1))
        ref[0:shape[0], :] = table
        ref[shape[0]:2 * shape[0], :] = table

    def place(i):
        tile = i // LANES
        return jnp.where(lvl == 0, i, i - 2 * tile * LANES + LANES)

    def rim_place(i):
        return i + jnp.where(lvl == 0, -RIM, half)

    def out_place(far, j):
        return j + jnp.where(lvl == far, 0, LANES)

    def wide(i, j):
        column = level_one_column(lvl, i)
        left = (i < LANES) == (lvl == 0)
        return jnp.where(left == (j < LANES // 2), down_taps(column - 2 * j), 0.0)

    def up_pair(column, far):
        def value(i, j):
            lane = j & (LANES - 1)
            taps = up_taps(2 * column(lvl, i) - (out_place(far, lane) + RIM))
            return jnp.where(j < LANES, taps, 0.25 * taps)
        return value

    put(own_ref, (3 * LANES, half),
        lambda i, j: down_taps(place(i) - 2 * (level_one_column(lvl, j) - RIM // 2)))
    put(rim_ref, (RIM, LANES), lambda i, j: down_taps(rim_place(i) - 2 * (near_column(lvl, j) - RIM // 2)))
    put(wide_ref, (half, LANES), wide)
    put(small_ref, (LANES, LANES), lambda i, j: down_taps(i - 2 * j))
    put(near_ref, (LANES, half), up_pair(near_column, 0))
    put(away_ref, (LANES, half), up_pair(away_column, 1))
    put(narrow_ref, (LANES, half), lambda i, j: up_taps(2 * i - level_one_column(lvl, j)))
    put(raise_ref, (LANES, LANES), lambda i, j: up_taps(2 * i - j))
    wait_all(copies[:SUB])
    kept = kept_lanes(lvl)
    for group in range(planes // 4):
        *three, fourth = [edge_ref[4 * group + at] for at in range(4)]
        for at, x in enumerate(three):
            sent_ref[3 * group + at] = jnp.where(kept, x, pltpu.roll(fourth, LANES - PIECE * (at + 1), axis=1))
    wait_all(copies[SUB:])


def put_kernel(half_ref, out_ref, sems, lvl):
    planes = half_ref.shape[1]
    pairs = []
    for tile, at in enumerate((3 * lvl, 1 + lvl)):
        columns = pl.ds(pl.multiple_of(at * LANES, LANES), LANES)
        for q in range(SUB):
            pairs.append((half_ref.at[tile, :, q, :], out_ref.at[pl.ds(q * planes, planes), columns]))
    wait_all(start_all(pairs, sems))


def put_mine_kernel(mine_ref, out_ref, sems):
    put_kernel(mine_ref, out_ref, sems, lax.axis_index("lvl"))


def put_theirs_kernel(theirs_ref, begun_ref, out_ref, sems):
    put_kernel(theirs_ref, out_ref, sems, 1 - lax.axis_index("lvl"))


def pick(place, weight, values):
    even, odd = values(0), values(1)
    for k in range(2, LEVELS, 2):
        even = jnp.where(place >= float(k - 1), values(k), even)
        odd = jnp.where(place >= float(k), values(k + 1), odd)
    return odd + weight * (even - odd)


def split_store(ref, reduced, column, width):
    for pair in range(len(reduced) // 2):
        both = jnp.concatenate(reduced[2 * pair:2 * pair + 2], axis=0)
        high = both.astype(jnp.bfloat16)
        low = (both - high.astype(jnp.float32)).astype(jnp.bfloat16)
        ref[pair, :, column:column + LANES] = high
        ref[pair, :, width + column:width + column + LANES] = low


def scale_odd(planes):
    return [4.0 * x if p % 2 else x for p, x in enumerate(planes)]


def all_tables(table_ref, curves_ref, first):
    for row in range(LEVELS // 2):
        for kind, table in enumerate(curve_tables(curves_ref[row:row + 1, :], first + row)):
            table_ref[first + row, kind] = table


def image_of(edge_ref, inner_ref, tile, p):
    lvl = lax.axis_index("lvl")
    return edge_ref[p] if tile == 0 else inner_ref[lvl if tile == 1 else 1 - lvl, p]


def multiply_own(part_ref, down_ref, gauss_ref, target):
    part = part_ref[...].reshape(-1, 6 * LANES)
    result = dot(part, down_ref[...]).reshape(2, part_ref.shape[1], 2, SUB, 2 * LANES)
    for copy in range(2):
        for tile in range(2):
            span = slice(tile * LANES, (tile + 1) * LANES)
            gauss_ref[tile, :, target + copy] = result[copy, :, :, :, span]


def own_pairs(steps, table_ref, first, cell_ref, fraction_ref, down_ref, gauss_ref, last_ref, part_scr, before):
    planes = cell_ref.shape[1]
    waiting = before
    for step in steps:
        multiply_own(waiting[0], down_ref, gauss_ref, waiting[1])
        ref = last_ref if step == steps[-1] else part_scr.at[step % 2]
        for tile in range(3):
            mapped = remap_pair(
                table_ref, first + 2 * step, planes, lambda p: cell_ref[tile, p], lambda p: fraction_ref[tile, p]
            )
            for copy in range(2):
                split_store(ref.at[copy], rows_down(mapped[copy], scaled=True), tile * LANES, 3 * LANES)
        waiting = (ref, FIRST + first + 2 * step)


def waits_longest():
    foremost = (lax.axis_index("band") == 0) | (lax.axis_index("lvl") == 1)
    return (lax.axis_index("tile") == 0) & foremost


def waits_for_both():
    return waits_longest() & (lax.axis_index("lvl") == 1)


def early_kernel(*refs):
    @pl.when(waits_longest())
    def _():
        mine_begin(*refs)

    @pl.when(waits_for_both())
    def _():
        mine_end(*refs)


def late_kernel(*refs):
    refs = refs[:4] + refs[11:]

    @pl.when(jnp.logical_not(waits_longest()))
    def _():
        mine_begin(*refs)

    @pl.when(jnp.logical_not(waits_for_both()))
    def _():
        mine_end(*refs)


def mine_end(edge_ref, inner_ref, mine_ref, down_ref, gauss_ref, last_ref, place_ref, weight_ref,
             table_ref, cell_ref, fraction_ref, part_scr):
    first = lax.axis_index("lvl") * (LEVELS // 2)
    steps = range(LEVELS // 8, LEVELS // 4)
    before = (last_ref, FIRST + first + 2 * (steps[0] - 1))
    own_pairs(steps, table_ref, first, cell_ref, fraction_ref, down_ref, gauss_ref, last_ref, part_scr, before)


def mine_begin(edge_ref, inner_ref, mine_ref, down_ref, gauss_ref, last_ref, place_ref, weight_ref,
               table_ref, cell_ref, fraction_ref, part_scr):
    planes = edge_ref.shape[0]
    first = lax.axis_index("lvl") * (LEVELS // 2)
    all_tables(table_ref, mine_ref, first)
    image = functools.partial(image_of, edge_ref, inner_ref)
    for tile in range(3):
        for p in range(planes):
            x = image(tile, p)
            cell_ref[tile, p], fraction_ref[tile, p] = curve_cell(p, x)
            if tile < 2:
                place_ref[tile, p], weight_ref[tile, p] = scaled_level(x)
        reduced = rows_down(scale_odd([image(tile, p) for p in range(planes)]), scaled=True)
        for copy in range(2):
            split_store(part_scr.at[1, copy], reduced, tile * LANES, 3 * LANES)
    before = (part_scr.at[1], 0)
    steps = range(LEVELS // 8)
    own_pairs(steps, table_ref, first, cell_ref, fraction_ref, down_ref, gauss_ref, last_ref, part_scr, before)


def other_kernel(edge_ref, inner_ref, mine_ref, other_ref, down_ref, cell_ref, fraction_ref, last_in_ref,
                 gauss_in_ref, table_in_ref, gauss_ref, table_ref, last_ref, tone_ref, part_scr):
    lvl = lax.axis_index("lvl")
    first = (1 - lvl) * (LEVELS // 2)
    all_tables(table_ref, other_ref, first)
    low = jnp.where(lvl == 0, mine_ref[...], other_ref[...])
    high = jnp.where(lvl == 0, other_ref[...], mine_ref[...])
    tones = tone_tables(low, high)
    for tile in range(2):
        for p in range(edge_ref.shape[0]):
            tone_ref[tile, p] = tone(tones, image_of(edge_ref, inner_ref, tile, p))
    before = (last_in_ref, FIRST + lvl * (LEVELS // 2) + LEVELS // 2 - 2)
    steps = range(LEVELS // 4)
    own_pairs(steps, table_ref, first, cell_ref, fraction_ref, down_ref, gauss_ref, last_ref, part_scr, before)


def rest_kernel(halo_ref, gauss_in_ref, last_ref, tone_ref, place_ref, weight_ref, table_ref, down_ref,
                rim_ref, wide_ref, small_ref, near_ref, away_ref, narrow_ref, raise_ref, out_ref, gauss_ref,
                cell_scr, rest_scr, part_scr, up_scr):
    lvl = lax.axis_index("lvl")
    halo = unpack([halo_ref[at] for at in range(halo_ref.shape[0])], 1 - lvl)
    planes = len(halo)
    half = 2 * LANES
    pairs = LEVELS // 2

    multiply_own(last_ref, down_ref, gauss_ref, FIRST + (1 - lvl) * (LEVELS // 2) + LEVELS // 2 - 2)

    def columns_up(tile):
        source = jnp.concatenate([gauss_ref[tile, p // 2, FIRST:, p % 2] for p in range(planes // 2)], axis=0)
        result = dot(halves(source.reshape(-1, LANES)), tables_up[tile][...])
        up_scr[tile] = result.reshape(planes // 2, LEVELS, SUB, half)

    tables_up = (near_ref, away_ref)
    for p in range(planes):
        cell_scr[p], rest_scr[p] = curve_cell(p, halo[p])

    def multiply(slot, target):
        part = part_scr[slot].reshape(-1, 2 * RIM)
        result = dot(part, rim_ref[...]).reshape(2, planes // 4, 2, SUB, LANES)
        for copy in range(2):
            gauss_ref[0, :, target + copy] = gauss_ref[0, :, target + copy] + result[copy]

    reduced = rows_down(scale_odd(halo), scaled=True)
    for copy in range(2):
        split_store(part_scr.at[1, copy], reduced, 0, RIM)
    for step in range(pairs):
        slot = step % 2
        multiply(1 - slot, 2 * step)
        mapped = remap_pair(table_ref, 2 * step, planes, lambda p: cell_scr[p], lambda p: rest_scr[p])
        for copy in range(2):
            split_store(part_scr.at[slot, copy], rows_down(mapped[copy], scaled=True), 0, RIM)
    multiply((pairs - 1) % 2, 2 * pairs)

    sums = {}

    def quarter_sum(tile, at):
        if (tile, at) not in sums:
            count = planes // 2
            edge = lambda p: up_scr[tile, p, :, :, LANES:half]
            if at == 0:
                before = jnp.where(sublane(edge(0)) == 0, edge(0), shift_down(edge(count - 1)))
            else:
                before = edge(at - 1)
            if at == count:
                after = jnp.where(sublane(edge(0)) == SUB - 1, edge(count - 1), shift_up(edge(0)))
            else:
                after = edge(at)
            sums[tile, at] = before + after
        return sums[tile, at]

    def level_zero(tile, p):
        above, below = quarter_sum(tile, p // 2), quarter_sum(tile, p // 2 + 1)
        at = (place_ref[tile, p], weight_ref[tile, p])
        if p % 2 == 0:
            detail = pick(*at, lambda k: (above[k] + below[k]) + up_scr[tile, p // 2, k, :, 0:LANES])
        else:
            detail = 4.0 * pick(*at, lambda k: below[k])
        out_ref[tile, p] = tone_ref[tile, p] - detail

    waiting = [(tile, p) for tile in (1, 0) for p in range(planes)]

    def meanwhile(count):
        for _ in range(min(count, len(waiting))):
            level_zero(*waiting.pop(0))

    def level_one(p):
        guide = [gauss_ref[tile, p // 2, 0:1, p % 2] for tile in range(2)]
        copies = [gauss_ref[tile, p // 2, FIRST:, p % 2] for tile in range(2)]
        return jnp.concatenate([jnp.concatenate(part, axis=-1) for part in (guide, copies)], axis=0)

    def next_level(coarse, table):
        reduced = rows_down(coarse)
        stacked = jnp.concatenate(reduced, axis=0)
        result = dot(halves(stacked.reshape(-1, stacked.shape[-1])), table)
        result = result.reshape(len(reduced), 1 + LEVELS, SUB, LANES)
        return [result[p] for p in range(len(reduced))]

    def raise_columns(stacks, table):
        stacked = jnp.concatenate(stacks, axis=0)
        result = dot(halves(stacked.reshape(-1, LANES)), table)
        return result.reshape((len(stacks), -1, SUB, table.shape[1]))

    def raise_stack(coarse, table):
        result = raise_columns([plane[1:] for plane in coarse], table)
        return rows_up([result[p] for p in range(len(coarse))])

    def raise_one(planes_of, table):
        result = raise_columns([plane[None] for plane in planes_of], table)
        return rows_up([result[p, 0] for p in range(len(planes_of))])

    def coefficient(level, raised, p):
        here = gauss[level][p]
        return pick(*scaled_level(here[0]), lambda k: here[1 + k] - raised[p][k])

    columns_up(1)
    lift = raise_ref[...]
    gauss = [None, [level_one(p) for p in range(planes // 2)]]
    gauss.append(next_level(gauss[1], wide_ref[...]))
    raised = [None, raise_stack(gauss[2], narrow_ref[...])]
    columns_up(0)
    coeffs = [None, []]
    quarter = planes // 8
    for level in range(2, PYR - 1):
        gauss.append(next_level(gauss[level], small_ref[...]))
        coeffs[1] += [coefficient(1, raised[1], p) for p in range(quarter * (level - 2), quarter * (level - 1))]
        raised.append(raise_stack(gauss[level + 1], lift))
    base = raise_one([gauss[PYR - 1][0][0]], lift)
    coeffs[1] += [coefficient(1, raised[1], p) for p in range(3 * quarter, planes // 2)]
    for level in range(2, PYR - 1):
        coeffs.append([coefficient(level, raised[level], p) for p in range(len(gauss[level]))])
    for level in range(PYR - 2, 0, -1):
        out = [one + two for one, two in zip(coeffs[level], base)]
        if level > 1:
            base = raise_one(out, narrow_ref[...] if level == 2 else lift)
        else:
            base = []
            for tile in range(2):
                span = slice(tile * LANES, (tile + 1) * LANES)
                base.append(raise_one([plane[:, span] for plane in out], tables_up[tile][:, 0:LANES]))
        meanwhile(planes // 2)
    meanwhile(2 * planes)
    for tile in range(2):
        for p in range(planes):
            out_ref[tile, p] = out_ref[tile, p] + base[tile][p]


def call(kernel, name, in_specs, out_shape, scratch, out_space=VMEM, **others):
    return pl.pallas_call(
        kernel,
        name=name,
        in_specs=in_specs,
        out_specs=jax.tree.map(lambda _: out_space, out_shape),
        out_shape=out_shape,
        scratch_shapes=scratch,
        compiler_params=PARAMS,
        **others,
    )


def body(image, curves):
    rows, width = image.shape
    planes = rows // SUB
    half = width // 2
    count = lax.axis_size("tile")
    f32 = lambda *shape: jax.ShapeDtypeStruct(shape, jnp.float32)
    b16 = lambda *shape: jax.ShapeDtypeStruct(shape, jnp.bfloat16)
    fast = lambda *shape: pltpu.VMEM(shape, jnp.float32)
    i32 = lambda *shape: jax.ShapeDtypeStruct(shape, jnp.int32)
    fast_int = lambda *shape: pltpu.VMEM(shape, jnp.int32)
    fast_half = lambda *shape: pltpu.VMEM(shape, jnp.bfloat16)
    in_hbm = lambda x: pltpu.with_memory_space_constraint(x, pltpu.HBM)
    swap = [(0, 1), (1, 0)]

    edge, inner, sent, mine, down, rim, wide, small, near, away, narrow, lift = call(
        stage_kernel, "stage", [HBM] * 2,
        [f32(planes, SUB, LANES), f32(2, planes, SUB, LANES), f32(planes * 3 // 4, SUB, LANES), f32(*curves.shape), b16(6 * LANES, half),
         b16(2 * RIM, LANES), b16(2 * half, LANES), b16(2 * LANES, LANES), b16(2 * LANES, half),
         b16(2 * LANES, half), b16(2 * LANES, half), b16(2 * LANES, LANES)],
        [pltpu.SemaphoreType.DMA((3 * SUB + 1,))],
    )(in_hbm(image), in_hbm(curves))
    pairs = []
    for tile in range(count):
        pairs.append((2 * tile + 1, 2 * ((tile + 1) % count)))
        pairs.append((2 * tile, 2 * ((tile - 1) % count) + 1))

    gauss_shape = f32(2, planes // 4, STACK, 2, SUB, LANES)
    out_shape = f32(2, planes, SUB, LANES)
    last_shape = b16(2, planes // 4, 2 * SUB, 6 * LANES)
    table_shape = f32(LEVELS, TABLES, SUB, LANES)
    strip = (3, planes, SUB, LANES)
    part = [fast_half(2, *last_shape.shape)]
    own_shapes = [gauss_shape, last_shape, out_shape, out_shape, table_shape, i32(*strip), f32(*strip)]
    begun = call(early_kernel, "early", [VMEM] * 4, own_shapes, part)(edge, inner, mine, down)
    sent, mine, begun = lax.optimization_barrier((sent, mine, begun))
    halo = lax.ppermute(sent, ("tile", "lvl"), pairs)
    other_curves = lax.ppermute(mine, "lvl", swap)
    gauss, last, place, weight, tables, cells, fractions = call(
        late_kernel, "late", [VMEM] * 11, own_shapes, part,
        input_output_aliases={4 + at: at for at in range(7)},
    )(edge, inner, mine, down, *begun)
    gauss, tables, last, toned = call(
        other_kernel, "other", [VMEM] * 10, [gauss_shape, table_shape, last_shape, out_shape], part,
        input_output_aliases={8: 0, 9: 1},
    )(edge, inner, mine, other_curves, down, cells, fractions, last, gauss, tables)
    mine, _ = call(
        rest_kernel, "rest", [VMEM] * 15, [out_shape, gauss_shape],
        [fast_int(planes, SUB, RIM), fast(planes, SUB, RIM),
         fast_half(2, 2, planes // 4, 2 * SUB, 2 * RIM), fast(2, planes // 2, LEVELS, SUB, half)],
        input_output_aliases={1: 1},
    )(halo, gauss, last, toned, place, weight, tables, down, rim, wide, small, near, away, narrow, lift)
    theirs = lax.ppermute(mine, "lvl", swap)
    sems = [pltpu.SemaphoreType.DMA((2 * SUB,))]
    begun = call(put_mine_kernel, "put_mine", [VMEM], f32(rows, width), sems, HBM)(mine)
    return call(
        put_theirs_kernel, "put_theirs", [VMEM, HBM], f32(rows, width), sems, HBM, input_output_aliases={1: 0}
    )(theirs, begun)


def solution(mesh):
    placed = (P("band", "tile"), P("lvl", None))
    return jax.shard_map(
        body, mesh=mesh, in_specs=placed, out_specs=P("band", "tile"), check_vma=False
    )
```
